256 devices in a mesh: ty: 16 (over z_lo, x), tx: 16 (over z_hi, y, core).
Axes of the slice: x: 4, y: 4, z: 8 (z_hi: 2, z_lo: 4; z = z_hi * 4 + z_lo), core: 2. Of those that a mesh axis runs over, the one named last changes fastest.
Arguments:
- specimen: float32 [2, 8192, 8192], P(None, 'ty', 'tx'), may hold values from -3 to 3
- illumination: float32 [2, 256, 256], replicated, may hold values from -4 to 4
- patterns: float32 [16, 96, 256, 256], P('ty', 'tx'), may hold values from 0.05 to 2
- scan_offsets: int32 [16, 96, 2], P('ty', 'tx'), may hold values from 0 to 7936, as said below
- counts: int32 [16, 16], P('ty', 'tx'), may hold values from 1 to 6, as said below
Outputs:
- specimen_out: float32 [2, 8192, 8192], P(None, 'ty', 'tx')
- illumination_out: float32 [2, 256, 256], replicated
The draws below stay inside these ranges and needn't reach their ends.
Inputs may be any that keep to these rules, and one draw needn't show every extreme that they name: `counts`: each tile has 1 to 6 live slots, and some tile has exactly 6. `scan_offsets`: the corner of every slot of tile (a, b) lies in that tile, and its 256 x 256 window lies inside the object.
All inputs are finite; a program needn't handle non-finite values.
Results may differ from the reference program's by a relative error of at most 0.0003.
Values sent between devices are 32-bit elements; how exact they have to be, the bound alone decides.
A program may use at most 128 MiB of HBM per device.

```python
import math
import jax
import jax.numpy as jnp
from jax import lax

W = 256
TILE = 512
POS_DEV = 3
CAP = 6
ITERS = 2
NY = 8192
NX = 8192
N_TY = 16
N_TX = 16


def draw_counts(key, part):
    key = jax.random.fold_in(key, 11)
    first_key, second_key = jax.random.split(key)
    tiles = N_TY * N_TX
    drawn = jax.random.randint(first_key, (tiles,), 1, CAP + 1)
    fullest = jax.random.randint(second_key, (), 0, tiles)
    drawn = jnp.where(jnp.arange(tiles) == fullest, CAP, drawn)
    return drawn.reshape(N_TY, N_TX).astype(jnp.int32)


def draw_scan_offsets(key, part):
    key = jax.random.fold_in(key, 23)
    row_key, col_key = jax.random.split(key)
    tile_row = jnp.arange(N_TY, dtype=jnp.int32)[:, None, None]
    tile_col = (jnp.arange(N_TX * CAP, dtype=jnp.int32) // CAP)[None, :, None]
    row_limit = jnp.where(tile_row == N_TY - 1, TILE - W + 1, TILE)
    col_limit = jnp.where(tile_col == N_TX - 1, TILE - W + 1, TILE)
    row_limit = jnp.broadcast_to(row_limit, (N_TY, N_TX * CAP, 1))
    col_limit = jnp.broadcast_to(col_limit, (N_TY, N_TX * CAP, 1))
    rows_local = jax.random.randint(row_key, (N_TY, N_TX * CAP, 1), 0, row_limit)
    cols_local = jax.random.randint(col_key, (N_TY, N_TX * CAP, 1), 0, col_limit)
    rows_global = tile_row * TILE + rows_local
    cols_global = tile_col * TILE + cols_local
    result = jnp.concatenate([rows_global, cols_global], axis=-1).astype(jnp.int32)
    result = result.at[0, 0, :].set(jnp.zeros((2,), jnp.int32))
    far_corner = jnp.array([N_TY * TILE - W, N_TX * TILE - W], dtype=jnp.int32)
    result = result.at[N_TY - 1, (N_TX - 1) * CAP, :].set(far_corner)
    return result


def levels(rng, shape, cuts, low, largest):
    gain = 1.0
    for dim, blocks in cuts:
        heights = jax.random.uniform(jax.random.fold_in(jax.random.fold_in(rng, 6), dim), (blocks,), jnp.float32, low / len(cuts), largest / len(cuts))
        gain = gain * jnp.repeat(jnp.exp(heights), shape[dim] // blocks).reshape((-1,) + (1,) * (len(shape) - 1 - dim))
    return gain


def bell_draw(rng, dims, spread, bound, pieces=(), kind=jnp.bfloat16):
    factor_of = levels(rng, dims, pieces, -0.22, 0.18) if pieces else 1.0
    values = jax.random.normal(rng, dims, jnp.float32) * spread * factor_of
    return jnp.minimum(jnp.maximum(values, -bound), bound).astype(kind)


def setup_inputs(seed: int = 0) -> dict:
    splits = jax.random.split(jax.random.key(seed), 6)
    specimen = bell_draw(splits[0], (2, NY, NX), 0.5, 3.0, ((1, 16), (2, 16)), jnp.float32)
    illumination = bell_draw(splits[1], (2, W, W), 0.7, 4.0, (), jnp.float32)
    patterns = jnp.clip(jnp.exp(math.log(2.0) - 3.6888794 * jax.random.uniform(splits[2], (N_TY, N_TX * CAP, W, W), jnp.float32) ** levels(splits[2], (N_TY, N_TX * CAP, W, W), ((0, 16), (1, 16)), -0.2, 0.2)), 0.05, 2.0)
    scan_offsets = draw_scan_offsets(jax.random.fold_in(splits[5], 71), 0)
    counts = draw_counts(jax.random.fold_in(splits[5], 71), 0)
    return dict(specimen=specimen, illumination=illumination, patterns=patterns, scan_offsets=scan_offsets, counts=counts)


HIGHEST = lax.Precision.HIGHEST
OBJECT_STEP = 0.05
PROBE_GAIN = 0.5

def dft_tables(window):
    indices = jnp.arange(window, dtype=jnp.int32)
    products = indices[:, None] * indices[None, :] % window
    angles = products.astype(jnp.float32) * (2.0 * jnp.pi / window)
    scale = 1.0 / jnp.sqrt(jnp.float32(window))
    return (jnp.cos(angles) * scale, -jnp.sin(angles) * scale)

def complex_dot(left_real, left_imag, right_real, right_imag):
    real_part = jnp.dot(left_real, right_real, precision=HIGHEST) - jnp.dot(left_imag, right_imag, precision=HIGHEST)
    imag_part = jnp.dot(left_real, right_imag, precision=HIGHEST) + jnp.dot(left_imag, right_real, precision=HIGHEST)
    return (real_part, imag_part)

def slot_terms(patch_real, patch_imag, probe_real, probe_imag, measured, active, dft_real, dft_imag):
    psi_real = probe_real * patch_real - probe_imag * patch_imag
    psi_imag = probe_real * patch_imag + probe_imag * patch_real
    half_real, half_imag = complex_dot(dft_real, dft_imag, psi_real, psi_imag)
    far_real, far_imag = complex_dot(half_real, half_imag, dft_real, dft_imag)
    factor = active * (far_real * far_real + far_imag * far_imag - measured)
    back_real, back_imag = complex_dot(dft_real, -dft_imag, factor * far_real, factor * far_imag)
    chi_real, chi_imag = complex_dot(back_real, back_imag, dft_real, -dft_imag)
    object_real = probe_real * chi_real + probe_imag * chi_imag
    object_imag = probe_real * chi_imag - probe_imag * chi_real
    probe_grad_real = patch_real * chi_real + patch_imag * chi_imag
    probe_grad_imag = patch_real * chi_imag - patch_imag * chi_real
    return (jnp.stack([object_real, object_imag]), jnp.stack([probe_grad_real, probe_grad_imag]))

def reference(specimen, illumination, patterns, scan_offsets, counts):
    dft_real, dft_imag = dft_tables(W)
    total_slots = N_TY * N_TX * CAP
    measured = patterns.reshape(total_slots, W, W)
    offsets = scan_offsets.reshape(total_slots, 2).astype(jnp.int32)
    slot_ids = jnp.arange(CAP, dtype=jnp.int32)
    active = (slot_ids[None, None, :] < counts[:, :, None]).astype(jnp.float32).reshape(total_slots)
    probe_step = PROBE_GAIN / (POS_DEV * N_TY * N_TX)
    zero = jnp.zeros((), jnp.int32)
    for iteration in range(ITERS):

        def visit(carry, item):
            grad_object, grad_probe = carry
            offset, pattern, live = item
            corner_row = offset[0].astype(jnp.int32)
            corner_col = offset[1].astype(jnp.int32)
            patch = lax.dynamic_slice(specimen, (zero, corner_row, corner_col), (2, W, W))
            object_term, probe_term = slot_terms(patch[0], patch[1], illumination[0], illumination[1], pattern, live, dft_real, dft_imag)
            current = lax.dynamic_slice(grad_object, (zero, corner_row, corner_col), (2, W, W))
            grad_object = lax.dynamic_update_slice(grad_object, current + object_term, (zero, corner_row, corner_col))
            return ((grad_object, grad_probe + probe_term), None)
        start = (jnp.zeros(specimen.shape, jnp.float32), jnp.zeros(illumination.shape, jnp.float32))
        (grad_object, grad_probe), unused = lax.scan(visit, start, (offsets, measured, active))
        specimen = specimen - OBJECT_STEP * grad_object
        illumination = illumination - probe_step * grad_probe
    return (specimen, illumination)
```

```python
import functools

import jax
import jax.numpy as jnp
import ml_dtypes
import numpy as np
from jax import lax
from jax.experimental import pallas as pl
from jax.experimental.pallas import tpu as pltpu
from jax.sharding import PartitionSpec as P

POS_DEV = 3
ITERS = 2
OBJECT_STEP = 0.05
PROBE_GAIN = 0.5
MESH = pl.DeviceIdType.MESH
VMEM_LIMIT = 48 * 1024 * 1024
SUBLANES = 8


def real_table(window):
    half = window // 2
    k = np.arange(window)
    freq = np.where(k <= half, k, k - half)
    angles = 2.0 * np.pi * ((freq[:, None] * k[None, :]) % window) / window
    table = np.where((k <= half)[:, None], np.cos(angles), np.sin(angles))
    return table / np.sqrt(window)


def split_table(table):
    high = table.astype(ml_dtypes.bfloat16)
    low = (table - high.astype(np.float64)).astype(ml_dtypes.bfloat16)
    return high, low


def tables(window):
    high, low = split_table(real_table(window))
    left = np.concatenate([high, low, high], axis=1)
    left_back = np.concatenate([high.T, low.T, high.T], axis=1)
    right = np.concatenate([high.T, low.T, high.T], axis=0)
    right_back = np.concatenate([high, low, high], axis=0)
    return [jnp.asarray(t) for t in (left, right, left_back, right_back)]


def reorder_table(window):
    half = window // 2
    i = np.arange(window)
    freq = np.where(i <= half, i, window + half - i)
    return jnp.asarray((freq[:, None] == i[None, :]).astype(ml_dtypes.bfloat16))


def split(value):
    high = value.astype(jnp.bfloat16)
    low = (value - high.astype(jnp.float32)).astype(jnp.bfloat16)
    return high, low


def left_product(table, value):
    high, low = split(value)
    return jnp.dot(
        table, jnp.concatenate([high, high, low], axis=0), preferred_element_type=jnp.float32
    )


def right_product(value, table):
    high, low = split(value)
    return jnp.dot(
        jnp.concatenate([high, high, low], axis=1), table, preferred_element_type=jnp.float32
    )


def compute_kernel(
    count_ref, offsets_ref, specimen_ref, probe_ref, measured_ref,
    left_ref, right_ref, left_back_ref, right_back_ref,
    grad_ref, probe_grad_ref,
):
    window = probe_ref.shape[1]
    half = window // 2
    lanes = 128
    blocks = window // lanes
    grad_ref[...] = jnp.zeros_like(grad_ref)
    probe_grad_ref[...] = jnp.zeros_like(probe_grad_ref)
    lane = lax.broadcasted_iota(jnp.int32, (window + SUBLANES, lanes), 1)
    sublane = lax.broadcasted_iota(jnp.int32, (window // SUBLANES, SUBLANES, lanes), 1)
    sublane_ext = lax.broadcasted_iota(jnp.int32, (window // SUBLANES + 1, SUBLANES, lanes), 1)
    first_row = lax.broadcasted_iota(jnp.int32, (half, window), 0) == 0
    first_col = lax.broadcasted_iota(jnp.int32, (window, half), 1) == 0

    def visit(slot, carry):
        row = offsets_ref[slot, 0]
        col = offsets_ref[slot, 1]
        row_block = pl.multiple_of((row // SUBLANES) * SUBLANES, SUBLANES)
        col_block = pl.multiple_of((col // lanes) * lanes, lanes)
        row_rest = row - row_block
        col_rest = col - col_block

        def place(part, j):
            return (
                part,
                pl.ds(row_block, window + SUBLANES),
                pl.ds(pl.multiple_of(col_block + lanes * j, lanes), lanes),
            )

        def cut(part):
            keep = lane < lanes - col_rest
            pieces = [
                pltpu.roll(specimen_ref[place(part, j)], lax.rem(lanes - col_rest, lanes), 1)
                for j in range(blocks + 1)
            ]
            columns = []
            for j in range(blocks):
                taken = jnp.where(keep, pieces[j], pieces[j + 1])
                taken = taken.reshape(window // SUBLANES + 1, SUBLANES, lanes)
                taken = pltpu.roll(taken, lax.rem(SUBLANES - row_rest, SUBLANES), 1)
                upper = sublane < SUBLANES - row_rest
                columns.append(jnp.where(upper, taken[:-1], taken[1:]).reshape(window, lanes))
            return jnp.concatenate(columns, axis=1)

        patch_real, patch_imag = cut(0), cut(1)
        probe_real, probe_imag = probe_ref[0], probe_ref[1]
        psi_real = probe_real * patch_real - probe_imag * patch_imag
        psi_imag = probe_real * patch_imag + probe_imag * patch_real

        both = left_product(left_ref[...], jnp.concatenate([psi_real, psi_imag], axis=1))
        u_top, v_top = both[:half, :window], both[:half, window:]
        u_bot, v_bot = both[half:, :window], both[half:, window:]
        u_add = jnp.where(first_row, 0.0, u_bot)
        v_add = jnp.where(first_row, 0.0, v_bot)
        mid_real = jnp.concatenate([u_top + v_add, jnp.where(first_row, u_bot, u_top - v_bot)], axis=0)
        mid_imag = jnp.concatenate([v_top - u_add, jnp.where(first_row, v_bot, v_top + u_bot)], axis=0)

        both = right_product(jnp.concatenate([mid_real, mid_imag], axis=0), right_ref[...])
        u_top, v_top = both[:window, :half], both[window:, :half]
        u_bot, v_bot = both[:window, half:], both[window:, half:]
        u_add = jnp.where(first_col, 0.0, u_bot)
        v_add = jnp.where(first_col, 0.0, v_bot)
        far_real = jnp.concatenate([u_top + v_add, jnp.where(first_col, u_bot, u_top - v_bot)], axis=1)
        far_imag = jnp.concatenate([v_top - u_add, jnp.where(first_col, v_bot, v_top + u_bot)], axis=1)

        factor = far_real * far_real + far_imag * far_imag - measured_ref[slot]
        g_real = factor * far_real
        g_imag = factor * far_imag

        r_top, r_bot = g_real[:half], g_real[half:]
        i_top, i_bot = g_imag[:half], g_imag[half:]
        z_real = jnp.concatenate(
            [r_top + jnp.where(first_row, 0.0, r_bot), jnp.where(first_row, r_bot, i_bot - i_top)], axis=0)
        z_imag = jnp.concatenate(
            [i_top + jnp.where(first_row, 0.0, i_bot), jnp.where(first_row, i_bot, r_top - r_bot)], axis=0)
        both = left_product(left_back_ref[...], jnp.concatenate([z_real, z_imag], axis=1))

        r_top, r_bot = both[:, :half], both[:, half:window]
        i_top, i_bot = both[:, window:window + half], both[:, window + half:]
        z_real = jnp.concatenate(
            [r_top + jnp.where(first_col, 0.0, r_bot), jnp.where(first_col, r_bot, i_bot - i_top)], axis=1)
        z_imag = jnp.concatenate(
            [i_top + jnp.where(first_col, 0.0, i_bot), jnp.where(first_col, i_bot, r_top - r_bot)], axis=1)
        both = right_product(jnp.concatenate([z_real, z_imag], axis=0), right_back_ref[...])
        chi_real, chi_imag = both[:window], both[window:]

        probe_grad_ref[0] += patch_real * chi_real + patch_imag * chi_imag
        probe_grad_ref[1] += patch_real * chi_imag - patch_imag * chi_real
        terms = (
            probe_real * chi_real + probe_imag * chi_imag,
            probe_real * chi_imag - probe_imag * chi_real,
        )
        before = lane < col_rest
        above = sublane_ext < row_rest
        for part in range(2):
            turned = []
            for j in range(blocks):
                piece = terms[part][:, lanes * j:lanes * (j + 1)]
                piece = piece.reshape(window // SUBLANES, SUBLANES, lanes)
                piece = pltpu.roll(piece, row_rest, 1)
                edge = jnp.zeros((1, SUBLANES, lanes), jnp.float32)
                piece = jnp.where(
                    above,
                    jnp.concatenate([edge, piece], axis=0),
                    jnp.concatenate([piece, edge], axis=0),
                ).reshape(window + SUBLANES, lanes)
                turned.append(pltpu.roll(piece, col_rest, 1))
            for j in range(blocks + 1):
                if j == 0:
                    add = jnp.where(before, 0.0, turned[0])
                elif j == blocks:
                    add = jnp.where(before, turned[-1], 0.0)
                else:
                    add = jnp.where(before, turned[j - 1], turned[j])
                grad_ref[place(part, j)] += add
        return carry

    lax.fori_loop(0, count_ref[0], visit, 0)


def slot_gradients(count, offsets, extended, illumination, measured, dft):
    smem = pl.BlockSpec(memory_space=pltpu.SMEM)
    vmem = pl.BlockSpec(memory_space=pltpu.VMEM)
    return pl.pallas_call(
        compute_kernel,
        out_shape=(
            jax.ShapeDtypeStruct(extended.shape, jnp.float32),
            jax.ShapeDtypeStruct(illumination.shape, jnp.float32),
        ),
        in_specs=[smem, smem] + [vmem] * 7,
        out_specs=(vmem, vmem),
        compiler_params=pltpu.CompilerParams(vmem_limit_bytes=VMEM_LIMIT),
        name="slot_gradients",
    )(count, offsets, extended, illumination, measured, *dft)


def place_of():
    return lax.axis_index("ty"), lax.axis_index("tx"), lax.axis_size("ty"), lax.axis_size("tx")


def send_to(source, target, sems, index, row, col):
    send_sem, recv_sem = sems
    return pltpu.make_async_remote_copy(
        src_ref=source,
        dst_ref=target,
        send_sem=send_sem.at[index],
        recv_sem=recv_sem.at[index],
        device_id=(row, col),
        device_id_type=MESH,
    )


def wait_bytes(ref, sem):
    pltpu.make_async_copy(ref, ref, sem).wait()


def greet(partners):
    barrier = pltpu.get_barrier_semaphore()
    for exists, row, col in partners:
        @pl.when(exists)
        def _():
            pl.semaphore_signal(barrier, inc=1, device_id=(row, col), device_id_type=MESH)
    pl.semaphore_wait(barrier, sum(jnp.int32(exists) for exists, _, _ in partners))


def fetch_kernel(specimen, measured, reorder, reorder_t, extended, measured_out, send, recv, local):
    a, b, n_ty, n_tx = place_of()
    window = measured.shape[1]
    tile = specimen.shape[1]
    up, down, left, right = a > 0, a < n_ty - 1, b > 0, b < n_tx - 1
    greet([(up, a - 1, b), (down, a + 1, b), (left, a, b - 1), (right, a, b + 1)])
    sems = (send, recv)
    first, second = pl.ds(0, window), pl.ds(window, tile - window)
    beyond, inside = pl.ds(tile, window), pl.ds(0, tile)
    up_a = send_to(specimen.at[:, first, first], extended.at[:, beyond, first], sems, 0, a - 1, b)
    up_b = send_to(specimen.at[:, first, second], extended.at[:, beyond, second], sems, 1, a - 1, b)
    aside = send_to(specimen.at[:, :, first], extended.at[:, inside, beyond], sems, 2, a, b - 1)
    corner = send_to(extended.at[:, beyond, first], extended.at[:, beyond, beyond], sems, 3, a, b - 1)
    keep = pltpu.make_async_copy(specimen, extended.at[:, inside, inside], local)
    pl.when(up)(up_a.start)
    pl.when(left)(aside.start)
    keep.start()

    def rearrange(slot, carry):
        def pieces(value):
            high, low = split(value)
            rest = (value - high.astype(jnp.float32) - low.astype(jnp.float32)).astype(jnp.bfloat16)
            return [high, low, rest]

        rows = jnp.dot(
            reorder[...], jnp.concatenate(pieces(measured[slot]), axis=0),
            preferred_element_type=jnp.float32)
        measured_out[slot] = jnp.dot(
            jnp.concatenate(pieces(rows), axis=1), reorder_t[...],
            preferred_element_type=jnp.float32)
        return carry

    lax.fori_loop(0, measured.shape[0], rearrange, 0)

    @pl.when(up)
    def _():
        up_a.wait_send()
        up_b.start()

    @pl.when(down)
    def _():
        up_a.wait_recv()
        pl.when(left)(corner.start)

    keep.wait()
    pl.when(right)(aside.wait_recv)
    pl.when(left)(aside.wait_send)
    pl.when(up)(up_b.wait_send)
    pl.when(down)(up_b.wait_recv)
    pl.when(down & right)(corner.wait_recv)
    pl.when(down & left)(corner.wait_send)


def fetch(specimen, measured):
    window = measured.shape[1]
    side = specimen.shape[1] + window
    table = reorder_table(window)
    vmem = pl.BlockSpec(memory_space=pltpu.VMEM)
    hbm = pl.BlockSpec(memory_space=pl.ANY)
    return pl.pallas_call(
        fetch_kernel,
        out_shape=(
            jax.ShapeDtypeStruct((2, side, side), jnp.float32),
            jax.ShapeDtypeStruct(measured.shape, jnp.float32),
        ),
        in_specs=[hbm, vmem, vmem, vmem],
        out_specs=(hbm, vmem),
        scratch_shapes=[
            pltpu.SemaphoreType.DMA((4,)),
            pltpu.SemaphoreType.DMA((4,)),
            pltpu.SemaphoreType.DMA,
        ],
        compiler_params=pltpu.CompilerParams(
            collective_id=0, has_side_effects=True, vmem_limit_bytes=VMEM_LIMIT),
        name="fetch",
    )(specimen, measured, jnp.tile(table, (1, 3)), jnp.tile(table.T, (3, 1)))


class ProbeSum:
    def __init__(self, terms, buffers, send, recv):
        self.terms = terms
        self.mate, self.mine, self.pieces, self.strips, self.full, self.other = buffers
        self.send, self.recv = send, recv
        self.a, self.b, self.n_ty, n_tx = place_of()
        self.core = lax.rem(self.b, 2)
        self.pair = self.b // 2
        self.n_pair = n_tx // 2
        self.mate_col = self.b + 1 - 2 * self.core
        self.rows = self.full.shape[0] // self.n_ty

    @staticmethod
    def scratch(window, n_ty, n_tx):
        rows = window // n_ty
        return [
            pltpu.VMEM((window, window), jnp.float32),
            pltpu.VMEM((window, window), jnp.float32),
            pltpu.VMEM((n_ty - 1, rows, window), jnp.float32),
            pltpu.VMEM((n_tx // 2, rows, window), jnp.float32),
            pltpu.VMEM((window, window), jnp.float32),
            pltpu.VMEM((window, window), jnp.float32),
            pltpu.SemaphoreType.DMA((5,)),
            pltpu.SemaphoreType.DMA((5,)),
        ]

    def partners(self):
        found = [(True, self.a, self.mate_col)]
        found += [(True, lax.rem(self.a + d, self.n_ty), self.b) for d in range(1, self.n_ty)]
        found += [(True, self.a, 2 * lax.rem(self.pair + d, self.n_pair) + self.core) for d in range(1, self.n_pair)]
        return found

    def to(self, source, target, stage, row, col):
        return send_to(source, target, (self.send, self.recv), stage, row, col)

    def own(self, ref, row):
        return ref.at[pl.ds(pl.multiple_of(row * self.rows, SUBLANES), self.rows), :]

    def start(self):
        self.to(self.terms.at[1 - self.core], self.mate, 0, self.a, self.mate_col).start()

    def scatter(self):
        self.to(self.terms.at[1 - self.core], self.mate, 0, self.a, self.mate_col).wait()
        self.mine[...] = self.terms[self.core] + self.mate[...]

        def go(d, carry):
            row = lax.rem(self.a + d, self.n_ty)
            self.to(self.own(self.mine, row), self.pieces.at[d - 1], 1, row, self.b).start()
            return carry

        lax.fori_loop(1, self.n_ty, go, 0)

    def across(self):
        wait_bytes(self.pieces, self.recv.at[1])
        total = self.own(self.mine, self.a)[...]
        for d in range(self.n_ty - 1):
            total = total + self.pieces[d]
        self.strips[self.pair] = total

        def go(d, carry):
            col = 2 * lax.rem(self.pair + d, self.n_pair) + self.core
            self.to(self.strips.at[self.pair], self.strips.at[self.pair], 2, self.a, col).start()
            return carry

        lax.fori_loop(1, self.n_pair, go, 0)

    def gather(self):
        wait_bytes(self.strips.at[pl.ds(0, self.n_pair - 1)], self.recv.at[2])
        total = self.strips[0]
        for i in range(1, self.n_pair):
            total = total + self.strips[i]
        self.own(self.full, self.a)[...] = total

        def go(d, carry):
            row = lax.rem(self.a + d, self.n_ty)
            self.to(self.own(self.full, self.a), self.own(self.full, self.a), 3, row, self.b).start()
            return carry

        lax.fori_loop(1, self.n_ty, go, 0)

    def share(self):
        wait_bytes(self.full.at[pl.ds(0, (self.n_ty - 1) * self.rows)], self.recv.at[3])
        self.to(self.full, self.other, 4, self.a, self.mate_col).start()

    def finish(self, probe, probe_out):
        step = PROBE_GAIN / (POS_DEV * self.n_ty * 2 * self.n_pair)
        probe_out[self.core] = probe[self.core] - step * self.full[...]
        self.to(self.full, self.other, 4, self.a, self.mate_col).wait()
        probe_out[1 - self.core] = probe[1 - self.core] - step * self.other[...]
        wait_bytes(self.pieces, self.send.at[1])
        wait_bytes(self.strips.at[pl.ds(0, self.n_pair - 1)], self.send.at[2])
        wait_bytes(self.full.at[pl.ds(0, (self.n_ty - 1) * self.rows)], self.send.at[3])


def far_neighbour(a, b, n_tx):
    core = lax.rem(b, 2)
    col = b - 1 + 2 * core
    return ((col >= 0) & (col < n_tx), a, col)


def exchange_kernel(
    grad, extended, probe, probe_grad, extended_out, probe_out,
    gv, ev, from_left, from_right, from_up, from_down, send, recv, local,
    *probe_scratch,
):
    a, b, n_ty, n_tx = place_of()
    window = probe.shape[1]
    side = gv.shape[1]
    tile = side - window
    core = lax.rem(b, 2)
    has_up, has_down, has_left, has_right = a > 0, a < n_ty - 1, b > 0, b < n_tx - 1
    odd = core == 1
    total = ProbeSum(probe_grad, probe_scratch[:6], *probe_scratch[6:])
    greet(total.partners() + [far_neighbour(a, b, n_tx)])
    sems = (send, recv)
    start, middle, end = pl.ds(0, window), pl.ds(window, tile - window), pl.ds(tile, window)

    def across(rows, index):
        return (
            send_to(grad.at[:, rows, end], from_left.at[:, rows, :], sems, index, a, b + 1),
            send_to(grad.at[:, rows, start], from_right.at[:, rows, :], sems, index + 1, a, b - 1),
        )

    def along(source, cols, index):
        return (
            send_to(source.at[:, end, cols], from_up.at[:, :, cols], sems, index, a + 1, b),
            send_to(source.at[:, start, cols], from_down.at[:, :, cols], sems, index + 1, a - 1, b),
        )

    right_top, left_top = across(start, 0)
    right_mid, left_mid = across(middle, 2)
    right_end, left_end = across(end, 4)
    down_1, up_1 = along(grad, middle, 6)
    down_0, up_0 = along(gv, start, 8)
    down_2, up_2 = along(gv, end, 10)
    keep_top = send_to(ev.at[:, start, start], extended_out.at[:, start, end], sems, 12, a, b - 1)
    keep_end = send_to(ev.at[:, end, start], extended_out.at[:, end, end], sems, 13, a, b - 1)

    load_grad = pltpu.make_async_copy(grad, gv, local.at[0])
    load_extended = pltpu.make_async_copy(extended, ev, local.at[1])

    @pl.when(has_right)
    def _():
        right_top.start()
        right_end.start()

    @pl.when(has_left)
    def _():
        left_top.start()
        left_end.start()

    pl.when(has_down)(down_1.start)
    pl.when(has_up)(up_1.start)
    total.start()
    load_grad.start()
    load_extended.start()
    load_grad.wait()
    total.scatter()

    @pl.when(has_left)
    def _():
        right_top.wait_recv()
        right_end.wait_recv()
        gv[:, start, start] += from_left[:, start, :]
        gv[:, end, start] += from_left[:, end, :]

    @pl.when(has_down)
    def _():
        down_0.start()

    @pl.when(has_up)
    def _():
        up_0.start()

    @pl.when(has_right)
    def _():
        left_top.wait_recv()
        left_end.wait_recv()
        gv[:, start, end] += from_right[:, start, :]
        gv[:, end, end] += from_right[:, end, :]

    pl.when(has_down & odd)(down_2.start)
    pl.when(has_up & odd)(up_2.start)

    @pl.when(has_right)
    def _():
        right_top.wait_send()
        right_end.wait_send()
        right_mid.start()

    @pl.when(has_left)
    def _():
        left_top.wait_send()
        left_end.wait_send()
        left_mid.start()

    total.across()
    load_extended.wait()
    total.gather()

    @pl.when(has_left)
    def _():
        right_mid.wait_recv()
        gv[:, middle, start] += from_left[:, middle, :]

    @pl.when(has_right)
    def _():
        left_mid.wait_recv()
        gv[:, middle, end] += from_right[:, middle, :]

    ev[:, middle, :] -= OBJECT_STEP * gv[:, middle, :]
    store_mid = pltpu.make_async_copy(ev.at[:, middle, :], extended_out.at[:, middle, :], local.at[0])
    store_mid.start()
    total.share()

    def update(rows, cols, received, exists):
        @pl.when(exists)
        def _():
            ev[:, rows, cols] -= OBJECT_STEP * (gv[:, rows, cols] + received[:, :, cols])

        @pl.when(jnp.logical_not(exists))
        def _():
            ev[:, rows, cols] -= OBJECT_STEP * gv[:, rows, cols]

    pl.when(has_up)(down_0.wait_recv)
    pl.when(has_down)(up_0.wait_recv)
    update(start, start, from_up, has_up)
    update(end, start, from_down, has_down)

    @pl.when(odd)
    def _():
        keep_top.start()
        keep_end.start()

    pl.when(has_up)(down_1.wait_recv)
    pl.when(has_down)(up_1.wait_recv)
    update(start, middle, from_up, has_up)
    update(end, middle, from_down, has_down)
    inner = pl.ds(0, tile)
    store_top = pltpu.make_async_copy(ev.at[:, start, inner], extended_out.at[:, start, inner], local.at[1])
    store_end = pltpu.make_async_copy(ev.at[:, end, inner], extended_out.at[:, end, inner], local.at[2])
    store_top.start()
    store_end.start()

    @pl.when(odd)
    def _():
        pl.when(has_up)(down_2.wait_recv)
        pl.when(has_down)(up_2.wait_recv)
        update(start, end, from_up, has_up)
        update(end, end, from_down, has_down)
        rim_top = pltpu.make_async_copy(ev.at[:, start, end], extended_out.at[:, start, end], local.at[3])
        rim_end = pltpu.make_async_copy(ev.at[:, end, end], extended_out.at[:, end, end], local.at[4])
        rim_top.start()
        rim_end.start()
        rim_top.wait()
        rim_end.wait()
        keep_top.wait_send()
        keep_end.wait_send()

    total.finish(probe, probe_out)

    @pl.when(has_right)
    def _():
        right_mid.wait_send()

    @pl.when(has_left)
    def _():
        left_mid.wait_send()

    @pl.when(has_down)
    def _():
        down_0.wait_send()
        down_1.wait_send()
        pl.when(odd)(down_2.wait_send)

    @pl.when(has_up)
    def _():
        up_0.wait_send()
        up_1.wait_send()
        pl.when(odd)(up_2.wait_send)

    store_mid.wait()
    store_top.wait()
    store_end.wait()

    @pl.when(jnp.logical_not(odd))
    def _():
        keep_top.wait_recv()
        keep_end.wait_recv()


def exchange(grad, extended, illumination, probe_grad):
    window = illumination.shape[1]
    side = grad.shape[1]
    vmem = pl.BlockSpec(memory_space=pltpu.VMEM)
    hbm = pl.BlockSpec(memory_space=pl.ANY)
    return pl.pallas_call(
        exchange_kernel,
        out_shape=(
            jax.ShapeDtypeStruct(extended.shape, jnp.float32),
            jax.ShapeDtypeStruct(illumination.shape, jnp.float32),
        ),
        in_specs=[hbm, hbm, vmem, vmem],
        out_specs=(hbm, vmem),
        scratch_shapes=[
            pltpu.VMEM((2, side, side), jnp.float32),
            pltpu.VMEM((2, side, side), jnp.float32),
            pltpu.VMEM((2, side, window), jnp.float32),
            pltpu.VMEM((2, side, window), jnp.float32),
            pltpu.VMEM((2, window, side), jnp.float32),
            pltpu.VMEM((2, window, side), jnp.float32),
            pltpu.SemaphoreType.DMA((14,)),
            pltpu.SemaphoreType.DMA((14,)),
            pltpu.SemaphoreType.DMA((5,)),
        ] + ProbeSum.scratch(window, lax.axis_size("ty"), lax.axis_size("tx")),
        compiler_params=pltpu.CompilerParams(
            collective_id=1, has_side_effects=True, vmem_limit_bytes=VMEM_LIMIT),
        name="exchange",
    )(grad, extended, illumination, probe_grad)


def fold_kernel(
    grad, extended, probe, probe_grad, specimen_out, probe_out,
    gv, ev, corner, from_left, from_up, send, recv, local,
    *probe_scratch,
):
    a, b, n_ty, n_tx = place_of()
    window = probe.shape[1]
    side = gv.shape[1]
    tile = side - window
    has_up, has_down, has_left, has_right = a > 0, a < n_ty - 1, b > 0, b < n_tx - 1
    total = ProbeSum(probe_grad, probe_scratch[:6], *probe_scratch[6:])
    greet(total.partners() + [far_neighbour(a, b, n_tx)])
    sems = (send, recv)
    start, middle, end = pl.ds(0, window), pl.ds(window, tile - window), pl.ds(tile, window)
    inner = pl.ds(0, tile)
    right_end = send_to(grad.at[:, end, end], from_left.at[:, end, :], sems, 0, a, b + 1)
    right_rest = send_to(grad.at[:, inner, end], from_left.at[:, inner, :], sems, 1, a, b + 1)
    down_1 = send_to(grad.at[:, end, middle], from_up.at[:, :, middle], sems, 2, a + 1, b)
    down_0 = send_to(corner, from_up.at[:, :, start], sems, 3, a + 1, b)
    load_grad = pltpu.make_async_copy(grad.at[:, :, inner], gv, local.at[0])
    load_extended = pltpu.make_async_copy(extended.at[:, inner, inner], ev, local.at[1])
    pl.when(has_right)(right_end.start)
    pl.when(has_down)(down_1.start)
    total.start()
    load_grad.start()
    load_extended.start()
    total.scatter()
    load_grad.wait()

    @pl.when(has_left)
    def _():
        right_end.wait_recv()
        corner[...] = gv[:, end, start] + from_left[:, end, :]

    @pl.when(jnp.logical_not(has_left))
    def _():
        corner[...] = gv[:, end, start]

    pl.when(has_down)(down_0.start)

    @pl.when(has_right)
    def _():
        right_end.wait_send()
        right_rest.start()

    total.across()
    load_extended.wait()
    total.gather()
    ev[...] -= OBJECT_STEP * gv[:, inner, :]

    @pl.when(has_left)
    def _():
        right_rest.wait_recv()
        ev[:, :, start] -= OBJECT_STEP * from_left[:, inner, :]

    total.share()

    @pl.when(has_up)
    def _():
        down_1.wait_recv()
        down_0.wait_recv()
        ev[:, start, :] -= OBJECT_STEP * from_up[...]

    specimen_out[...] = ev[...]
    total.finish(probe, probe_out)
    pl.when(has_right)(right_rest.wait_send)

    @pl.when(has_down)
    def _():
        down_1.wait_send()
        down_0.wait_send()


def fold(grad, extended, illumination, probe_grad):
    window = illumination.shape[1]
    side = grad.shape[1]
    tile = side - window
    vmem = pl.BlockSpec(memory_space=pltpu.VMEM)
    hbm = pl.BlockSpec(memory_space=pl.ANY)
    return pl.pallas_call(
        fold_kernel,
        out_shape=(
            jax.ShapeDtypeStruct((2, tile, tile), jnp.float32),
            jax.ShapeDtypeStruct(illumination.shape, jnp.float32),
        ),
        in_specs=[hbm, hbm, vmem, vmem],
        out_specs=(vmem, vmem),
        scratch_shapes=[
            pltpu.VMEM((2, side, tile), jnp.float32),
            pltpu.VMEM((2, tile, tile), jnp.float32),
            pltpu.VMEM((2, window, window), jnp.float32),
            pltpu.VMEM((2, side, window), jnp.float32),
            pltpu.VMEM((2, window, tile), jnp.float32),
            pltpu.SemaphoreType.DMA((4,)),
            pltpu.SemaphoreType.DMA((4,)),
            pltpu.SemaphoreType.DMA((2,)),
        ] + ProbeSum.scratch(window, lax.axis_size("ty"), lax.axis_size("tx")),
        compiler_params=pltpu.CompilerParams(
            collective_id=2, has_side_effects=True, vmem_limit_bytes=VMEM_LIMIT),
        name="fold",
    )(grad, extended, illumination, probe_grad)


def body(specimen, illumination, patterns, scan_offsets, counts):
    window = illumination.shape[1]
    tile = specimen.shape[1]
    row_anchor = lax.axis_index("ty") * tile
    col_anchor = lax.axis_index("tx") * tile
    offsets = scan_offsets[0] - jnp.stack([row_anchor, col_anchor])[None, :].astype(jnp.int32)
    count = counts.reshape(1)
    dft = tables(window)
    extended, measured = fetch(specimen, patterns[0])
    for iteration in range(ITERS):
        grad, probe_grad = slot_gradients(count, offsets, extended, illumination, measured, dft)
        if iteration < ITERS - 1:
            extended, illumination = exchange(grad, extended, illumination, probe_grad)
        else:
            specimen, illumination = fold(grad, extended, illumination, probe_grad)
    return (specimen, illumination)


def solution(mesh):
    placed = (
        P(None, "ty", "tx"),
        P(),
        P("ty", "tx", None, None),
        P("ty", "tx", None),
        P("ty", "tx"),
    )
    return jax.shard_map(
        body, mesh=mesh, in_specs=placed, out_specs=(P(None, "ty", "tx"), P()), check_vma=False
    )
```

```python
import functools

import jax
import jax.numpy as jnp
import ml_dtypes
import numpy as np
from jax import lax
from jax.experimental import pallas as pl
from jax.experimental.pallas import tpu as pltpu
from jax.sharding import PartitionSpec as P

POS_DEV = 3
ITERS = 2
OBJECT_STEP = 0.05
PROBE_GAIN = 0.5
MESH = pl.DeviceIdType.MESH
VMEM_LIMIT = 48 * 1024 * 1024
SUBLANES = 8


def real_table(window):
    half = window // 2
    k = np.arange(window)
    freq = np.where(k <= half, k, k - half)
    angles = 2.0 * np.pi * ((freq[:, None] * k[None, :]) % window) / window
    table = np.where((k <= half)[:, None], np.cos(angles), np.sin(angles))
    return table / np.sqrt(window)


def split_table(table):
    high = table.astype(ml_dtypes.bfloat16)
    low = (table - high.astype(np.float64)).astype(ml_dtypes.bfloat16)
    return high, low


def tables(window):
    high, low = split_table(real_table(window))
    left = np.concatenate([high, low, high], axis=1)
    left_back = np.concatenate([high.T, low.T, high.T], axis=1)
    right = np.concatenate([high.T, low.T, high.T], axis=0)
    right_back = np.concatenate([high, low, high], axis=0)
    return [jnp.asarray(t) for t in (left, right, left_back, right_back)]


def reorder_table(window):
    half = window // 2
    i = np.arange(window)
    freq = np.where(i <= half, i, window + half - i)
    return (freq[:, None] == i[None, :]).astype(ml_dtypes.bfloat16)


def split(value):
    high = value.astype(jnp.bfloat16)
    low = (value - high.astype(jnp.float32)).astype(jnp.bfloat16)
    return high, low


def left_product(table, value):
    high, low = split(value)
    return jnp.dot(
        table, jnp.concatenate([high, high, low], axis=0), preferred_element_type=jnp.float32
    )


def right_product(value, table):
    high, low = split(value)
    return jnp.dot(
        jnp.concatenate([high, high, low], axis=1), table, preferred_element_type=jnp.float32
    )


def compute_kernel(
    count_ref, offsets_ref, specimen_ref, probe_ref, measured_ref,
    left_ref, right_ref, left_back_ref, right_back_ref,
    grad_ref, probe_grad_ref,
):
    window = probe_ref.shape[1]
    half = window // 2
    lanes = 128
    blocks = window // lanes
    grad_ref[...] = jnp.zeros_like(grad_ref)
    probe_grad_ref[...] = jnp.zeros_like(probe_grad_ref)
    lane = lax.broadcasted_iota(jnp.int32, (window + SUBLANES, lanes), 1)
    sublane = lax.broadcasted_iota(jnp.int32, (window // SUBLANES, SUBLANES, lanes), 1)
    sublane_ext = lax.broadcasted_iota(jnp.int32, (window // SUBLANES + 1, SUBLANES, lanes), 1)
    first_row = lax.broadcasted_iota(jnp.int32, (half, window), 0) == 0
    first_col = lax.broadcasted_iota(jnp.int32, (window, half), 1) == 0

    def visit(slot, carry):
        row = offsets_ref[slot, 0]
        col = offsets_ref[slot, 1]
        row_block = pl.multiple_of((row // SUBLANES) * SUBLANES, SUBLANES)
        col_block = pl.multiple_of((col // lanes) * lanes, lanes)
        row_rest = row - row_block
        col_rest = col - col_block

        def place(part, j):
            return (
                part,
                pl.ds(row_block, window + SUBLANES),
                pl.ds(pl.multiple_of(col_block + lanes * j, lanes), lanes),
            )

        def cut(part):
            keep = lane < lanes - col_rest
            pieces = [
                pltpu.roll(specimen_ref[place(part, j)], lax.rem(lanes - col_rest, lanes), 1)
                for j in range(blocks + 1)
            ]
            columns = []
            for j in range(blocks):
                taken = jnp.where(keep, pieces[j], pieces[j + 1])
                taken = taken.reshape(window // SUBLANES + 1, SUBLANES, lanes)
                taken = pltpu.roll(taken, lax.rem(SUBLANES - row_rest, SUBLANES), 1)
                upper = sublane < SUBLANES - row_rest
                columns.append(jnp.where(upper, taken[:-1], taken[1:]).reshape(window, lanes))
            return jnp.concatenate(columns, axis=1)

        patch_real, patch_imag = cut(0), cut(1)
        probe_real, probe_imag = probe_ref[0], probe_ref[1]
        psi_real = probe_real * patch_real - probe_imag * patch_imag
        psi_imag = probe_real * patch_imag + probe_imag * patch_real

        both = left_product(left_ref[...], jnp.concatenate([psi_real, psi_imag], axis=1))
        u_top, v_top = both[:half, :window], both[:half, window:]
        u_bot, v_bot = both[half:, :window], both[half:, window:]
        u_add = jnp.where(first_row, 0.0, u_bot)
        v_add = jnp.where(first_row, 0.0, v_bot)
        mid_real = jnp.concatenate([u_top + v_add, jnp.where(first_row, u_bot, u_top - v_bot)], axis=0)
        mid_imag = jnp.concatenate([v_top - u_add, jnp.where(first_row, v_bot, v_top + u_bot)], axis=0)

        both = right_product(jnp.concatenate([mid_real, mid_imag], axis=0), right_ref[...])
        u_top, v_top = both[:window, :half], both[window:, :half]
        u_bot, v_bot = both[:window, half:], both[window:, half:]
        u_add = jnp.where(first_col, 0.0, u_bot)
        v_add = jnp.where(first_col, 0.0, v_bot)
        far_real = jnp.concatenate([u_top + v_add, jnp.where(first_col, u_bot, u_top - v_bot)], axis=1)
        far_imag = jnp.concatenate([v_top - u_add, jnp.where(first_col, v_bot, v_top + u_bot)], axis=1)

        factor = far_real * far_real + far_imag * far_imag - measured_ref[slot]
        g_real = factor * far_real
        g_imag = factor * far_imag

        r_top, r_bot = g_real[:half], g_real[half:]
        i_top, i_bot = g_imag[:half], g_imag[half:]
        z_real = jnp.concatenate(
            [r_top + jnp.where(first_row, 0.0, r_bot), jnp.where(first_row, r_bot, i_bot - i_top)], axis=0)
        z_imag = jnp.concatenate(
            [i_top + jnp.where(first_row, 0.0, i_bot), jnp.where(first_row, i_bot, r_top - r_bot)], axis=0)
        both = left_product(left_back_ref[...], jnp.concatenate([z_real, z_imag], axis=1))

        r_top, r_bot = both[:, :half], both[:, half:window]
        i_top, i_bot = both[:, window:window + half], both[:, window + half:]
        z_real = jnp.concatenate(
            [r_top + jnp.where(first_col, 0.0, r_bot), jnp.where(first_col, r_bot, i_bot - i_top)], axis=1)
        z_imag = jnp.concatenate(
            [i_top + jnp.where(first_col, 0.0, i_bot), jnp.where(first_col, i_bot, r_top - r_bot)], axis=1)
        both = right_product(jnp.concatenate([z_real, z_imag], axis=0), right_back_ref[...])
        chi_real, chi_imag = both[:window], both[window:]

        probe_grad_ref[0] += patch_real * chi_real + patch_imag * chi_imag
        probe_grad_ref[1] += patch_real * chi_imag - patch_imag * chi_real
        terms = (
            probe_real * chi_real + probe_imag * chi_imag,
            probe_real * chi_imag - probe_imag * chi_real,
        )
        before = lane < col_rest
        above = sublane_ext < row_rest
        for part in range(2):
            turned = []
            for j in range(blocks):
                piece = terms[part][:, lanes * j:lanes * (j + 1)]
                piece = piece.reshape(window // SUBLANES, SUBLANES, lanes)
                piece = pltpu.roll(piece, row_rest, 1)
                edge = jnp.zeros((1, SUBLANES, lanes), jnp.float32)
                piece = jnp.where(
                    above,
                    jnp.concatenate([edge, piece], axis=0),
                    jnp.concatenate([piece, edge], axis=0),
                ).reshape(window + SUBLANES, lanes)
                turned.append(pltpu.roll(piece, col_rest, 1))
            for j in range(blocks + 1):
                if j == 0:
                    add = jnp.where(before, 0.0, turned[0])
                elif j == blocks:
                    add = jnp.where(before, turned[-1], 0.0)
                else:
                    add = jnp.where(before, turned[j - 1], turned[j])
                grad_ref[place(part, j)] += add
        return carry

    lax.fori_loop(0, count_ref[0], visit, 0)


def slot_gradients(count, offsets, extended, illumination, measured, dft):
    smem = pl.BlockSpec(memory_space=pltpu.SMEM)
    vmem = pl.BlockSpec(memory_space=pltpu.VMEM)
    return pl.pallas_call(
        compute_kernel,
        out_shape=(
            jax.ShapeDtypeStruct(extended.shape, jnp.float32),
            jax.ShapeDtypeStruct(illumination.shape, jnp.float32),
        ),
        in_specs=[smem, smem] + [vmem] * 7,
        out_specs=(vmem, vmem),
        compiler_params=pltpu.CompilerParams(vmem_limit_bytes=VMEM_LIMIT),
        name="slot_gradients",
    )(count, offsets, extended, illumination, measured, *dft)


def place_of():
    return lax.axis_index("ty"), lax.axis_index("tx"), lax.axis_size("ty"), lax.axis_size("tx")


def send_to(source, target, sems, index, row, col):
    send_sem, recv_sem = sems
    return pltpu.make_async_remote_copy(
        src_ref=source,
        dst_ref=target,
        send_sem=send_sem.at[index],
        recv_sem=recv_sem.at[index],
        device_id=(row, col),
        device_id_type=MESH,
    )


def wait_bytes(ref, sem):
    pltpu.make_async_copy(ref, ref, sem).wait()


def greet(partners):
    barrier = pltpu.get_barrier_semaphore()
    for exists, row, col in partners:
        @pl.when(exists)
        def _():
            pl.semaphore_signal(barrier, inc=1, device_id=(row, col), device_id_type=MESH)
    pl.semaphore_wait(barrier, sum(jnp.int32(exists) for exists, _, _ in partners))


class Boundary:
    def __init__(self, relay, sems):
        self.relay = relay
        self.hop_send, self.hop_recv, self.end_send, self.end_recv = sems
        self.a, self.b, _, self.n_tx = place_of()
        self.low = self.n_tx // 2 - 1
        self.at_low, self.at_high = self.b == self.low, self.b == self.low + 1

    @staticmethod
    def scratch(window):
        return [
            pltpu.VMEM((2, 3, window, window), jnp.float32),
            pltpu.SemaphoreType.DMA((2, 3, 2)),
            pltpu.SemaphoreType.DMA((2, 3)),
            pltpu.SemaphoreType.DMA((2, 3)),
            pltpu.SemaphoreType.DMA((2, 3, 2)),
        ]

    def partner(self):
        last = self.n_tx - 1
        col = jnp.where(
            self.b == 0, self.low, jnp.where(
                self.at_low, 0, jnp.where(self.at_high, last, self.low + 1)))
        exists = (self.b == 0) | (self.b == last) | self.at_low | self.at_high
        return (exists, self.a, col)

    def origin(self, way):
        return self.low if way == 0 else self.low + 1

    def stop(self, part):
        return 0 if part == 0 else self.n_tx - 1

    def first(self, way, index, part, source):
        return pltpu.make_async_remote_copy(
            src_ref=source.at[part],
            dst_ref=self.relay.at[way, index],
            send_sem=self.hop_send.at[way, index, part],
            recv_sem=self.hop_recv.at[way, index],
            device_id=(self.a, self.stop(part)),
            device_id_type=MESH,
        )

    def second(self, way, index, part, target):
        return pltpu.make_async_remote_copy(
            src_ref=self.relay.at[way, index],
            dst_ref=target.at[part],
            send_sem=self.end_send.at[way, index],
            recv_sem=self.end_recv.at[way, index, part],
            device_id=(self.a, self.origin(1 - way)),
            device_id_type=MESH,
        )

    def start(self, way, index, source):
        for part in range(2):
            self.first(way, index, part, source).start()

    def pass_on(self, way, index, source, target):
        for part in range(2):
            @pl.when(self.b == self.stop(part))
            def _():
                self.first(way, index, part, source).wait_recv()
                self.second(way, index, part, target).start()

    def passed(self, way, index, target):
        for part in range(2):
            @pl.when(self.b == self.stop(part))
            def _():
                self.second(way, index, part, target).wait_send()

    def wait_recv(self, way, index, target):
        for part in range(2):
            self.second(way, index, part, target).wait_recv()

    def wait_send(self, way, index, source):
        for part in range(2):
            self.first(way, index, part, source).wait_send()


class Sideways:
    def __init__(self, boundary, way, index, source, target, sems, slot):
        a, b, _, n_tx = place_of()
        self.boundary, self.way, self.index = boundary, way, index
        self.source, self.target = source, target
        step = 1 if way == 0 else -1
        self.direct = send_to(source, target, sems, slot, a, b + step)
        left, right = b > 0, b < n_tx - 1
        self.has_target, self.has_source = (right, left) if way == 0 else (left, right)
        self.from_origin = b == boundary.origin(way)
        self.at_end = b == boundary.origin(1 - way)

    def start(self):
        pl.when(self.from_origin)(lambda: self.boundary.start(self.way, self.index, self.source))
        pl.when(self.has_target & ~self.from_origin)(self.direct.start)

    def pass_on(self):
        self.boundary.pass_on(self.way, self.index, self.source, self.target)

    def wait_recv(self):
        pl.when(self.at_end)(lambda: self.boundary.wait_recv(self.way, self.index, self.target))
        pl.when(self.has_source & ~self.at_end)(self.direct.wait_recv)

    def wait_send(self):
        pl.when(self.from_origin)(lambda: self.boundary.wait_send(self.way, self.index, self.source))
        pl.when(self.has_target & ~self.from_origin)(self.direct.wait_send)

    def passed(self):
        self.boundary.passed(self.way, self.index, self.target)


def fetch_kernel(
    specimen, patterns, reorder, reorder_t, extended, measured_out,
    measured, send, recv, local, *boundary_scratch,
):
    a, b, n_ty, n_tx = place_of()
    window = measured.shape[1]
    tile = specimen.shape[1]
    up, down, left, right = a > 0, a < n_ty - 1, b > 0, b < n_tx - 1
    boundary = Boundary(boundary_scratch[0], boundary_scratch[1:])
    near = (True, a, b + 1 - 2 * lax.rem(b, 2))
    relays = [(b == 0, a, boundary.low + 1), (boundary.at_high, a, 0)]
    relays += [(b == n_tx - 1, a, boundary.low), (boundary.at_low, a, n_tx - 1)]
    greet([(up, a - 1, b), (down, a + 1, b), near, far_neighbour(a, b, n_tx), boundary.partner()] + relays)
    sems = (send, recv)
    first, second = pl.ds(0, window), pl.ds(window, tile - window)
    beyond, inside = pl.ds(tile, window), pl.ds(0, tile)
    up_a = send_to(specimen.at[:, first, first], extended.at[:, beyond, first], sems, 0, a - 1, b)
    up_b = send_to(specimen.at[:, first, second], extended.at[:, beyond, second], sems, 1, a - 1, b)

    def aside(index, source, rows):
        return Sideways(
            boundary, 1, index, source.at[:, rows, first], extended.at[:, rows, beyond], sems, 2 + index)

    aside_a = aside(0, specimen, first)
    aside_b = aside(1, specimen, second)
    corner = aside(2, extended, beyond)
    keep = pltpu.make_async_copy(specimen, extended.at[:, inside, inside], local.at[0])
    load = pltpu.make_async_copy(patterns.at[0], measured, local.at[1])
    pl.when(up)(up_a.start)
    aside_a.start()
    aside_b.start()
    load.start()
    keep.start()
    aside_a.pass_on()
    aside_b.pass_on()

    @pl.when(up)
    def _():
        up_a.wait_send()
        up_b.start()

    @pl.when(down)
    def _():
        up_a.wait_recv()
        corner.start()

    load.wait()

    def rearrange(slot, carry):
        def pieces(value):
            high, low = split(value)
            rest = (value - high.astype(jnp.float32) - low.astype(jnp.float32)).astype(jnp.bfloat16)
            return [high, low, rest]

        rows = jnp.dot(
            reorder[...], jnp.concatenate(pieces(measured[slot]), axis=0),
            preferred_element_type=jnp.float32)
        measured_out[slot] = jnp.dot(
            jnp.concatenate(pieces(rows), axis=1), reorder_t[...],
            preferred_element_type=jnp.float32)
        return carry

    lax.fori_loop(0, measured.shape[0], rearrange, 0)
    pl.when(down)(corner.pass_on)
    keep.wait()
    aside_a.wait_recv()
    aside_b.wait_recv()

    @pl.when(up)
    def _():
        up_b.wait_send()

    @pl.when(down)
    def _():
        up_b.wait_recv()
        corner.wait_recv()
        corner.wait_send()
        corner.passed()

    for strip in (aside_a, aside_b):
        strip.wait_send()
        strip.passed()


def fetch(specimen, patterns):
    window = patterns.shape[2]
    side = specimen.shape[1] + window
    table = reorder_table(window)
    vmem = pl.BlockSpec(memory_space=pltpu.VMEM)
    hbm = pl.BlockSpec(memory_space=pl.ANY)
    return pl.pallas_call(
        fetch_kernel,
        out_shape=(
            jax.ShapeDtypeStruct((2, side, side), jnp.float32),
            jax.ShapeDtypeStruct(patterns.shape[1:], jnp.float32),
        ),
        in_specs=[hbm, hbm, vmem, vmem],
        out_specs=(hbm, vmem),
        scratch_shapes=[
            pltpu.VMEM(patterns.shape[1:], jnp.float32),
            pltpu.SemaphoreType.DMA((5,)),
            pltpu.SemaphoreType.DMA((5,)),
            pltpu.SemaphoreType.DMA((2,)),
        ] + Boundary.scratch(window),
        compiler_params=pltpu.CompilerParams(
            collective_id=0, has_side_effects=True, vmem_limit_bytes=VMEM_LIMIT),
        name="fetch",
    )(specimen, patterns, jnp.asarray(np.tile(table, (1, 3))), jnp.asarray(np.tile(table.T, (3, 1))))


class ProbeSum:
    def __init__(self, terms, buffers, send, recv):
        self.terms = terms
        self.mate, self.mine, self.pieces, self.strips, self.full, self.other = buffers
        self.send, self.recv = send, recv
        self.a, self.b, self.n_ty, n_tx = place_of()
        self.core = lax.rem(self.b, 2)
        self.pair = self.b // 2
        self.n_pair = n_tx // 2
        self.mate_col = self.b + 1 - 2 * self.core
        self.rows = self.full.shape[0] // self.n_ty

    @staticmethod
    def scratch(window, n_ty, n_tx):
        rows = window // n_ty
        return [
            pltpu.VMEM((window, window), jnp.float32),
            pltpu.VMEM((window, window), jnp.float32),
            pltpu.VMEM((n_ty - 1, rows, window), jnp.float32),
            pltpu.VMEM((n_tx // 2, rows, window), jnp.float32),
            pltpu.VMEM((window, window), jnp.float32),
            pltpu.VMEM((window, window), jnp.float32),
            pltpu.SemaphoreType.DMA((5,)),
            pltpu.SemaphoreType.DMA((5,)),
        ]

    def partners(self):
        found = [(True, self.a, self.mate_col)]
        found += [(True, lax.rem(self.a + d, self.n_ty), self.b) for d in range(1, self.n_ty)]
        found += [(True, self.a, 2 * lax.rem(self.pair + d, self.n_pair) + self.core) for d in range(1, self.n_pair)]
        return found

    def to(self, source, target, stage, row, col):
        return send_to(source, target, (self.send, self.recv), stage, row, col)

    def own(self, ref, row):
        return ref.at[pl.ds(pl.multiple_of(row * self.rows, SUBLANES), self.rows), :]

    def start(self):
        self.to(self.terms.at[1 - self.core], self.mate, 0, self.a, self.mate_col).start()

    def scatter(self):
        self.to(self.terms.at[1 - self.core], self.mate, 0, self.a, self.mate_col).wait()
        self.mine[...] = self.terms[self.core] + self.mate[...]

        def go(d, carry):
            row = lax.rem(self.a + d, self.n_ty)
            self.to(self.own(self.mine, row), self.pieces.at[d - 1], 1, row, self.b).start()
            return carry

        lax.fori_loop(1, self.n_ty, go, 0)

    def across(self):
        wait_bytes(self.pieces, self.recv.at[1])
        total = self.own(self.mine, self.a)[...]
        for d in range(self.n_ty - 1):
            total = total + self.pieces[d]
        self.strips[self.pair] = total

        def go(d, carry):
            col = 2 * lax.rem(self.pair + d, self.n_pair) + self.core
            self.to(self.strips.at[self.pair], self.strips.at[self.pair], 2, self.a, col).start()
            return carry

        lax.fori_loop(1, self.n_pair, go, 0)

    def gather(self):
        wait_bytes(self.strips.at[pl.ds(0, self.n_pair - 1)], self.recv.at[2])
        total = self.strips[0]
        for i in range(1, self.n_pair):
            total = total + self.strips[i]
        self.own(self.full, self.a)[...] = total

        def go(d, carry):
            row = lax.rem(self.a + d, self.n_ty)
            self.to(self.own(self.full, self.a), self.own(self.full, self.a), 3, row, self.b).start()
            return carry

        lax.fori_loop(1, self.n_ty, go, 0)

    def share(self):
        wait_bytes(self.full.at[pl.ds(0, (self.n_ty - 1) * self.rows)], self.recv.at[3])
        self.to(self.full, self.other, 4, self.a, self.mate_col).start()

    def finish(self, probe, probe_out):
        step = PROBE_GAIN / (POS_DEV * self.n_ty * 2 * self.n_pair)
        probe_out[self.core] = probe[self.core] - step * self.full[...]
        self.to(self.full, self.other, 4, self.a, self.mate_col).wait()
        probe_out[1 - self.core] = probe[1 - self.core] - step * self.other[...]
        wait_bytes(self.pieces, self.send.at[1])
        wait_bytes(self.strips.at[pl.ds(0, self.n_pair - 1)], self.send.at[2])
        wait_bytes(self.full.at[pl.ds(0, (self.n_ty - 1) * self.rows)], self.send.at[3])


def far_neighbour(a, b, n_tx):
    core = lax.rem(b, 2)
    col = b - 1 + 2 * core
    return ((col >= 0) & (col < n_tx) & (b != n_tx // 2 - 1) & (b != n_tx // 2), a, col)


def exchange_kernel(
    grad, extended, probe, probe_grad, extended_out, probe_out,
    gv, ev, from_left, from_right, from_up, from_down, send, recv, local,
    *rest,
):
    a, b, n_ty, n_tx = place_of()
    window = probe.shape[1]
    side = gv.shape[1]
    tile = side - window
    core = lax.rem(b, 2)
    has_up, has_down, has_left, has_right = a > 0, a < n_ty - 1, b > 0, b < n_tx - 1
    odd = core == 1
    total = ProbeSum(probe_grad, rest[:6], *rest[6:8])
    boundary = Boundary(rest[8], rest[9:])
    greet(total.partners() + [far_neighbour(a, b, n_tx), boundary.partner()])
    sems = (send, recv)
    start, middle, end = pl.ds(0, window), pl.ds(window, tile - window), pl.ds(tile, window)

    def across(rows, index):
        return (
            Sideways(boundary, 0, index, grad.at[:, rows, end], from_left.at[:, rows, :], sems, 2 * index),
            Sideways(boundary, 1, index, grad.at[:, rows, start], from_right.at[:, rows, :], sems, 2 * index + 1),
        )

    def along(source, cols, index):
        return (
            send_to(source.at[:, end, cols], from_up.at[:, :, cols], sems, index, a + 1, b),
            send_to(source.at[:, start, cols], from_down.at[:, :, cols], sems, index + 1, a - 1, b),
        )

    right_top, left_top = across(start, 0)
    right_end, left_end = across(end, 1)
    right_mid, left_mid = across(middle, 2)
    down_1, up_1 = along(grad, middle, 6)
    down_0, up_0 = along(gv, start, 8)
    down_2, up_2 = along(gv, end, 10)
    keep_top = send_to(ev.at[:, start, start], extended_out.at[:, start, end], sems, 12, a, b - 1)
    keep_end = send_to(ev.at[:, end, start], extended_out.at[:, end, end], sems, 13, a, b - 1)

    load_grad = pltpu.make_async_copy(grad, gv, local.at[0])
    load_extended = pltpu.make_async_copy(extended, ev, local.at[1])

    outer = (right_top, right_end, left_top, left_end)
    for strip in outer:
        strip.start()
    pl.when(has_down)(down_1.start)
    pl.when(has_up)(up_1.start)
    total.start()
    load_grad.start()
    load_extended.start()
    total.scatter()
    right_top.pass_on()
    right_end.pass_on()
    total.across()
    left_top.pass_on()
    left_end.pass_on()
    total.gather()
    load_grad.wait()
    right_top.wait_recv()
    right_end.wait_recv()

    @pl.when(has_left)
    def _():
        gv[:, start, start] += from_left[:, start, :]
        gv[:, end, start] += from_left[:, end, :]

    pl.when(has_down)(down_0.start)
    pl.when(has_up)(up_0.start)
    left_top.wait_recv()
    left_end.wait_recv()

    @pl.when(has_right)
    def _():
        gv[:, start, end] += from_right[:, start, :]
        gv[:, end, end] += from_right[:, end, :]

    pl.when(has_down & odd)(down_2.start)
    pl.when(has_up & odd)(up_2.start)
    for strip in outer:
        strip.wait_send()
    right_mid.start()
    left_mid.start()
    right_mid.pass_on()
    left_mid.pass_on()
    total.share()
    load_extended.wait()
    right_mid.wait_recv()
    left_mid.wait_recv()

    @pl.when(has_left)
    def _():
        gv[:, middle, start] += from_left[:, middle, :]

    @pl.when(has_right)
    def _():
        gv[:, middle, end] += from_right[:, middle, :]

    ev[:, middle, :] -= OBJECT_STEP * gv[:, middle, :]
    store_mid = pltpu.make_async_copy(ev.at[:, middle, :], extended_out.at[:, middle, :], local.at[0])
    store_mid.start()

    def update(rows, cols, received, exists):
        @pl.when(exists)
        def _():
            ev[:, rows, cols] -= OBJECT_STEP * (gv[:, rows, cols] + received[:, :, cols])

        @pl.when(jnp.logical_not(exists))
        def _():
            ev[:, rows, cols] -= OBJECT_STEP * gv[:, rows, cols]

    pl.when(has_up)(down_0.wait_recv)
    pl.when(has_down)(up_0.wait_recv)
    update(start, start, from_up, has_up)
    update(end, start, from_down, has_down)

    @pl.when(odd)
    def _():
        keep_top.start()
        keep_end.start()

    pl.when(has_up)(down_1.wait_recv)
    pl.when(has_down)(up_1.wait_recv)
    update(start, middle, from_up, has_up)
    update(end, middle, from_down, has_down)
    inner = pl.ds(0, tile)
    store_top = pltpu.make_async_copy(ev.at[:, start, inner], extended_out.at[:, start, inner], local.at[1])
    store_end = pltpu.make_async_copy(ev.at[:, end, inner], extended_out.at[:, end, inner], local.at[2])
    store_top.start()
    store_end.start()

    @pl.when(odd)
    def _():
        pl.when(has_up)(down_2.wait_recv)
        pl.when(has_down)(up_2.wait_recv)
        update(start, end, from_up, has_up)
        update(end, end, from_down, has_down)
        rim_top = pltpu.make_async_copy(ev.at[:, start, end], extended_out.at[:, start, end], local.at[3])
        rim_end = pltpu.make_async_copy(ev.at[:, end, end], extended_out.at[:, end, end], local.at[4])
        rim_top.start()
        rim_end.start()
        rim_top.wait()
        rim_end.wait()
        keep_top.wait_send()
        keep_end.wait_send()

    total.finish(probe, probe_out)
    right_mid.wait_send()
    left_mid.wait_send()
    for strip in outer + (right_mid, left_mid):
        strip.passed()

    @pl.when(has_down)
    def _():
        down_0.wait_send()
        down_1.wait_send()
        pl.when(odd)(down_2.wait_send)

    @pl.when(has_up)
    def _():
        up_0.wait_send()
        up_1.wait_send()
        pl.when(odd)(up_2.wait_send)

    store_mid.wait()
    store_top.wait()
    store_end.wait()

    @pl.when(jnp.logical_not(odd))
    def _():
        keep_top.wait_recv()
        keep_end.wait_recv()


def exchange(grad, extended, illumination, probe_grad):
    window = illumination.shape[1]
    side = grad.shape[1]
    vmem = pl.BlockSpec(memory_space=pltpu.VMEM)
    hbm = pl.BlockSpec(memory_space=pl.ANY)
    return pl.pallas_call(
        exchange_kernel,
        out_shape=(
            jax.ShapeDtypeStruct(extended.shape, jnp.float32),
            jax.ShapeDtypeStruct(illumination.shape, jnp.float32),
        ),
        in_specs=[hbm, hbm, vmem, vmem],
        out_specs=(hbm, vmem),
        scratch_shapes=[
            pltpu.VMEM((2, side, side), jnp.float32),
            pltpu.VMEM((2, side, side), jnp.float32),
            pltpu.VMEM((2, side, window), jnp.float32),
            pltpu.VMEM((2, side, window), jnp.float32),
            pltpu.VMEM((2, window, side), jnp.float32),
            pltpu.VMEM((2, window, side), jnp.float32),
            pltpu.SemaphoreType.DMA((14,)),
            pltpu.SemaphoreType.DMA((14,)),
            pltpu.SemaphoreType.DMA((5,)),
        ] + ProbeSum.scratch(window, lax.axis_size("ty"), lax.axis_size("tx")) + Boundary.scratch(window),
        compiler_params=pltpu.CompilerParams(
            collective_id=1, has_side_effects=True, vmem_limit_bytes=VMEM_LIMIT),
        name="exchange",
    )(grad, extended, illumination, probe_grad)


def fold_kernel(
    grad, extended, probe, probe_grad, specimen_out, probe_out,
    gv, ev, corner, from_left, from_up, send, recv, local,
    *rest,
):
    a, b, n_ty, n_tx = place_of()
    window = probe.shape[1]
    side = gv.shape[1]
    tile = side - window
    has_up, has_down, has_left, has_right = a > 0, a < n_ty - 1, b > 0, b < n_tx - 1
    total = ProbeSum(probe_grad, rest[:6], *rest[6:8])
    boundary = Boundary(rest[8], rest[9:])
    greet(total.partners() + [far_neighbour(a, b, n_tx), boundary.partner()])
    sems = (send, recv)
    start, middle, end = pl.ds(0, window), pl.ds(window, tile - window), pl.ds(tile, window)
    inner = pl.ds(0, tile)

    def across(rows, index):
        return Sideways(boundary, 0, index, grad.at[:, rows, end], from_left.at[:, rows, :], sems, index)

    right_end = across(end, 0)
    right_top = across(start, 1)
    right_mid = across(middle, 2)
    down_1 = send_to(grad.at[:, end, middle], from_up.at[:, :, middle], sems, 3, a + 1, b)
    down_0 = send_to(corner, from_up.at[:, :, start], sems, 4, a + 1, b)
    load_grad = pltpu.make_async_copy(grad.at[:, :, inner], gv, local.at[0])
    load_extended = pltpu.make_async_copy(extended.at[:, inner, inner], ev, local.at[1])
    right_end.start()
    pl.when(has_down)(down_1.start)
    total.start()
    load_grad.start()
    load_extended.start()
    total.scatter()
    right_end.pass_on()
    total.across()
    load_grad.wait()
    right_end.wait_recv()

    @pl.when(has_left)
    def _():
        corner[...] = gv[:, end, start] + from_left[:, end, :]

    @pl.when(jnp.logical_not(has_left))
    def _():
        corner[...] = gv[:, end, start]

    pl.when(has_down)(down_0.start)
    right_end.wait_send()
    right_top.start()
    right_mid.start()
    total.gather()
    right_top.pass_on()
    right_mid.pass_on()
    load_extended.wait()
    ev[...] -= OBJECT_STEP * gv[:, inner, :]
    total.share()
    right_top.wait_recv()
    right_mid.wait_recv()

    @pl.when(has_left)
    def _():
        ev[:, :, start] -= OBJECT_STEP * from_left[:, inner, :]

    @pl.when(has_up)
    def _():
        down_1.wait_recv()
        down_0.wait_recv()
        ev[:, start, :] -= OBJECT_STEP * from_up[...]

    specimen_out[...] = ev[...]
    total.finish(probe, probe_out)
    right_top.wait_send()
    right_mid.wait_send()
    for strip in (right_end, right_top, right_mid):
        strip.passed()

    @pl.when(has_down)
    def _():
        down_1.wait_send()
        down_0.wait_send()


def fold(grad, extended, illumination, probe_grad):
    window = illumination.shape[1]
    side = grad.shape[1]
    tile = side - window
    vmem = pl.BlockSpec(memory_space=pltpu.VMEM)
    hbm = pl.BlockSpec(memory_space=pl.ANY)
    return pl.pallas_call(
        fold_kernel,
        out_shape=(
            jax.ShapeDtypeStruct((2, tile, tile), jnp.float32),
            jax.ShapeDtypeStruct(illumination.shape, jnp.float32),
        ),
        in_specs=[hbm, hbm, vmem, vmem],
        out_specs=(vmem, vmem),
        scratch_shapes=[
            pltpu.VMEM((2, side, tile), jnp.float32),
            pltpu.VMEM((2, tile, tile), jnp.float32),
            pltpu.VMEM((2, window, window), jnp.float32),
            pltpu.VMEM((2, side, window), jnp.float32),
            pltpu.VMEM((2, window, tile), jnp.float32),
            pltpu.SemaphoreType.DMA((5,)),
            pltpu.SemaphoreType.DMA((5,)),
            pltpu.SemaphoreType.DMA((2,)),
        ] + ProbeSum.scratch(window, lax.axis_size("ty"), lax.axis_size("tx")) + Boundary.scratch(window),
        compiler_params=pltpu.CompilerParams(
            collective_id=2, has_side_effects=True, vmem_limit_bytes=VMEM_LIMIT),
        name="fold",
    )(grad, extended, illumination, probe_grad)


def body(specimen, illumination, patterns, scan_offsets, counts):
    window = illumination.shape[1]
    tile = specimen.shape[1]
    row_anchor = lax.axis_index("ty") * tile
    col_anchor = lax.axis_index("tx") * tile
    offsets = scan_offsets[0] - jnp.stack([row_anchor, col_anchor])[None, :].astype(jnp.int32)
    count = counts.reshape(1)
    dft = tables(window)
    extended, measured = fetch(specimen, patterns)
    for iteration in range(ITERS):
        grad, probe_grad = slot_gradients(count, offsets, extended, illumination, measured, dft)
        if iteration < ITERS - 1:
            extended, illumination = exchange(grad, extended, illumination, probe_grad)
        else:
            specimen, illumination = fold(grad, extended, illumination, probe_grad)
    return (specimen, illumination)


def solution(mesh):
    placed = (
        P(None, "ty", "tx"),
        P(),
        P("ty", "tx", None, None),
        P("ty", "tx", None),
        P("ty", "tx"),
    )
    return jax.shard_map(
        body, mesh=mesh, in_specs=placed, out_specs=(P(None, "ty", "tx"), P()), check_vma=False
    )
```

```python
import functools

import jax
import jax.numpy as jnp
import ml_dtypes
import numpy as np
from jax import lax
from jax.experimental import pallas as pl
from jax.experimental.pallas import tpu as pltpu
from jax.sharding import PartitionSpec as P

POS_DEV = 3
ITERS = 2
OBJECT_STEP = 0.05
PROBE_GAIN = 0.5
MESH = pl.DeviceIdType.MESH
VMEM_LIMIT = 48 * 1024 * 1024
SUBLANES = 8
TOGETHER = 3


def real_table(window):
    half = window // 2
    k = np.arange(window)
    freq = np.where(k <= half, k, k - half)
    angles = 2.0 * np.pi * ((freq[:, None] * k[None, :]) % window) / window
    table = np.where((k <= half)[:, None], np.cos(angles), np.sin(angles))
    return table / np.sqrt(window)


def split_table(table):
    high = table.astype(ml_dtypes.bfloat16)
    low = (table - high.astype(np.float64)).astype(ml_dtypes.bfloat16)
    return high, low


def tables(window):
    high, low = split_table(real_table(window))
    return [jnp.asarray(t) for t in (high, low, high.T, low.T)]


def split(value):
    high = value.astype(jnp.bfloat16)
    low = (value - high.astype(jnp.float32)).astype(jnp.bfloat16)
    return high, low


def dot(left, right):
    return jnp.dot(left, right, preferred_element_type=jnp.float32)


def left_product(table, value):
    high, low = split(value)
    return dot(table[0][...], high) + dot(table[1][...], high) + dot(table[0][...], low)


def right_product(value, table):
    high, low = split(value)
    return dot(high, table[0][...]) + dot(high, table[1][...]) + dot(low, table[0][...])


def compute_kernel(
    count_ref, offsets_ref, specimen_ref, probe_ref, measured_ref,
    high_ref, low_ref, high_t_ref, low_t_ref,
    grad_ref, probe_grad_ref,
    windows, levels, window_sems, level_sems,
):
    table, table_t = (high_ref, low_ref), (high_t_ref, low_t_ref)
    window = probe_ref.shape[1]
    half = window // 2
    lanes = 128
    blocks = window // lanes
    lane = lax.broadcasted_iota(jnp.int32, (window + SUBLANES, lanes), 1)
    sublane = lax.broadcasted_iota(jnp.int32, (window // SUBLANES, SUBLANES, lanes), 1)
    sublane_ext = lax.broadcasted_iota(jnp.int32, (window // SUBLANES + 1, SUBLANES, lanes), 1)
    first_row = lax.broadcasted_iota(jnp.int32, (half, window), 0) == 0
    first_col = lax.broadcasted_iota(jnp.int32, (window, half), 1) == 0

    probe_real, probe_imag = probe_ref[0], probe_ref[1]

    def position(slot):
        row = offsets_ref[slot, 0]
        col = offsets_ref[slot, 1]
        row_block = pl.multiple_of((row // SUBLANES) * SUBLANES, SUBLANES)
        col_block = pl.multiple_of((col // lanes) * lanes, lanes)
        return row_block, col_block, row - row_block, col - col_block

    def place(where, part, j):
        return (
            part,
            pl.ds(where[0], window + SUBLANES),
            pl.ds(pl.multiple_of(where[1] + lanes * j, lanes), lanes),
        )

    def loads(slot):
        row_block, col_block, _, _ = position(slot)
        rows, cols = pl.ds(row_block, window + SUBLANES), pl.ds(col_block, window + lanes)
        return (
            pltpu.make_async_copy(specimen_ref.at[:, rows, cols], windows.at[slot], window_sems.at[slot]),
            pltpu.make_async_copy(measured_ref.at[slot], levels.at[slot], level_sems.at[slot]),
        )

    def cut(slot, where, part):
        row_rest, col_rest = where[2:]
        keep = lane < lanes - col_rest
        pieces = [
            pltpu.roll(
                windows[slot, part, :, lanes * j:lanes * (j + 1)], lax.rem(lanes - col_rest, lanes), 1)
            for j in range(blocks + 1)
        ]
        columns = []
        for j in range(blocks):
            taken = jnp.where(keep, pieces[j], pieces[j + 1])
            taken = taken.reshape(window // SUBLANES + 1, SUBLANES, lanes)
            taken = pltpu.roll(taken, lax.rem(SUBLANES - row_rest, SUBLANES), 1)
            upper = sublane < SUBLANES - row_rest
            columns.append(jnp.where(upper, taken[:-1], taken[1:]).reshape(window, lanes))
        return jnp.concatenate(columns, axis=1)

    def add_term(where, part, term):
        row_rest, col_rest = where[2:]
        before = lane < col_rest
        above = sublane_ext < row_rest
        turned = []
        for j in range(blocks):
            piece = term[:, lanes * j:lanes * (j + 1)]
            piece = piece.reshape(window // SUBLANES, SUBLANES, lanes)
            piece = pltpu.roll(piece, row_rest, 1)
            edge = jnp.zeros((1, SUBLANES, lanes), jnp.float32)
            piece = jnp.where(
                above,
                jnp.concatenate([edge, piece], axis=0),
                jnp.concatenate([piece, edge], axis=0),
            ).reshape(window + SUBLANES, lanes)
            turned.append(pltpu.roll(piece, col_rest, 1))
        for j in range(blocks + 1):
            if j == 0:
                add = jnp.where(before, 0.0, turned[0])
            elif j == blocks:
                add = jnp.where(before, turned[-1], 0.0)
            else:
                add = jnp.where(before, turned[j - 1], turned[j])
            grad_ref[place(where, part, j)] += add

    def exit_wave(patch):
        real, imag = patch
        psi_real = probe_real * real - probe_imag * imag
        psi_imag = probe_real * imag + probe_imag * real
        return jnp.concatenate([psi_real, psi_imag], axis=1)

    def unfold_rows(both):
        u_top, v_top = both[:half, :window], both[:half, window:]
        u_bot, v_bot = both[half:, :window], both[half:, window:]
        u_add = jnp.where(first_row, 0.0, u_bot)
        v_add = jnp.where(first_row, 0.0, v_bot)
        return jnp.concatenate([
            u_top + v_add, jnp.where(first_row, u_bot, u_top - v_bot),
            v_top - u_add, jnp.where(first_row, v_bot, v_top + u_bot)], axis=0)

    def unfold_cols(both):
        u_top, v_top = both[:window, :half], both[window:, :half]
        u_bot, v_bot = both[:window, half:], both[window:, half:]
        u_add = jnp.where(first_col, 0.0, u_bot)
        v_add = jnp.where(first_col, 0.0, v_bot)
        far_real = jnp.concatenate([u_top + v_add, jnp.where(first_col, u_bot, u_top - v_bot)], axis=1)
        far_imag = jnp.concatenate([v_top - u_add, jnp.where(first_col, v_bot, v_top + u_bot)], axis=1)
        return far_real, far_imag

    def fold_rows(g_real, g_imag):
        r_top, r_bot = g_real[:half], g_real[half:]
        i_top, i_bot = g_imag[:half], g_imag[half:]
        z_real = jnp.concatenate(
            [r_top + jnp.where(first_row, 0.0, r_bot), jnp.where(first_row, r_bot, i_bot - i_top)], axis=0)
        z_imag = jnp.concatenate(
            [i_top + jnp.where(first_row, 0.0, i_bot), jnp.where(first_row, i_bot, r_top - r_bot)], axis=0)
        return jnp.concatenate([z_real, z_imag], axis=1)

    def fold_cols(both):
        r_top, r_bot = both[:, :half], both[:, half:window]
        i_top, i_bot = both[:, window:window + half], both[:, window + half:]
        z_real = jnp.concatenate(
            [r_top + jnp.where(first_col, 0.0, r_bot), jnp.where(first_col, r_bot, i_bot - i_top)], axis=1)
        z_imag = jnp.concatenate(
            [i_top + jnp.where(first_col, 0.0, i_bot), jnp.where(first_col, i_bot, r_top - r_bot)], axis=1)
        return jnp.concatenate([z_real, z_imag], axis=0)

    def visit(step, carry):
        slots = [TOGETHER * step + i for i in range(TOGETHER)]
        where = [position(slot) for slot in slots]
        live = [(slot < count_ref[0]).astype(jnp.float32) for slot in slots]
        for slot in slots:
            for copy in loads(slot):
                copy.wait()
        patches = [(cut(slot, w, 0), cut(slot, w, 1)) for slot, w in zip(slots, where)]
        waves = [left_product(table, exit_wave(patch)) for patch in patches]
        waves = [right_product(unfold_rows(wave), table_t) for wave in waves]
        sources = []
        for wave, slot, on in zip(waves, slots, live):
            far_real, far_imag = unfold_cols(wave)
            factor = on * (far_real * far_real + far_imag * far_imag - levels[slot])
            sources.append(fold_rows(factor * far_real, factor * far_imag))
        waves = [left_product(table_t, source) for source in sources]
        waves = [right_product(fold_cols(wave), table) for wave in waves]
        for wave, patch, w in zip(waves, patches, where):
            chi_real, chi_imag = wave[:window], wave[window:]
            probe_grad_ref[0] += patch[0] * chi_real + patch[1] * chi_imag
            probe_grad_ref[1] += patch[0] * chi_imag - patch[1] * chi_real
            add_term(w, 0, probe_real * chi_real + probe_imag * chi_imag)
            add_term(w, 1, probe_real * chi_imag - probe_imag * chi_real)
        return carry

    steps = (count_ref[0] + TOGETHER - 1) // TOGETHER

    def fetch_slot(slot, carry):
        for copy in loads(slot):
            copy.start()
        return carry

    lax.fori_loop(0, steps * TOGETHER, fetch_slot, 0)
    grad_ref[...] = jnp.zeros_like(grad_ref)
    probe_grad_ref[...] = jnp.zeros_like(probe_grad_ref)
    lax.fori_loop(0, steps, visit, 0)


def slot_gradients(count, offsets, extended, illumination, measured, dft):
    smem = pl.BlockSpec(memory_space=pltpu.SMEM)
    vmem = pl.BlockSpec(memory_space=pltpu.VMEM)
    hbm = pl.BlockSpec(memory_space=pl.ANY)
    slots, window, _ = measured.shape
    return pl.pallas_call(
        compute_kernel,
        out_shape=(
            jax.ShapeDtypeStruct(extended.shape, jnp.float32),
            jax.ShapeDtypeStruct(illumination.shape, jnp.float32),
        ),
        in_specs=[smem, smem, hbm, vmem, hbm] + [vmem] * 4,
        out_specs=(vmem, vmem),
        scratch_shapes=[
            pltpu.VMEM((slots, 2, window + SUBLANES, window + 128), jnp.float32),
            pltpu.VMEM(measured.shape, jnp.float32),
            pltpu.SemaphoreType.DMA((slots,)),
            pltpu.SemaphoreType.DMA((slots,)),
        ],
        compiler_params=pltpu.CompilerParams(vmem_limit_bytes=VMEM_LIMIT),
        name="slot_gradients",
    )(count, offsets, extended, illumination, measured, *dft)


def place_of():
    return lax.axis_index("ty"), lax.axis_index("tx"), lax.axis_size("ty"), lax.axis_size("tx")


def send_to(source, target, sems, index, row, col):
    send_sem, recv_sem = sems
    return pltpu.make_async_remote_copy(
        src_ref=source,
        dst_ref=target,
        send_sem=send_sem.at[index],
        recv_sem=recv_sem.at[index],
        device_id=(row, col),
        device_id_type=MESH,
    )


def wait_bytes(ref, sem):
    pltpu.make_async_copy(ref, ref, sem).wait()


def greet(partners):
    barrier = pltpu.get_barrier_semaphore()
    for exists, row, col in partners:
        @pl.when(exists)
        def _():
            pl.semaphore_signal(barrier, inc=1, device_id=(row, col), device_id_type=MESH)
    pl.semaphore_wait(barrier, sum(jnp.int32(exists) for exists, _, _ in partners))


class Boundary:
    LINES = 4

    def __init__(self, relay, sems):
        self.relay = relay
        self.first_send, self.hop_recv, self.hop_send, self.last_recv = sems
        self.a, self.b, _, n = place_of()
        half = n // 2
        self.low, self.high = half - 1, half
        if n >= 16:
            inner = ((half, half + 3, 3, half - 1), (half, n - 4, half - 4, half - 1))
        else:
            inner = ((half, half + 2, 2, half - 1), (half, n - 3, half - 3, half - 1))
        self.paths = ((half, 0, half - 1), *inner, (half, n - 1, half - 1))
        self.at_low, self.at_high = self.b == self.low, self.b == self.high

    @staticmethod
    def scratch(window):
        return [
            pltpu.VMEM((2, 3, window // 2, window), jnp.float32),
            pltpu.SemaphoreType.DMA((2, 3, Boundary.LINES)),
            pltpu.SemaphoreType.DMA((2, 3)),
            pltpu.SemaphoreType.DMA((2, 3)),
            pltpu.SemaphoreType.DMA((2, 3, Boundary.LINES)),
        ]

    def partners(self, every):
        pairs = sorted({tuple(sorted(pair)) for path in self.paths for pair in zip(path, path[1:])})
        found = []
        for p, q in pairs:
            if p // 2 != q // 2 and (every or p % 2 != q % 2):
                found += [(self.b == p, self.a, q), (self.b == q, self.a, p)]
        return found

    def path(self, way, line):
        return self.paths[line] if way == 1 else self.paths[line][::-1]

    def origin(self, way):
        return self.low if way == 0 else self.high

    @staticmethod
    def quarter(ref, line):
        rows = ref.shape[1] // 2
        return ref.at[line // 2, pl.ds(line % 2 * rows, rows), :]

    def leg(self, way, index, line, k, source, target):
        path = self.path(way, line)
        last = k == len(path) - 2
        return pltpu.make_async_remote_copy(
            src_ref=self.quarter(source, line) if k == 0 else self.relay.at[way, index],
            dst_ref=self.quarter(target, line) if last else self.relay.at[way, index],
            send_sem=self.first_send.at[way, index, line] if k == 0 else self.hop_send.at[way, index],
            recv_sem=self.last_recv.at[way, index, line] if last else self.hop_recv.at[way, index],
            device_id=(self.a, path[k + 1]),
            device_id_type=MESH,
        )

    def start(self, way, index, source, target):
        for line in range(self.LINES):
            self.leg(way, index, line, 0, source, target).start()

    def relays(self, way):
        return [(line, k, node) for line in range(self.LINES)
                for k, node in enumerate(self.path(way, line)) if 0 < k < len(self.path(way, line)) - 1]

    def pass_on(self, way, index, source, target):
        for line, k, node in self.relays(way):
            @pl.when(self.b == node)
            def _():
                self.leg(way, index, line, k - 1, source, target).wait_recv()
                self.leg(way, index, line, k, source, target).start()

    def passed(self, way, index, source, target):
        for line, k, node in self.relays(way):
            @pl.when(self.b == node)
            def _():
                self.leg(way, index, line, k, source, target).wait_send()

    def wait_recv(self, way, index, source, target):
        for line in range(self.LINES):
            self.leg(way, index, line, len(self.path(way, line)) - 2, source, target).wait_recv()

    def wait_send(self, way, index, source, target):
        for line in range(self.LINES):
            self.leg(way, index, line, 0, source, target).wait_send()


class Sideways:
    def __init__(self, boundary, way, index, source, target, sems, slot):
        a, b, _, n_tx = place_of()
        self.boundary = boundary
        self.strip = (way, index, source, target)
        step = 1 if way == 0 else -1
        self.direct = send_to(source, target, sems, slot, a, b + step)
        left, right = b > 0, b < n_tx - 1
        self.has_target, self.has_source = (right, left) if way == 0 else (left, right)
        self.from_origin = b == boundary.origin(way)
        self.at_end = b == boundary.origin(1 - way)

    def start(self):
        self.start_relayed()
        self.start_direct()

    def start_relayed(self):
        pl.when(self.from_origin)(lambda: self.boundary.start(*self.strip))

    def start_direct(self):
        pl.when(self.has_target & ~self.from_origin)(self.direct.start)

    def pass_on(self):
        self.boundary.pass_on(*self.strip)

    def wait_recv(self):
        pl.when(self.at_end)(lambda: self.boundary.wait_recv(*self.strip))
        pl.when(self.has_source & ~self.at_end)(self.direct.wait_recv)

    def wait_send(self):
        pl.when(self.from_origin)(lambda: self.boundary.wait_send(*self.strip))
        pl.when(self.has_target & ~self.from_origin)(self.direct.wait_send)

    def passed(self):
        self.boundary.passed(*self.strip)


def fetch_kernel(
    specimen, patterns, extended, measured_out,
    measured, send, recv, local, *rest,
):
    a, b, n_ty, n_tx = place_of()
    window = measured.shape[1]
    tile = specimen.shape[1]
    half = window // 2
    up, down, left, right = a > 0, a < n_ty - 1, b > 0, b < n_tx - 1
    boundary = Boundary(rest[0], rest[1:])
    near = (True, a, b + 1 - 2 * lax.rem(b, 2))
    greet([(up, a - 1, b), (down, a + 1, b), near, far_neighbour(a, b, n_tx)] + boundary.partners(True))
    sems = (send, recv)
    first, second = pl.ds(0, window), pl.ds(window, tile - window)
    beyond, inside = pl.ds(tile, window), pl.ds(0, tile)

    def aside(index, source, rows):
        return Sideways(
            boundary, 1, index, source.at[:, rows, first], extended.at[:, rows, beyond], sems, 2 + index)

    up_a = send_to(specimen.at[:, first, first], extended.at[:, beyond, first], sems, 0, a - 1, b)
    up_b = send_to(specimen.at[:, first, second], extended.at[:, beyond, second], sems, 1, a - 1, b)
    aside_a = aside(0, specimen, first)
    aside_b = aside(1, specimen, second)
    corner = send_to(
        extended.at[:, beyond, first], extended.at[:, beyond, beyond], sems, 4, a, b - 1)
    corner_up = send_to(
        extended.at[:, first, beyond], extended.at[:, beyond, beyond], sems, 5, a - 1, b)
    corner_left = down & left & ~boundary.at_high
    keep = pltpu.make_async_copy(specimen, extended.at[:, inside, inside], local.at[0])
    load = pltpu.make_async_copy(patterns.at[0], measured, local.at[1])
    pl.when(up)(up_a.start)
    aside_a.start()
    aside_b.start()
    load.start()
    keep.start()
    aside_a.pass_on()

    @pl.when(up)
    def _():
        up_a.wait_send()
        up_b.start()

    aside_b.pass_on()

    pl.when(down)(up_a.wait_recv)
    pl.when(corner_left)(corner.start)

    @pl.when(boundary.at_low)
    def _():
        aside_a.wait_recv()
        pl.when(up)(corner_up.start)

    load.wait()
    row = lax.broadcasted_iota(jnp.int32, (window, window), 0)
    col = lax.broadcasted_iota(jnp.int32, (window, window), 1)

    def order(place, freq):
        picked = jnp.where(place <= half, place, window + half - place) == freq
        return picked.astype(jnp.float32).astype(jnp.bfloat16)

    reorder = jnp.concatenate([order(row, col)] * 3, axis=1)
    reorder_back = jnp.concatenate([order(col, row)] * 3, axis=0)

    def rearrange(slot, carry):
        def pieces(value):
            high, low = split(value)
            rest = (value - high.astype(jnp.float32) - low.astype(jnp.float32)).astype(jnp.bfloat16)
            return [high, low, rest]

        rows = jnp.dot(
            reorder, jnp.concatenate(pieces(measured[slot]), axis=0), preferred_element_type=jnp.float32)
        measured_out[slot] = jnp.dot(
            jnp.concatenate(pieces(rows), axis=1), reorder_back, preferred_element_type=jnp.float32)
        return carry

    lax.fori_loop(0, measured.shape[0], rearrange, 0)
    keep.wait()
    pl.when(~boundary.at_low)(aside_a.wait_recv)
    aside_b.wait_recv()
    pl.when(up)(up_b.wait_send)
    pl.when(down)(up_b.wait_recv)
    pl.when(corner_left)(corner.wait_send)
    pl.when(down & right & ~boundary.at_low)(corner.wait_recv)

    @pl.when(boundary.at_low)
    def _():
        pl.when(up)(corner_up.wait_send)
        pl.when(down)(corner_up.wait_recv)

    for strip in (aside_a, aside_b):
        strip.wait_send()
        strip.passed()


def fetch(specimen, patterns):
    window = patterns.shape[2]
    side = specimen.shape[1] + window
    vmem = pl.BlockSpec(memory_space=pltpu.VMEM)
    hbm = pl.BlockSpec(memory_space=pl.ANY)
    return pl.pallas_call(
        fetch_kernel,
        out_shape=(
            jax.ShapeDtypeStruct((2, side, side), jnp.float32),
            jax.ShapeDtypeStruct(patterns.shape[1:], jnp.float32),
        ),
        in_specs=[hbm, hbm],
        out_specs=(hbm, vmem),
        scratch_shapes=[
            pltpu.VMEM(patterns.shape[1:], jnp.float32),
            pltpu.SemaphoreType.DMA((6,)),
            pltpu.SemaphoreType.DMA((6,)),
            pltpu.SemaphoreType.DMA((2,)),
        ] + Boundary.scratch(window),
        compiler_params=pltpu.CompilerParams(
            collective_id=0, has_side_effects=True, vmem_limit_bytes=VMEM_LIMIT),
        name="fetch",
    )(specimen, patterns)


class ProbeSum:
    STAGES = 7

    def __init__(self, terms, buffers, send, recv):
        self.terms = terms
        self.mate, self.mine, self.y_in, self.y_sum, self.z_in, self.x_in, self.z_out, self.full, self.other = buffers
        self.send, self.recv = send, recv
        self.a, self.b, n_ty, n_tx = place_of()
        self.n_x, self.n_y, self.n_z = self.sizes(n_ty, n_tx)
        self.n_low = self.n_z // 2
        self.devices = n_ty * n_tx
        self.core = lax.rem(self.b, 2)
        self.y = lax.rem(self.b // 2, self.n_y)
        self.x = lax.rem(self.a, self.n_x)
        self.z = self.b // (2 * self.n_y) * self.n_low + self.a // self.n_x
        self.mate_col = self.b + 1 - 2 * self.core
        self.y_rows = self.full.shape[0] // self.n_y
        self.z_rows = self.y_rows // self.n_z

    @staticmethod
    def sizes(n_ty, n_tx):
        n_x = 4 if n_ty == 16 else 2
        return n_x, n_tx // 4, 2 * (n_ty // n_x)

    @staticmethod
    def scratch(window, n_ty, n_tx):
        n_x, n_y, n_z = ProbeSum.sizes(n_ty, n_tx)
        y_rows = window // n_y
        z_rows = y_rows // n_z
        shapes = [
            (window, window), (window, window), (n_y - 1, y_rows, window), (y_rows, window),
            (n_z - 1, z_rows, window), (n_x, z_rows, window), (y_rows, window),
            (window, window), (window, window),
        ]
        return [pltpu.VMEM(shape, jnp.float32) for shape in shapes] + [
            pltpu.SemaphoreType.DMA((ProbeSum.STAGES,)),
            pltpu.SemaphoreType.DMA((ProbeSum.STAGES,)),
        ]

    def at_y(self, y):
        return self.a, (self.b // (2 * self.n_y)) * 2 * self.n_y + 2 * y + self.core

    def at_z(self, z):
        return lax.rem(z, self.n_low) * self.n_x + self.x, (z // self.n_low) * 2 * self.n_y + 2 * self.y + self.core

    def at_x(self, x):
        return self.a - self.x + x, self.b

    def partners(self):
        found = [(True, self.a, self.mate_col)]
        found += [(True, *self.at_y(lax.rem(self.y + d, self.n_y))) for d in range(1, self.n_y)]
        found += [(True, *self.at_z(lax.rem(self.z + d, self.n_z))) for d in range(1, self.n_z)]
        found += [(True, *self.at_x(lax.rem(self.x + d, self.n_x))) for d in range(1, self.n_x)]
        n_ty = self.n_low * self.n_x
        wraps_down = (self.x == self.n_x - 1) & (self.a < n_ty - 1)
        wraps_up = (self.x == 0) & (self.a > 0)
        found.append((wraps_down | wraps_up, jnp.where(wraps_up, self.a - 1, self.a + 1), self.b))
        return found

    def to(self, source, target, stage, row, col):
        return send_to(source, target, (self.send, self.recv), stage, row, col)

    @staticmethod
    def rows(ref, index, count):
        return ref.at[pl.ds(pl.multiple_of(index * count, SUBLANES), count), :]

    def each(self, count, go):
        def step(d, carry):
            go(d)
            return carry

        lax.fori_loop(1, count, step, 0)

    def start(self):
        self.to(self.terms.at[1 - self.core], self.mate, 0, self.a, self.mate_col).start()

    def scatter_y(self):
        self.to(self.terms.at[1 - self.core], self.mate, 0, self.a, self.mate_col).wait()
        self.mine[...] = self.terms[self.core] + self.mate[...]

        def go(d):
            y = lax.rem(self.y + d, self.n_y)
            self.to(self.rows(self.mine, y, self.y_rows), self.y_in.at[d - 1], 1, *self.at_y(y)).start()

        self.each(self.n_y, go)

    def scatter_z(self):
        wait_bytes(self.y_in, self.recv.at[1])
        total = self.rows(self.mine, self.y, self.y_rows)[...]
        for d in range(self.n_y - 1):
            total = total + self.y_in[d]
        self.y_sum[...] = total

        def go(d):
            z = lax.rem(self.z + d, self.n_z)
            self.to(self.rows(self.y_sum, z, self.z_rows), self.z_in.at[d - 1], 2, *self.at_z(z)).start()

        self.each(self.n_z, go)

    def across_x(self):
        wait_bytes(self.z_in, self.recv.at[2])
        total = self.rows(self.y_sum, self.z, self.z_rows)[...]
        for d in range(self.n_z - 1):
            total = total + self.z_in[d]
        self.x_in[self.x] = total

        def go(d):
            x = lax.rem(self.x + d, self.n_x)
            self.to(self.x_in.at[self.x], self.x_in.at[self.x], 3, *self.at_x(x)).start()

        self.each(self.n_x, go)

    def gather_z(self):
        wait_bytes(self.x_in.at[pl.ds(0, self.n_x - 1)], self.recv.at[3])
        total = self.x_in[0]
        for i in range(1, self.n_x):
            total = total + self.x_in[i]
        own = self.rows(self.z_out, self.z, self.z_rows)
        own[...] = total

        def go(d):
            z = lax.rem(self.z + d, self.n_z)
            self.to(own, own, 4, *self.at_z(z)).start()

        self.each(self.n_z, go)

    def gather_y(self):
        wait_bytes(self.z_out.at[pl.ds(0, (self.n_z - 1) * self.z_rows)], self.recv.at[4])
        own = self.rows(self.full, self.y, self.y_rows)
        own[...] = self.z_out[...]

        def go(d):
            y = lax.rem(self.y + d, self.n_y)
            self.to(self.z_out, own, 5, *self.at_y(y)).start()

        self.each(self.n_y, go)

    def share(self):
        wait_bytes(self.full.at[pl.ds(0, (self.n_y - 1) * self.y_rows)], self.recv.at[5])
        self.to(self.full, self.other, 6, self.a, self.mate_col).start()

    def finish(self, probe, probe_out):
        step = PROBE_GAIN / (POS_DEV * self.devices)
        probe_out[self.core] = probe[self.core] - step * self.full[...]
        self.to(self.full, self.other, 6, self.a, self.mate_col).wait()
        probe_out[1 - self.core] = probe[1 - self.core] - step * self.other[...]
        wait_bytes(self.y_in, self.send.at[1])
        wait_bytes(self.z_in, self.send.at[2])
        wait_bytes(self.x_in.at[pl.ds(0, self.n_x - 1)], self.send.at[3])
        wait_bytes(self.z_out.at[pl.ds(0, (self.n_z - 1) * self.z_rows)], self.send.at[4])
        wait_bytes(self.full.at[pl.ds(0, (self.n_y - 1) * self.y_rows)], self.send.at[5])


def far_neighbour(a, b, n_tx):
    core = lax.rem(b, 2)
    col = b - 1 + 2 * core
    return ((col >= 0) & (col < n_tx) & (b != n_tx // 2 - 1) & (b != n_tx // 2), a, col)


def exchange_kernel(
    grad, extended, probe, probe_grad, extended_out, probe_out,
    gv, ev, from_left, from_right, from_up, from_down, send, recv, local,
    *rest,
):
    a, b, n_ty, n_tx = place_of()
    window = probe.shape[1]
    side = gv.shape[1]
    tile = side - window
    core = lax.rem(b, 2)
    has_up, has_down, has_left, has_right = a > 0, a < n_ty - 1, b > 0, b < n_tx - 1
    odd = core == 1
    total = ProbeSum(probe_grad, rest[:9], *rest[9:11])
    boundary = Boundary(rest[11], rest[12:])
    greet(total.partners() + [far_neighbour(a, b, n_tx)] + boundary.partners(False))
    sems = (send, recv)
    start, middle, end = pl.ds(0, window), pl.ds(window, tile - window), pl.ds(tile, window)

    def across(rows, index):
        return (
            Sideways(boundary, 0, index, grad.at[:, rows, end], from_left.at[:, rows, :], sems, 2 * index),
            Sideways(boundary, 1, index, grad.at[:, rows, start], from_right.at[:, rows, :], sems, 2 * index + 1),
        )

    def along(source, cols, index):
        return (
            send_to(source.at[:, end, cols], from_up.at[:, :, cols], sems, index, a + 1, b),
            send_to(source.at[:, start, cols], from_down.at[:, :, cols], sems, index + 1, a - 1, b),
        )

    right_top, left_top = across(start, 0)
    right_end, left_end = across(end, 1)
    right_mid, left_mid = across(middle, 2)
    down_1, up_1 = along(grad, middle, 6)
    down_0, up_0 = along(gv, start, 8)
    down_2, up_2 = along(gv, end, 10)
    keep_top = send_to(ev.at[:, start, start], extended_out.at[:, start, end], sems, 12, a, b - 1)
    keep_end = send_to(ev.at[:, end, start], extended_out.at[:, end, end], sems, 13, a, b - 1)

    load_grad = pltpu.make_async_copy(grad, gv, local.at[0])
    load_extended = pltpu.make_async_copy(extended, ev, local.at[1])

    outer = (right_top, right_end, left_top, left_end)
    total.start()
    right_top.start()
    left_top.start()
    pl.when(has_down)(down_1.start)
    pl.when(has_up)(up_1.start)
    load_grad.start()
    load_extended.start()
    total.scatter_y()
    right_end.start()
    left_end.start()
    right_mid.start_relayed()
    left_mid.start_relayed()
    right_top.pass_on()
    left_top.pass_on()
    total.scatter_z()
    right_end.pass_on()
    left_end.pass_on()
    total.across_x()
    late = boundary.at_low | boundary.at_high

    @pl.when(late)
    def _():
        total.gather_z()
        total.gather_y()

    load_grad.wait()
    right_top.wait_recv()
    right_end.wait_recv()

    @pl.when(has_left)
    def _():
        gv[:, start, start] += from_left[:, start, :]
        gv[:, end, start] += from_left[:, end, :]

    pl.when(has_down)(down_0.start)
    pl.when(has_up)(up_0.start)
    left_top.wait_recv()
    left_end.wait_recv()

    @pl.when(has_right)
    def _():
        gv[:, start, end] += from_right[:, start, :]
        gv[:, end, end] += from_right[:, end, :]

    pl.when(has_down & odd)(down_2.start)
    pl.when(has_up & odd)(up_2.start)

    @pl.when(~late)
    def _():
        total.gather_z()
        total.gather_y()

    for strip in outer:
        strip.wait_send()
    right_mid.start_direct()
    left_mid.start_direct()
    right_mid.pass_on()
    left_mid.pass_on()
    load_extended.wait()
    right_mid.wait_recv()
    left_mid.wait_recv()

    @pl.when(has_left)
    def _():
        gv[:, middle, start] += from_left[:, middle, :]

    @pl.when(has_right)
    def _():
        gv[:, middle, end] += from_right[:, middle, :]

    ev[:, middle, :] -= OBJECT_STEP * gv[:, middle, :]
    store_mid = pltpu.make_async_copy(ev.at[:, middle, :], extended_out.at[:, middle, :], local.at[0])
    store_mid.start()
    total.share()

    def update(rows, cols, received, exists):
        @pl.when(exists)
        def _():
            ev[:, rows, cols] -= OBJECT_STEP * (gv[:, rows, cols] + received[:, :, cols])

        @pl.when(jnp.logical_not(exists))
        def _():
            ev[:, rows, cols] -= OBJECT_STEP * gv[:, rows, cols]

    pl.when(has_up)(down_0.wait_recv)
    pl.when(has_down)(up_0.wait_recv)
    update(start, start, from_up, has_up)
    update(end, start, from_down, has_down)

    @pl.when(odd)
    def _():
        keep_top.start()
        keep_end.start()

    pl.when(has_up)(down_1.wait_recv)
    pl.when(has_down)(up_1.wait_recv)
    update(start, middle, from_up, has_up)
    update(end, middle, from_down, has_down)
    inner = pl.ds(0, tile)
    store_top = pltpu.make_async_copy(ev.at[:, start, inner], extended_out.at[:, start, inner], local.at[1])
    store_end = pltpu.make_async_copy(ev.at[:, end, inner], extended_out.at[:, end, inner], local.at[2])
    store_top.start()
    store_end.start()

    @pl.when(odd)
    def _():
        pl.when(has_up)(down_2.wait_recv)
        pl.when(has_down)(up_2.wait_recv)
        update(start, end, from_up, has_up)
        update(end, end, from_down, has_down)
        rim_top = pltpu.make_async_copy(ev.at[:, start, end], extended_out.at[:, start, end], local.at[3])
        rim_end = pltpu.make_async_copy(ev.at[:, end, end], extended_out.at[:, end, end], local.at[4])
        rim_top.start()
        rim_end.start()
        rim_top.wait()
        rim_end.wait()
        keep_top.wait_send()
        keep_end.wait_send()

    total.finish(probe, probe_out)
    right_mid.wait_send()
    left_mid.wait_send()
    for strip in outer + (right_mid, left_mid):
        strip.passed()

    @pl.when(has_down)
    def _():
        down_0.wait_send()
        down_1.wait_send()
        pl.when(odd)(down_2.wait_send)

    @pl.when(has_up)
    def _():
        up_0.wait_send()
        up_1.wait_send()
        pl.when(odd)(up_2.wait_send)

    store_mid.wait()
    store_top.wait()
    store_end.wait()

    @pl.when(jnp.logical_not(odd))
    def _():
        keep_top.wait_recv()
        keep_end.wait_recv()


def exchange(grad, extended, illumination, probe_grad):
    window = illumination.shape[1]
    side = grad.shape[1]
    vmem = pl.BlockSpec(memory_space=pltpu.VMEM)
    hbm = pl.BlockSpec(memory_space=pl.ANY)
    return pl.pallas_call(
        exchange_kernel,
        out_shape=(
            jax.ShapeDtypeStruct(extended.shape, jnp.float32),
            jax.ShapeDtypeStruct(illumination.shape, jnp.float32),
        ),
        in_specs=[hbm, hbm, vmem, vmem],
        out_specs=(hbm, vmem),
        scratch_shapes=[
            pltpu.VMEM((2, side, side), jnp.float32),
            pltpu.VMEM((2, side, side), jnp.float32),
            pltpu.VMEM((2, side, window), jnp.float32),
            pltpu.VMEM((2, side, window), jnp.float32),
            pltpu.VMEM((2, window, side), jnp.float32),
            pltpu.VMEM((2, window, side), jnp.float32),
            pltpu.SemaphoreType.DMA((14,)),
            pltpu.SemaphoreType.DMA((14,)),
            pltpu.SemaphoreType.DMA((5,)),
        ] + ProbeSum.scratch(window, lax.axis_size("ty"), lax.axis_size("tx")) + Boundary.scratch(window),
        compiler_params=pltpu.CompilerParams(
            collective_id=1, has_side_effects=True, vmem_limit_bytes=VMEM_LIMIT),
        name="exchange",
    )(grad, extended, illumination, probe_grad)


def fold_kernel(
    grad, extended, probe, probe_grad, specimen_out, probe_out,
    gv, ev, corner, from_left, from_up, send, recv, local,
    *rest,
):
    a, b, n_ty, n_tx = place_of()
    window = probe.shape[1]
    side = gv.shape[1]
    tile = side - window
    has_up, has_down, has_left, has_right = a > 0, a < n_ty - 1, b > 0, b < n_tx - 1
    total = ProbeSum(probe_grad, rest[:9], *rest[9:11])
    boundary = Boundary(rest[11], rest[12:])
    greet(total.partners() + [far_neighbour(a, b, n_tx)] + boundary.partners(False))
    sems = (send, recv)
    start, middle, end = pl.ds(0, window), pl.ds(window, tile - window), pl.ds(tile, window)
    inner = pl.ds(0, tile)

    def across(rows, index):
        return Sideways(boundary, 0, index, grad.at[:, rows, end], from_left.at[:, rows, :], sems, index)

    right_end = across(end, 0)
    right_top = across(start, 1)
    right_mid = across(middle, 2)
    down_1 = send_to(grad.at[:, end, middle], from_up.at[:, :, middle], sems, 3, a + 1, b)
    down_0 = send_to(corner, from_up.at[:, :, start], sems, 4, a + 1, b)
    load_grad = pltpu.make_async_copy(grad.at[:, :, inner], gv, local.at[0])
    load_extended = pltpu.make_async_copy(extended.at[:, inner, inner], ev, local.at[1])
    total.start()
    right_end.start()
    right_top.start_relayed()
    right_mid.start_relayed()
    pl.when(has_down)(down_1.start)
    load_grad.start()
    load_extended.start()
    total.scatter_y()
    right_top.start_direct()
    right_end.pass_on()
    total.scatter_z()
    right_top.pass_on()
    load_grad.wait()

    @pl.when(boundary.at_high)
    def _():
        total.across_x()
        total.gather_z()
        total.gather_y()

    right_end.wait_recv()

    @pl.when(has_left)
    def _():
        corner[...] = gv[:, end, start] + from_left[:, end, :]

    @pl.when(jnp.logical_not(has_left))
    def _():
        corner[...] = gv[:, end, start]

    @pl.when(~boundary.at_high)
    def _():
        total.across_x()

    pl.when(has_down)(down_0.start)

    @pl.when(~boundary.at_high)
    def _():
        total.gather_z()
        total.gather_y()

    right_end.wait_send()
    right_mid.start_direct()
    right_mid.pass_on()
    load_extended.wait()
    ev[...] -= OBJECT_STEP * gv[:, inner, :]
    total.share()
    right_top.wait_recv()
    right_mid.wait_recv()

    @pl.when(has_left)
    def _():
        ev[:, :, start] -= OBJECT_STEP * from_left[:, inner, :]

    @pl.when(has_up)
    def _():
        down_1.wait_recv()
        down_0.wait_recv()
        ev[:, start, :] -= OBJECT_STEP * from_up[...]

    specimen_out[...] = ev[...]
    total.finish(probe, probe_out)
    right_top.wait_send()
    right_mid.wait_send()
    for strip in (right_end, right_top, right_mid):
        strip.passed()

    @pl.when(has_down)
    def _():
        down_1.wait_send()
        down_0.wait_send()


def fold(grad, extended, illumination, probe_grad):
    window = illumination.shape[1]
    side = grad.shape[1]
    tile = side - window
    vmem = pl.BlockSpec(memory_space=pltpu.VMEM)
    hbm = pl.BlockSpec(memory_space=pl.ANY)
    return pl.pallas_call(
        fold_kernel,
        out_shape=(
            jax.ShapeDtypeStruct((2, tile, tile), jnp.float32),
            jax.ShapeDtypeStruct(illumination.shape, jnp.float32),
        ),
        in_specs=[hbm, hbm, vmem, vmem],
        out_specs=(vmem, vmem),
        scratch_shapes=[
            pltpu.VMEM((2, side, tile), jnp.float32),
            pltpu.VMEM((2, tile, tile), jnp.float32),
            pltpu.VMEM((2, window, window), jnp.float32),
            pltpu.VMEM((2, side, window), jnp.float32),
            pltpu.VMEM((2, window, tile), jnp.float32),
            pltpu.SemaphoreType.DMA((5,)),
            pltpu.SemaphoreType.DMA((5,)),
            pltpu.SemaphoreType.DMA((2,)),
        ] + ProbeSum.scratch(window, lax.axis_size("ty"), lax.axis_size("tx")) + Boundary.scratch(window),
        compiler_params=pltpu.CompilerParams(
            collective_id=2, has_side_effects=True, vmem_limit_bytes=VMEM_LIMIT),
        name="fold",
    )(grad, extended, illumination, probe_grad)


def body(specimen, illumination, patterns, scan_offsets, counts):
    window = illumination.shape[1]
    tile = specimen.shape[1]
    row_anchor = lax.axis_index("ty") * tile
    col_anchor = lax.axis_index("tx") * tile
    offsets = scan_offsets[0] - jnp.stack([row_anchor, col_anchor])[None, :].astype(jnp.int32)
    count = counts.reshape(1)
    dft = tables(window)
    extended, measured = fetch(specimen, patterns)
    for iteration in range(ITERS):
        grad, probe_grad = slot_gradients(count, offsets, extended, illumination, measured, dft)
        if iteration < ITERS - 1:
            extended, illumination = exchange(grad, extended, illumination, probe_grad)
        else:
            specimen, illumination = fold(grad, extended, illumination, probe_grad)
    return (specimen, illumination)


def solution(mesh):
    placed = (
        P(None, "ty", "tx"),
        P(),
        P("ty", "tx", None, None),
        P("ty", "tx", None),
        P("ty", "tx"),
    )
    return jax.shard_map(
        body, mesh=mesh, in_specs=placed, out_specs=(P(None, "ty", "tx"), P()), check_vma=False
    )
```

```python
import functools

import jax
import jax.numpy as jnp
import ml_dtypes
import numpy as np
from jax import lax
from jax.experimental import pallas as pl
from jax.experimental.pallas import tpu as pltpu
from jax.sharding import PartitionSpec as P

POS_DEV = 3
ITERS = 2
OBJECT_STEP = 0.05
PROBE_GAIN = 0.5
MESH = pl.DeviceIdType.MESH
VMEM_LIMIT = 36 * 1024 * 1024
SUBLANES = 8
TOGETHER = 3


def real_table(window):
    half = window // 2
    k = np.arange(window)
    freq = np.where(k <= half, k, k - half)
    angles = 2.0 * np.pi * ((freq[:, None] * k[None, :]) % window) / window
    table = np.where((k <= half)[:, None], np.cos(angles), np.sin(angles))
    return table / np.sqrt(window)


def split_table(table):
    high = table.astype(ml_dtypes.bfloat16)
    low = (table - high.astype(np.float64)).astype(ml_dtypes.bfloat16)
    return high, low


def tables(window):
    high, low = split_table(real_table(window))
    return [jnp.asarray(t) for t in (high, low, high.T, low.T)]


def split(value):
    high = value.astype(jnp.bfloat16)
    low = (value - high.astype(jnp.float32)).astype(jnp.bfloat16)
    return high, low


def dot(left, right):
    return jnp.dot(left, right, preferred_element_type=jnp.float32)


def left_product(table, value):
    high, low = split(value)
    return dot(table[0][...], high) + dot(table[1][...], high) + dot(table[0][...], low)


def right_product(value, table):
    high, low = split(value)
    return dot(high, table[0][...]) + dot(high, table[1][...]) + dot(low, table[0][...])


def compute_kernel(
    count_ref, offsets_ref, specimen_ref, probe_ref, measured_ref,
    high_ref, low_ref, high_t_ref, low_t_ref,
    grad_ref, probe_grad_ref,
    windows, levels, window_sems, level_sems,
):
    table, table_t = (high_ref, low_ref), (high_t_ref, low_t_ref)
    window = probe_ref.shape[1]
    half = window // 2
    lanes = 128
    blocks = window // lanes
    lane = lax.broadcasted_iota(jnp.int32, (window + SUBLANES, lanes), 1)
    sublane = lax.broadcasted_iota(jnp.int32, (window // SUBLANES, SUBLANES, lanes), 1)
    sublane_ext = lax.broadcasted_iota(jnp.int32, (window // SUBLANES + 1, SUBLANES, lanes), 1)
    first_row = lax.broadcasted_iota(jnp.int32, (half, window), 0) == 0
    first_col = lax.broadcasted_iota(jnp.int32, (window, half), 1) == 0

    probe_real, probe_imag = probe_ref[0], probe_ref[1]

    def position(slot):
        row = offsets_ref[slot, 0]
        col = offsets_ref[slot, 1]
        row_block = pl.multiple_of((row // SUBLANES) * SUBLANES, SUBLANES)
        col_block = pl.multiple_of((col // lanes) * lanes, lanes)
        return row_block, col_block, row - row_block, col - col_block

    def place(where, part, j):
        return (
            part,
            pl.ds(where[0], window + SUBLANES),
            pl.ds(pl.multiple_of(where[1] + lanes * j, lanes), lanes),
        )

    def loads(slot):
        row_block, col_block, _, _ = position(slot)
        rows, cols = pl.ds(row_block, window + SUBLANES), pl.ds(col_block, window + lanes)
        return (
            pltpu.make_async_copy(specimen_ref.at[:, rows, cols], windows.at[slot], window_sems.at[slot]),
            pltpu.make_async_copy(measured_ref.at[slot], levels.at[slot], level_sems.at[slot]),
        )

    def cut(slot, where, part):
        row_rest, col_rest = where[2:]
        keep = lane < lanes - col_rest
        pieces = [
            pltpu.roll(
                windows[slot, part, :, lanes * j:lanes * (j + 1)], lax.rem(lanes - col_rest, lanes), 1)
            for j in range(blocks + 1)
        ]
        columns = []
        for j in range(blocks):
            taken = jnp.where(keep, pieces[j], pieces[j + 1])
            taken = taken.reshape(window // SUBLANES + 1, SUBLANES, lanes)
            taken = pltpu.roll(taken, lax.rem(SUBLANES - row_rest, SUBLANES), 1)
            upper = sublane < SUBLANES - row_rest
            columns.append(jnp.where(upper, taken[:-1], taken[1:]).reshape(window, lanes))
        return jnp.concatenate(columns, axis=1)

    def add_term(where, part, term):
        row_rest, col_rest = where[2:]
        before = lane < col_rest
        above = sublane_ext < row_rest
        turned = []
        for j in range(blocks):
            piece = term[:, lanes * j:lanes * (j + 1)]
            piece = piece.reshape(window // SUBLANES, SUBLANES, lanes)
            piece = pltpu.roll(piece, row_rest, 1)
            edge = jnp.zeros((1, SUBLANES, lanes), jnp.float32)
            piece = jnp.where(
                above,
                jnp.concatenate([edge, piece], axis=0),
                jnp.concatenate([piece, edge], axis=0),
            ).reshape(window + SUBLANES, lanes)
            turned.append(pltpu.roll(piece, col_rest, 1))
        for j in range(blocks + 1):
            if j == 0:
                add = jnp.where(before, 0.0, turned[0])
            elif j == blocks:
                add = jnp.where(before, turned[-1], 0.0)
            else:
                add = jnp.where(before, turned[j - 1], turned[j])
            grad_ref[place(where, part, j)] += add

    def exit_wave(patch):
        real, imag = patch
        psi_real = probe_real * real - probe_imag * imag
        psi_imag = probe_real * imag + probe_imag * real
        return jnp.concatenate([psi_real, psi_imag], axis=1)

    def unfold_rows(both):
        u_top, v_top = both[:half, :window], both[:half, window:]
        u_bot, v_bot = both[half:, :window], both[half:, window:]
        u_add = jnp.where(first_row, 0.0, u_bot)
        v_add = jnp.where(first_row, 0.0, v_bot)
        return jnp.concatenate([
            u_top + v_add, jnp.where(first_row, u_bot, u_top - v_bot),
            v_top - u_add, jnp.where(first_row, v_bot, v_top + u_bot)], axis=0)

    def unfold_cols(both):
        u_top, v_top = both[:window, :half], both[window:, :half]
        u_bot, v_bot = both[:window, half:], both[window:, half:]
        u_add = jnp.where(first_col, 0.0, u_bot)
        v_add = jnp.where(first_col, 0.0, v_bot)
        far_real = jnp.concatenate([u_top + v_add, jnp.where(first_col, u_bot, u_top - v_bot)], axis=1)
        far_imag = jnp.concatenate([v_top - u_add, jnp.where(first_col, v_bot, v_top + u_bot)], axis=1)
        return far_real, far_imag

    def fold_rows(g_real, g_imag):
        r_top, r_bot = g_real[:half], g_real[half:]
        i_top, i_bot = g_imag[:half], g_imag[half:]
        z_real = jnp.concatenate(
            [r_top + jnp.where(first_row, 0.0, r_bot), jnp.where(first_row, r_bot, i_bot - i_top)], axis=0)
        z_imag = jnp.concatenate(
            [i_top + jnp.where(first_row, 0.0, i_bot), jnp.where(first_row, i_bot, r_top - r_bot)], axis=0)
        return jnp.concatenate([z_real, z_imag], axis=1)

    def fold_cols(both):
        r_top, r_bot = both[:, :half], both[:, half:window]
        i_top, i_bot = both[:, window:window + half], both[:, window + half:]
        z_real = jnp.concatenate(
            [r_top + jnp.where(first_col, 0.0, r_bot), jnp.where(first_col, r_bot, i_bot - i_top)], axis=1)
        z_imag = jnp.concatenate(
            [i_top + jnp.where(first_col, 0.0, i_bot), jnp.where(first_col, i_bot, r_top - r_bot)], axis=1)
        return jnp.concatenate([z_real, z_imag], axis=0)

    def visit(step, carry):
        slots = [TOGETHER * step + i for i in range(TOGETHER)]
        where = [position(slot) for slot in slots]
        live = [(slot < count_ref[0]).astype(jnp.float32) for slot in slots]
        for slot in slots:
            for copy in loads(slot):
                copy.wait()
        patches = [(cut(slot, w, 0), cut(slot, w, 1)) for slot, w in zip(slots, where)]
        waves = [left_product(table, exit_wave(patch)) for patch in patches]
        waves = [right_product(unfold_rows(wave), table_t) for wave in waves]
        sources = []
        for wave, slot, on in zip(waves, slots, live):
            far_real, far_imag = unfold_cols(wave)
            factor = on * (far_real * far_real + far_imag * far_imag - levels[slot])
            sources.append(fold_rows(factor * far_real, factor * far_imag))
        waves = [left_product(table_t, source) for source in sources]
        waves = [right_product(fold_cols(wave), table) for wave in waves]
        for wave, patch, w in zip(waves, patches, where):
            chi_real, chi_imag = wave[:window], wave[window:]
            probe_grad_ref[0] += patch[0] * chi_real + patch[1] * chi_imag
            probe_grad_ref[1] += patch[0] * chi_imag - patch[1] * chi_real
            add_term(w, 0, probe_real * chi_real + probe_imag * chi_imag)
            add_term(w, 1, probe_real * chi_imag - probe_imag * chi_real)
        return carry

    steps = (count_ref[0] + TOGETHER - 1) // TOGETHER

    def fetch_slot(slot, carry):
        for copy in loads(slot):
            copy.start()
        return carry

    lax.fori_loop(0, steps * TOGETHER, fetch_slot, 0)
    grad_ref[...] = jnp.zeros_like(grad_ref)
    probe_grad_ref[...] = jnp.zeros_like(probe_grad_ref)
    lax.fori_loop(0, steps, visit, 0)


def slot_gradients(count, offsets, extended, illumination, measured, dft):
    smem = pl.BlockSpec(memory_space=pltpu.SMEM)
    vmem = pl.BlockSpec(memory_space=pltpu.VMEM)
    hbm = pl.BlockSpec(memory_space=pl.ANY)
    slots, window, _ = measured.shape
    return pl.pallas_call(
        compute_kernel,
        out_shape=(
            jax.ShapeDtypeStruct(extended.shape, jnp.float32),
            jax.ShapeDtypeStruct(illumination.shape, jnp.float32),
        ),
        in_specs=[smem, smem, hbm, vmem, hbm] + [vmem] * 4,
        out_specs=(vmem, vmem),
        scratch_shapes=[
            pltpu.VMEM((slots, 2, window + SUBLANES, window + 128), jnp.float32),
            pltpu.VMEM(measured.shape, jnp.float32),
            pltpu.SemaphoreType.DMA((slots,)),
            pltpu.SemaphoreType.DMA((slots,)),
        ],
        compiler_params=pltpu.CompilerParams(vmem_limit_bytes=VMEM_LIMIT),
        name="slot_gradients",
    )(count, offsets, extended, illumination, measured, *dft)


def place_of():
    return lax.axis_index("ty"), lax.axis_index("tx"), lax.axis_size("ty"), lax.axis_size("tx")


def send_to(source, target, sems, index, row, col):
    send_sem, recv_sem = sems
    return pltpu.make_async_remote_copy(
        src_ref=source,
        dst_ref=target,
        send_sem=send_sem.at[index],
        recv_sem=recv_sem.at[index],
        device_id=(row, col),
        device_id_type=MESH,
    )


def wait_bytes(ref, sem):
    pltpu.make_async_copy(ref, ref, sem).wait()


def greet(partners):
    barrier = pltpu.get_barrier_semaphore()
    for exists, row, col in partners:
        @pl.when(exists)
        def _():
            pl.semaphore_signal(barrier, inc=1, device_id=(row, col), device_id_type=MESH)
    pl.semaphore_wait(barrier, sum(jnp.int32(exists) for exists, _, _ in partners))


class Boundary:
    LINES = 4

    def __init__(self, relay, sems):
        self.relay = relay
        self.first_send, self.hop_recv, self.hop_send, self.last_recv = sems
        self.a, self.b, _, n = place_of()
        self.n = n
        half = n // 2
        self.low, self.high = half - 1, half
        if n >= 16:
            inner = ((half, half + 3, 3, half - 1), (half, n - 4, half - 4, half - 1))
        else:
            inner = ((half, half + 2, 2, half - 1), (half, n - 3, half - 3, half - 1))
        self.paths = ((half, 0, half - 1), *inner, (half, n - 1, half - 1))
        self.at_low, self.at_high = self.b == self.low, self.b == self.high

    @staticmethod
    def scratch(window):
        return [
            pltpu.VMEM((2, 3, window // 2, window), jnp.float32),
            pltpu.SemaphoreType.DMA((2, 3, Boundary.LINES)),
            pltpu.SemaphoreType.DMA((2, 3)),
            pltpu.SemaphoreType.DMA((2, 3)),
            pltpu.SemaphoreType.DMA((2, 3, Boundary.LINES)),
        ]

    def partners(self, every):
        pairs = sorted({tuple(sorted(pair)) for path in self.paths for pair in zip(path, path[1:])})
        found = []
        for p, q in pairs:
            if p // 2 != q // 2 and (every or p % 2 != q % 2):
                found += [(self.b == p, self.a, q), (self.b == q, self.a, p)]
        return found

    def before_z(self, way):
        n_x, n_y, _ = ProbeSum.sizes(lax.axis_size("ty"), self.n)
        high = 2 * n_y
        nodes = sorted({p for line in range(self.LINES)
                        for p, q in zip(self.path(way, line), self.path(way, line)[1:]) if (p >= high) != (q >= high)})
        found = self.b == nodes[0]
        for node in nodes[1:]:
            found = found | (self.b == node)
        return found

    def path(self, way, line):
        return self.paths[line] if way == 1 else self.paths[line][::-1]

    def origin(self, way):
        return self.low if way == 0 else self.high

    @staticmethod
    def quarter(ref, line):
        rows = ref.shape[1] // 2
        return ref.at[line // 2, pl.ds(line % 2 * rows, rows), :]

    def leg(self, way, index, line, k, source, target):
        path = self.path(way, line)
        last = k == len(path) - 2
        return pltpu.make_async_remote_copy(
            src_ref=self.quarter(source, line) if k == 0 else self.relay.at[way, index],
            dst_ref=self.quarter(target, line) if last else self.relay.at[way, index],
            send_sem=self.first_send.at[way, index, line] if k == 0 else self.hop_send.at[way, index],
            recv_sem=self.last_recv.at[way, index, line] if last else self.hop_recv.at[way, index],
            device_id=(self.a, path[k + 1]),
            device_id_type=MESH,
        )

    def start(self, way, index, source, target):
        for line in range(self.LINES):
            self.leg(way, index, line, 0, source, target).start()

    def relays(self, way):
        return [(line, k, node) for line in range(self.LINES)
                for k, node in enumerate(self.path(way, line)) if 0 < k < len(self.path(way, line)) - 1]

    def pass_on(self, way, index, source, target):
        for line, k, node in self.relays(way):
            @pl.when(self.b == node)
            def _():
                self.leg(way, index, line, k - 1, source, target).wait_recv()
                self.leg(way, index, line, k, source, target).start()

    def passed(self, way, index, source, target):
        for line, k, node in self.relays(way):
            @pl.when(self.b == node)
            def _():
                self.leg(way, index, line, k, source, target).wait_send()

    def wait_recv(self, way, index, source, target):
        for line in range(self.LINES):
            self.leg(way, index, line, len(self.path(way, line)) - 2, source, target).wait_recv()

    def wait_send(self, way, index, source, target):
        for line in range(self.LINES):
            self.leg(way, index, line, 0, source, target).wait_send()


class Sideways:
    def __init__(self, boundary, way, index, source, target, sems, slot):
        a, b, _, n_tx = place_of()
        self.boundary = boundary
        self.strip = (way, index, source, target)
        step = 1 if way == 0 else -1
        self.direct = send_to(source, target, sems, slot, a, b + step)
        left, right = b > 0, b < n_tx - 1
        self.has_target, self.has_source = (right, left) if way == 0 else (left, right)
        self.from_origin = b == boundary.origin(way)
        self.at_end = b == boundary.origin(1 - way)

    def start(self):
        self.start_relayed()
        self.start_direct()

    def start_relayed(self):
        pl.when(self.from_origin)(lambda: self.boundary.start(*self.strip))

    def start_direct(self):
        pl.when(self.has_target & ~self.from_origin)(self.direct.start)

    def pass_on(self):
        self.boundary.pass_on(*self.strip)

    def wait_recv(self):
        pl.when(self.at_end)(lambda: self.boundary.wait_recv(*self.strip))
        pl.when(self.has_source & ~self.at_end)(self.direct.wait_recv)

    def wait_send(self):
        pl.when(self.from_origin)(lambda: self.boundary.wait_send(*self.strip))
        pl.when(self.has_target & ~self.from_origin)(self.direct.wait_send)

    def passed(self):
        self.boundary.passed(*self.strip)


def fetch_kernel(
    specimen, patterns, extended, measured_out,
    measured, staged, send, recv, local, *rest,
):
    a, b, n_ty, n_tx = place_of()
    window = measured.shape[1]
    tile = specimen.shape[1]
    half = window // 2
    up, down, left, right = a > 0, a < n_ty - 1, b > 0, b < n_tx - 1
    boundary = Boundary(rest[0], rest[1:])
    near = (True, a, b + 1 - 2 * lax.rem(b, 2))
    greet([(up, a - 1, b), (down, a + 1, b), near, far_neighbour(a, b, n_tx)] + boundary.partners(True))
    sems = (send, recv)
    first, second = pl.ds(0, window), pl.ds(window, tile - window)
    beyond, inside = pl.ds(tile, window), pl.ds(0, tile)

    def aside(index, source, rows):
        return Sideways(
            boundary, 1, index, source.at[:, rows, first], extended.at[:, rows, beyond], sems, 2 + index)

    up_a = send_to(specimen.at[:, first, first], extended.at[:, beyond, first], sems, 0, a - 1, b)
    up_b = send_to(specimen.at[:, first, second], extended.at[:, beyond, second], sems, 1, a - 1, b)
    aside_a = aside(0, specimen, first)
    aside_b = aside(1, specimen, second)
    corner = send_to(
        extended.at[:, beyond, first], extended.at[:, beyond, beyond], sems, 4, a, b - 1)
    corner_up = send_to(
        extended.at[:, first, beyond], extended.at[:, beyond, beyond], sems, 5, a - 1, b)
    corner_left = down & left & ~boundary.at_high
    stage = pltpu.make_async_copy(specimen, staged, local.at[0])
    keep = pltpu.make_async_copy(staged, extended.at[:, inside, inside], local.at[2])
    load = pltpu.make_async_copy(patterns.at[0], measured, local.at[1])
    hold = (lax.rem(a, ProbeSum.sizes(n_ty, n_tx)[0]) == 0) & up & boundary.before_z(1)
    pl.when(up & ~hold)(up_a.start)
    aside_a.start()
    aside_b.start()
    load.start()
    stage.start()
    stage.wait()
    keep.start()

    @pl.when(hold)
    def _():
        aside_a.pass_on()
        aside_b.pass_on()
        up_a.start()

    pl.when(~hold)(aside_a.pass_on)

    @pl.when(up)
    def _():
        up_a.wait_send()
        up_b.start()

    pl.when(~hold)(aside_b.pass_on)
    pl.when(down)(up_a.wait_recv)
    pl.when(corner_left)(corner.start)

    @pl.when(boundary.at_low)
    def _():
        aside_a.wait_recv()
        pl.when(up)(corner_up.start)

    load.wait()
    row = lax.broadcasted_iota(jnp.int32, (window, window), 0)
    col = lax.broadcasted_iota(jnp.int32, (window, window), 1)

    def order(place, freq):
        picked = jnp.where(place <= half, place, window + half - place) == freq
        return picked.astype(jnp.float32).astype(jnp.bfloat16)

    reorder = jnp.concatenate([order(row, col)] * 3, axis=1)
    reorder_back = jnp.concatenate([order(col, row)] * 3, axis=0)

    def rearrange(slot, carry):
        def pieces(value):
            high, low = split(value)
            rest = (value - high.astype(jnp.float32) - low.astype(jnp.float32)).astype(jnp.bfloat16)
            return [high, low, rest]

        rows = jnp.dot(
            reorder, jnp.concatenate(pieces(measured[slot]), axis=0), preferred_element_type=jnp.float32)
        measured_out[slot] = jnp.dot(
            jnp.concatenate(pieces(rows), axis=1), reorder_back, preferred_element_type=jnp.float32)
        return carry

    lax.fori_loop(0, measured.shape[0], rearrange, 0)
    keep.wait()
    pl.when(~boundary.at_low)(aside_a.wait_recv)
    aside_b.wait_recv()
    pl.when(up)(up_b.wait_send)
    pl.when(down)(up_b.wait_recv)
    pl.when(corner_left)(corner.wait_send)
    pl.when(down & right & ~boundary.at_low)(corner.wait_recv)

    @pl.when(boundary.at_low)
    def _():
        pl.when(up)(corner_up.wait_send)
        pl.when(down)(corner_up.wait_recv)

    for strip in (aside_a, aside_b):
        strip.wait_send()
        strip.passed()


def fetch(specimen, patterns):
    window = patterns.shape[2]
    side = specimen.shape[1] + window
    vmem = pl.BlockSpec(memory_space=pltpu.VMEM)
    hbm = pl.BlockSpec(memory_space=pl.ANY)
    return pl.pallas_call(
        fetch_kernel,
        out_shape=(
            jax.ShapeDtypeStruct((2, side, side), jnp.float32),
            jax.ShapeDtypeStruct(patterns.shape[1:], jnp.float32),
        ),
        in_specs=[hbm, hbm],
        out_specs=(hbm, vmem),
        scratch_shapes=[
            pltpu.VMEM(patterns.shape[1:], jnp.float32),
            pltpu.VMEM(specimen.shape, jnp.float32),
            pltpu.SemaphoreType.DMA((6,)),
            pltpu.SemaphoreType.DMA((6,)),
            pltpu.SemaphoreType.DMA((3,)),
        ] + Boundary.scratch(window),
        compiler_params=pltpu.CompilerParams(
            collective_id=0, has_side_effects=True, vmem_limit_bytes=VMEM_LIMIT + 26 * 1024 * 1024),
        name="fetch",
    )(specimen, patterns)


class ProbeSum:
    STAGES = 7

    def __init__(self, terms, buffers, send, recv):
        self.terms = terms
        self.mate, self.mine, self.y_in, self.y_sum, self.z_in, self.x_in, self.z_out, self.full, self.other = buffers
        self.send, self.recv = send, recv
        self.a, self.b, n_ty, n_tx = place_of()
        self.n_x, self.n_y, self.n_z = self.sizes(n_ty, n_tx)
        self.n_low = self.n_z // 2
        self.devices = n_ty * n_tx
        self.core = lax.rem(self.b, 2)
        self.y = lax.rem(self.b // 2, self.n_y)
        self.x = lax.rem(self.a, self.n_x)
        self.z = self.b // (2 * self.n_y) * self.n_low + self.a // self.n_x
        self.mate_col = self.b + 1 - 2 * self.core
        self.y_rows = self.full.shape[0] // self.n_y
        self.z_rows = self.y_rows // self.n_z

    @staticmethod
    def sizes(n_ty, n_tx):
        n_x = 4 if n_ty == 16 else 2
        return n_x, n_tx // 4, 2 * (n_ty // n_x)

    @staticmethod
    def scratch(window, n_ty, n_tx):
        n_x, n_y, n_z = ProbeSum.sizes(n_ty, n_tx)
        y_rows = window // n_y
        z_rows = y_rows // n_z
        shapes = [
            (window, window), (window, window), (n_y - 1, y_rows, window), (y_rows, window),
            (n_z - 1, z_rows, window), (n_x, z_rows, window), (y_rows, window),
            (window, window), (window, window),
        ]
        return [pltpu.VMEM(shape, jnp.float32) for shape in shapes] + [
            pltpu.SemaphoreType.DMA((ProbeSum.STAGES,)),
            pltpu.SemaphoreType.DMA((ProbeSum.STAGES,)),
        ]

    def at_y(self, y):
        return self.a, (self.b // (2 * self.n_y)) * 2 * self.n_y + 2 * y + self.core

    def at_z(self, z):
        return lax.rem(z, self.n_low) * self.n_x + self.x, (z // self.n_low) * 2 * self.n_y + 2 * self.y + self.core

    def at_x(self, x):
        return self.a - self.x + x, self.b

    def partners(self):
        found = [(True, self.a, self.mate_col)]
        found += [(True, *self.at_y(lax.rem(self.y + d, self.n_y))) for d in range(1, self.n_y)]
        found += [(True, *self.at_z(lax.rem(self.z + d, self.n_z))) for d in range(1, self.n_z)]
        found += [(True, *self.at_x(lax.rem(self.x + d, self.n_x))) for d in range(1, self.n_x)]
        n_ty = self.n_low * self.n_x
        wraps_down = (self.x == self.n_x - 1) & (self.a < n_ty - 1)
        wraps_up = (self.x == 0) & (self.a > 0)
        found.append((wraps_down | wraps_up, jnp.where(wraps_up, self.a - 1, self.a + 1), self.b))
        return found

    def to(self, source, target, stage, row, col):
        return send_to(source, target, (self.send, self.recv), stage, row, col)

    @staticmethod
    def rows(ref, index, count):
        return ref.at[pl.ds(pl.multiple_of(index * count, SUBLANES), count), :]

    def each(self, count, go):
        def step(d, carry):
            go(d)
            return carry

        lax.fori_loop(1, count, step, 0)

    def start(self):
        self.to(self.terms.at[1 - self.core], self.mate, 0, self.a, self.mate_col).start()

    def scatter_y(self):
        self.to(self.terms.at[1 - self.core], self.mate, 0, self.a, self.mate_col).wait()
        self.mine[...] = self.terms[self.core] + self.mate[...]

        def go(d):
            y = lax.rem(self.y + d, self.n_y)
            self.to(self.rows(self.mine, y, self.y_rows), self.y_in.at[d - 1], 1, *self.at_y(y)).start()

        self.each(self.n_y, go)

    def scatter_z(self):
        wait_bytes(self.y_in, self.recv.at[1])
        total = self.rows(self.mine, self.y, self.y_rows)[...]
        for d in range(self.n_y - 1):
            total = total + self.y_in[d]
        self.y_sum[...] = total

        def go(d):
            z = lax.rem(self.z + d, self.n_z)
            self.to(self.rows(self.y_sum, z, self.z_rows), self.z_in.at[d - 1], 2, *self.at_z(z)).start()

        self.each(self.n_z, go)

    def across_x(self):
        wait_bytes(self.z_in, self.recv.at[2])
        total = self.rows(self.y_sum, self.z, self.z_rows)[...]
        for d in range(self.n_z - 1):
            total = total + self.z_in[d]
        self.x_in[self.x] = total

        def go(d):
            x = lax.rem(self.x + d, self.n_x)
            self.to(self.x_in.at[self.x], self.x_in.at[self.x], 3, *self.at_x(x)).start()

        self.each(self.n_x, go)

    def gather_z(self):
        wait_bytes(self.x_in.at[pl.ds(0, self.n_x - 1)], self.recv.at[3])
        total = self.x_in[0]
        for i in range(1, self.n_x):
            total = total + self.x_in[i]
        own = self.rows(self.z_out, self.z, self.z_rows)
        own[...] = total

        def go(d):
            z = lax.rem(self.z + d, self.n_z)
            self.to(own, own, 4, *self.at_z(z)).start()

        self.each(self.n_z, go)

    def gather_y(self):
        wait_bytes(self.z_out.at[pl.ds(0, (self.n_z - 1) * self.z_rows)], self.recv.at[4])
        own = self.rows(self.full, self.y, self.y_rows)
        own[...] = self.z_out[...]

        def go(d):
            y = lax.rem(self.y + d, self.n_y)
            self.to(self.z_out, own, 5, *self.at_y(y)).start()

        self.each(self.n_y, go)

    def share(self):
        wait_bytes(self.full.at[pl.ds(0, (self.n_y - 1) * self.y_rows)], self.recv.at[5])
        self.to(self.full, self.other, 6, self.a, self.mate_col).start()

    def finish(self, probe, probe_out):
        step = PROBE_GAIN / (POS_DEV * self.devices)
        probe_out[self.core] = probe[self.core] - step * self.full[...]
        self.to(self.full, self.other, 6, self.a, self.mate_col).wait()
        probe_out[1 - self.core] = probe[1 - self.core] - step * self.other[...]
        wait_bytes(self.y_in, self.send.at[1])
        wait_bytes(self.z_in, self.send.at[2])
        wait_bytes(self.x_in.at[pl.ds(0, self.n_x - 1)], self.send.at[3])
        wait_bytes(self.z_out.at[pl.ds(0, (self.n_z - 1) * self.z_rows)], self.send.at[4])
        wait_bytes(self.full.at[pl.ds(0, (self.n_y - 1) * self.y_rows)], self.send.at[5])


def far_neighbour(a, b, n_tx):
    core = lax.rem(b, 2)
    col = b - 1 + 2 * core
    return ((col >= 0) & (col < n_tx) & (b != n_tx // 2 - 1) & (b != n_tx // 2), a, col)


def exchange_kernel(
    grad, extended, probe, probe_grad, extended_out, probe_out,
    gv, ev, from_left, from_right, from_up, from_down, send, recv, local,
    *rest,
):
    a, b, n_ty, n_tx = place_of()
    window = probe.shape[1]
    side = gv.shape[1]
    tile = side - window
    core = lax.rem(b, 2)
    has_up, has_down, has_left, has_right = a > 0, a < n_ty - 1, b > 0, b < n_tx - 1
    odd = core == 1
    total = ProbeSum(probe_grad, rest[:9], *rest[9:11])
    boundary = Boundary(rest[11], rest[12:])
    greet(total.partners() + [far_neighbour(a, b, n_tx)] + boundary.partners(False))
    sems = (send, recv)
    start, middle, end = pl.ds(0, window), pl.ds(window, tile - window), pl.ds(tile, window)

    def across(rows, index):
        return (
            Sideways(boundary, 0, index, grad.at[:, rows, end], from_left.at[:, rows, :], sems, 2 * index),
            Sideways(boundary, 1, index, grad.at[:, rows, start], from_right.at[:, rows, :], sems, 2 * index + 1),
        )

    def along(source, cols, index):
        return (
            send_to(source.at[:, end, cols], from_up.at[:, :, cols], sems, index, a + 1, b),
            send_to(source.at[:, start, cols], from_down.at[:, :, cols], sems, index + 1, a - 1, b),
        )

    right_top, left_top = across(start, 0)
    right_end, left_end = across(end, 1)
    right_mid, left_mid = across(middle, 2)
    down_1, up_1 = along(grad, middle, 6)
    down_0, up_0 = along(gv, start, 8)
    down_2, up_2 = along(gv, end, 10)
    keep_top = send_to(ev.at[:, start, start], extended_out.at[:, start, end], sems, 12, a, b - 1)
    keep_end = send_to(ev.at[:, end, start], extended_out.at[:, end, end], sems, 13, a, b - 1)

    load_grad = pltpu.make_async_copy(grad, gv, local.at[0])
    load_extended = pltpu.make_async_copy(extended, ev, local.at[1])

    outer = (right_top, right_end, left_top, left_end)
    total.start()
    right_top.start()
    left_top.start()
    pl.when(has_down)(down_1.start)
    pl.when(has_up)(up_1.start)
    load_grad.start()
    load_extended.start()
    total.scatter_y()
    right_end.start()
    left_end.start()
    right_mid.start_relayed()
    left_mid.start_relayed()
    right_top.pass_on()
    left_top.pass_on()
    total.scatter_z()
    right_end.pass_on()
    left_end.pass_on()
    total.across_x()
    late = boundary.at_low | boundary.at_high

    @pl.when(late)
    def _():
        total.gather_z()
        total.gather_y()

    load_grad.wait()
    right_top.wait_recv()
    right_end.wait_recv()

    @pl.when(has_left)
    def _():
        gv[:, start, start] += from_left[:, start, :]
        gv[:, end, start] += from_left[:, end, :]

    pl.when(has_down)(down_0.start)
    pl.when(has_up)(up_0.start)
    left_top.wait_recv()
    left_end.wait_recv()

    @pl.when(has_right)
    def _():
        gv[:, start, end] += from_right[:, start, :]
        gv[:, end, end] += from_right[:, end, :]

    pl.when(has_down & odd)(down_2.start)
    pl.when(has_up & odd)(up_2.start)

    @pl.when(~late)
    def _():
        total.gather_z()
        total.gather_y()

    for strip in outer:
        strip.wait_send()
    right_mid.start_direct()
    left_mid.start_direct()
    right_mid.pass_on()
    left_mid.pass_on()
    load_extended.wait()
    right_mid.wait_recv()
    left_mid.wait_recv()

    @pl.when(has_left)
    def _():
        gv[:, middle, start] += from_left[:, middle, :]

    @pl.when(has_right)
    def _():
        gv[:, middle, end] += from_right[:, middle, :]

    ev[:, middle, :] -= OBJECT_STEP * gv[:, middle, :]
    store_mid = pltpu.make_async_copy(ev.at[:, middle, :], extended_out.at[:, middle, :], local.at[0])
    store_mid.start()
    total.share()

    def update(rows, cols, received, exists):
        @pl.when(exists)
        def _():
            ev[:, rows, cols] -= OBJECT_STEP * (gv[:, rows, cols] + received[:, :, cols])

        @pl.when(jnp.logical_not(exists))
        def _():
            ev[:, rows, cols] -= OBJECT_STEP * gv[:, rows, cols]

    pl.when(has_up)(down_0.wait_recv)
    pl.when(has_down)(up_0.wait_recv)
    update(start, start, from_up, has_up)
    update(end, start, from_down, has_down)

    @pl.when(odd)
    def _():
        keep_top.start()
        keep_end.start()

    pl.when(has_up)(down_1.wait_recv)
    pl.when(has_down)(up_1.wait_recv)
    update(start, middle, from_up, has_up)
    update(end, middle, from_down, has_down)
    inner = pl.ds(0, tile)
    store_top = pltpu.make_async_copy(ev.at[:, start, inner], extended_out.at[:, start, inner], local.at[1])
    store_end = pltpu.make_async_copy(ev.at[:, end, inner], extended_out.at[:, end, inner], local.at[2])
    store_top.start()
    store_end.start()

    @pl.when(odd)
    def _():
        pl.when(has_up)(down_2.wait_recv)
        pl.when(has_down)(up_2.wait_recv)
        update(start, end, from_up, has_up)
        update(end, end, from_down, has_down)
        rim_top = pltpu.make_async_copy(ev.at[:, start, end], extended_out.at[:, start, end], local.at[3])
        rim_end = pltpu.make_async_copy(ev.at[:, end, end], extended_out.at[:, end, end], local.at[4])
        rim_top.start()
        rim_end.start()
        rim_top.wait()
        rim_end.wait()
        keep_top.wait_send()
        keep_end.wait_send()

    total.finish(probe, probe_out)
    right_mid.wait_send()
    left_mid.wait_send()
    for strip in outer + (right_mid, left_mid):
        strip.passed()

    @pl.when(has_down)
    def _():
        down_0.wait_send()
        down_1.wait_send()
        pl.when(odd)(down_2.wait_send)

    @pl.when(has_up)
    def _():
        up_0.wait_send()
        up_1.wait_send()
        pl.when(odd)(up_2.wait_send)

    store_mid.wait()
    store_top.wait()
    store_end.wait()

    @pl.when(jnp.logical_not(odd))
    def _():
        keep_top.wait_recv()
        keep_end.wait_recv()


def exchange(grad, extended, illumination, probe_grad):
    window = illumination.shape[1]
    side = grad.shape[1]
    vmem = pl.BlockSpec(memory_space=pltpu.VMEM)
    hbm = pl.BlockSpec(memory_space=pl.ANY)
    return pl.pallas_call(
        exchange_kernel,
        out_shape=(
            jax.ShapeDtypeStruct(extended.shape, jnp.float32),
            jax.ShapeDtypeStruct(illumination.shape, jnp.float32),
        ),
        in_specs=[hbm, hbm, vmem, vmem],
        out_specs=(hbm, vmem),
        scratch_shapes=[
            pltpu.VMEM((2, side, side), jnp.float32),
            pltpu.VMEM((2, side, side), jnp.float32),
            pltpu.VMEM((2, side, window), jnp.float32),
            pltpu.VMEM((2, side, window), jnp.float32),
            pltpu.VMEM((2, window, side), jnp.float32),
            pltpu.VMEM((2, window, side), jnp.float32),
            pltpu.SemaphoreType.DMA((14,)),
            pltpu.SemaphoreType.DMA((14,)),
            pltpu.SemaphoreType.DMA((5,)),
        ] + ProbeSum.scratch(window, lax.axis_size("ty"), lax.axis_size("tx")) + Boundary.scratch(window),
        compiler_params=pltpu.CompilerParams(
            collective_id=1, has_side_effects=True, vmem_limit_bytes=VMEM_LIMIT),
        name="exchange",
    )(grad, extended, illumination, probe_grad)


def fold_kernel(
    grad, extended, probe, probe_grad, specimen_out, probe_out,
    gv, ev, corner, from_left, from_up, send, recv, local,
    *rest,
):
    a, b, n_ty, n_tx = place_of()
    window = probe.shape[1]
    side = gv.shape[1]
    tile = side - window
    has_up, has_down, has_left, has_right = a > 0, a < n_ty - 1, b > 0, b < n_tx - 1
    total = ProbeSum(probe_grad, rest[:9], *rest[9:11])
    boundary = Boundary(rest[11], rest[12:])
    greet(total.partners() + [far_neighbour(a, b, n_tx)] + boundary.partners(False))
    sems = (send, recv)
    start, middle, end = pl.ds(0, window), pl.ds(window, tile - window), pl.ds(tile, window)
    inner = pl.ds(0, tile)

    def across(rows, index):
        return Sideways(boundary, 0, index, grad.at[:, rows, end], from_left.at[:, rows, :], sems, index)

    right_end = across(end, 0)
    right_top = across(start, 1)
    right_mid = across(middle, 2)
    down_1 = send_to(grad.at[:, end, middle], from_up.at[:, :, middle], sems, 3, a + 1, b)
    down_0 = send_to(corner, from_up.at[:, :, start], sems, 4, a + 1, b)
    load_grad = pltpu.make_async_copy(grad.at[:, :, inner], gv, local.at[0])
    load_extended = pltpu.make_async_copy(extended.at[:, inner, inner], ev, local.at[1])
    total.start()
    right_end.start()
    right_top.start_relayed()
    right_mid.start_relayed()
    pl.when(has_down)(down_1.start)
    load_grad.start()
    load_extended.start()
    total.scatter_y()
    right_top.start_direct()
    right_end.pass_on()
    total.scatter_z()
    right_top.pass_on()
    load_grad.wait()

    @pl.when(boundary.at_high)
    def _():
        total.across_x()
        total.gather_z()
        total.gather_y()

    right_end.wait_recv()

    @pl.when(has_left)
    def _():
        corner[...] = gv[:, end, start] + from_left[:, end, :]

    @pl.when(jnp.logical_not(has_left))
    def _():
        corner[...] = gv[:, end, start]

    @pl.when(~boundary.at_high)
    def _():
        total.across_x()

    pl.when(has_down)(down_0.start)

    @pl.when(~boundary.at_high)
    def _():
        total.gather_z()
        total.gather_y()

    right_end.wait_send()
    right_mid.start_direct()
    right_mid.pass_on()
    load_extended.wait()
    ev[...] -= OBJECT_STEP * gv[:, inner, :]
    total.share()
    right_top.wait_recv()
    right_mid.wait_recv()

    @pl.when(has_left)
    def _():
        ev[:, :, start] -= OBJECT_STEP * from_left[:, inner, :]

    @pl.when(has_up)
    def _():
        down_1.wait_recv()
        down_0.wait_recv()
        ev[:, start, :] -= OBJECT_STEP * from_up[...]

    specimen_out[...] = ev[...]
    total.finish(probe, probe_out)
    right_top.wait_send()
    right_mid.wait_send()
    for strip in (right_end, right_top, right_mid):
        strip.passed()

    @pl.when(has_down)
    def _():
        down_1.wait_send()
        down_0.wait_send()


def fold(grad, extended, illumination, probe_grad):
    window = illumination.shape[1]
    side = grad.shape[1]
    tile = side - window
    vmem = pl.BlockSpec(memory_space=pltpu.VMEM)
    hbm = pl.BlockSpec(memory_space=pl.ANY)
    return pl.pallas_call(
        fold_kernel,
        out_shape=(
            jax.ShapeDtypeStruct((2, tile, tile), jnp.float32),
            jax.ShapeDtypeStruct(illumination.shape, jnp.float32),
        ),
        in_specs=[hbm, hbm, vmem, vmem],
        out_specs=(vmem, vmem),
        scratch_shapes=[
            pltpu.VMEM((2, side, tile), jnp.float32),
            pltpu.VMEM((2, tile, tile), jnp.float32),
            pltpu.VMEM((2, window, window), jnp.float32),
            pltpu.VMEM((2, side, window), jnp.float32),
            pltpu.VMEM((2, window, tile), jnp.float32),
            pltpu.SemaphoreType.DMA((5,)),
            pltpu.SemaphoreType.DMA((5,)),
            pltpu.SemaphoreType.DMA((2,)),
        ] + ProbeSum.scratch(window, lax.axis_size("ty"), lax.axis_size("tx")) + Boundary.scratch(window),
        compiler_params=pltpu.CompilerParams(
            collective_id=2, has_side_effects=True, vmem_limit_bytes=VMEM_LIMIT),
        name="fold",
    )(grad, extended, illumination, probe_grad)


def body(specimen, illumination, patterns, scan_offsets, counts):
    window = illumination.shape[1]
    tile = specimen.shape[1]
    row_anchor = lax.axis_index("ty") * tile
    col_anchor = lax.axis_index("tx") * tile
    offsets = scan_offsets[0] - jnp.stack([row_anchor, col_anchor])[None, :].astype(jnp.int32)
    count = counts.reshape(1)
    dft = tables(window)
    extended, measured = fetch(specimen, patterns)
    for iteration in range(ITERS):
        grad, probe_grad = slot_gradients(count, offsets, extended, illumination, measured, dft)
        if iteration < ITERS - 1:
            extended, illumination = exchange(grad, extended, illumination, probe_grad)
        else:
            specimen, illumination = fold(grad, extended, illumination, probe_grad)
    return (specimen, illumination)


def solution(mesh):
    placed = (
        P(None, "ty", "tx"),
        P(),
        P("ty", "tx", None, None),
        P("ty", "tx", None),
        P("ty", "tx"),
    )
    return jax.shard_map(
        body, mesh=mesh, in_specs=placed, out_specs=(P(None, "ty", "tx"), P()), check_vma=False
    )
```

```python
import functools

import jax
import jax.numpy as jnp
import ml_dtypes
import numpy as np
from jax import lax
from jax.experimental import pallas as pl
from jax.experimental.pallas import tpu as pltpu
from jax.sharding import PartitionSpec as P

POS_DEV = 3
ITERS = 2
OBJECT_STEP = 0.05
PROBE_GAIN = 0.5
MESH = pl.DeviceIdType.MESH
VMEM_LIMIT = 36 * 1024 * 1024
SUBLANES = 8
TOGETHER = 3


def real_table(window):
    half = window // 2
    k = np.arange(window)
    freq = np.where(k <= half, k, k - half)
    angles = 2.0 * np.pi * ((freq[:, None] * k[None, :]) % window) / window
    table = np.where((k <= half)[:, None], np.cos(angles), np.sin(angles))
    return table / np.sqrt(window)


def split_table(table):
    high = table.astype(ml_dtypes.bfloat16)
    low = (table - high.astype(np.float64)).astype(ml_dtypes.bfloat16)
    return high, low


def tables(window):
    high, low = split_table(real_table(window))
    return [jnp.asarray(t) for t in (high, low, high.T, low.T)]


def split(value):
    high = value.astype(jnp.bfloat16)
    low = (value - high.astype(jnp.float32)).astype(jnp.bfloat16)
    return high, low


def dot(left, right):
    return jnp.dot(left, right, preferred_element_type=jnp.float32)


def left_product(table, value):
    high, low = split(value)
    return dot(table[0][...], high) + dot(table[1][...], high) + dot(table[0][...], low)


def right_product(value, table):
    high, low = split(value)
    return dot(high, table[0][...]) + dot(high, table[1][...]) + dot(low, table[0][...])


def compute_kernel(
    count_ref, offsets_ref, specimen_ref, probe_ref, measured_ref,
    high_ref, low_ref, high_t_ref, low_t_ref,
    grad_ref, probe_grad_ref,
    windows, levels, window_sems, level_sems,
):
    table, table_t = (high_ref, low_ref), (high_t_ref, low_t_ref)
    window = probe_ref.shape[1]
    half = window // 2
    lanes = 128
    blocks = window // lanes
    lane = lax.broadcasted_iota(jnp.int32, (window + SUBLANES, lanes), 1)
    sublane = lax.broadcasted_iota(jnp.int32, (window // SUBLANES, SUBLANES, lanes), 1)
    sublane_ext = lax.broadcasted_iota(jnp.int32, (window // SUBLANES + 1, SUBLANES, lanes), 1)
    first_row = lax.broadcasted_iota(jnp.int32, (half, window), 0) == 0
    first_col = lax.broadcasted_iota(jnp.int32, (window, half), 1) == 0

    probe_real, probe_imag = probe_ref[0], probe_ref[1]

    def position(slot):
        row = offsets_ref[slot, 0]
        col = offsets_ref[slot, 1]
        row_block = pl.multiple_of((row // SUBLANES) * SUBLANES, SUBLANES)
        col_block = pl.multiple_of((col // lanes) * lanes, lanes)
        return row_block, col_block, row - row_block, col - col_block

    def place(where, part, j):
        return (
            part,
            pl.ds(where[0], window + SUBLANES),
            pl.ds(pl.multiple_of(where[1] + lanes * j, lanes), lanes),
        )

    def loads(slot):
        row_block, col_block, _, _ = position(slot)
        rows, cols = pl.ds(row_block, window + SUBLANES), pl.ds(col_block, window + lanes)
        return (
            pltpu.make_async_copy(specimen_ref.at[:, rows, cols], windows.at[slot], window_sems.at[slot]),
            pltpu.make_async_copy(measured_ref.at[slot], levels.at[slot], level_sems.at[slot]),
        )

    def cut(slot, where, part):
        row_rest, col_rest = where[2:]
        keep = lane < lanes - col_rest
        pieces = [
            pltpu.roll(
                windows[slot, part, :, lanes * j:lanes * (j + 1)], lax.rem(lanes - col_rest, lanes), 1)
            for j in range(blocks + 1)
        ]
        columns = []
        for j in range(blocks):
            taken = jnp.where(keep, pieces[j], pieces[j + 1])
            taken = taken.reshape(window // SUBLANES + 1, SUBLANES, lanes)
            taken = pltpu.roll(taken, lax.rem(SUBLANES - row_rest, SUBLANES), 1)
            upper = sublane < SUBLANES - row_rest
            columns.append(jnp.where(upper, taken[:-1], taken[1:]).reshape(window, lanes))
        return jnp.concatenate(columns, axis=1)

    def add_term(where, part, term):
        row_rest, col_rest = where[2:]
        before = lane < col_rest
        above = sublane_ext < row_rest
        turned = []
        for j in range(blocks):
            piece = term[:, lanes * j:lanes * (j + 1)]
            piece = piece.reshape(window // SUBLANES, SUBLANES, lanes)
            piece = pltpu.roll(piece, row_rest, 1)
            edge = jnp.zeros((1, SUBLANES, lanes), jnp.float32)
            piece = jnp.where(
                above,
                jnp.concatenate([edge, piece], axis=0),
                jnp.concatenate([piece, edge], axis=0),
            ).reshape(window + SUBLANES, lanes)
            turned.append(pltpu.roll(piece, col_rest, 1))
        for j in range(blocks + 1):
            if j == 0:
                add = jnp.where(before, 0.0, turned[0])
            elif j == blocks:
                add = jnp.where(before, turned[-1], 0.0)
            else:
                add = jnp.where(before, turned[j - 1], turned[j])
            grad_ref[place(where, part, j)] += add

    def exit_wave(patch):
        real, imag = patch
        psi_real = probe_real * real - probe_imag * imag
        psi_imag = probe_real * imag + probe_imag * real
        return jnp.concatenate([psi_real, psi_imag], axis=1)

    def unfold_rows(both):
        u_top, v_top = both[:half, :window], both[:half, window:]
        u_bot, v_bot = both[half:, :window], both[half:, window:]
        u_add = jnp.where(first_row, 0.0, u_bot)
        v_add = jnp.where(first_row, 0.0, v_bot)
        return jnp.concatenate([
            u_top + v_add, jnp.where(first_row, u_bot, u_top - v_bot),
            v_top - u_add, jnp.where(first_row, v_bot, v_top + u_bot)], axis=0)

    def unfold_cols(both):
        u_top, v_top = both[:window, :half], both[window:, :half]
        u_bot, v_bot = both[:window, half:], both[window:, half:]
        u_add = jnp.where(first_col, 0.0, u_bot)
        v_add = jnp.where(first_col, 0.0, v_bot)
        far_real = jnp.concatenate([u_top + v_add, jnp.where(first_col, u_bot, u_top - v_bot)], axis=1)
        far_imag = jnp.concatenate([v_top - u_add, jnp.where(first_col, v_bot, v_top + u_bot)], axis=1)
        return far_real, far_imag

    def fold_rows(g_real, g_imag):
        r_top, r_bot = g_real[:half], g_real[half:]
        i_top, i_bot = g_imag[:half], g_imag[half:]
        z_real = jnp.concatenate(
            [r_top + jnp.where(first_row, 0.0, r_bot), jnp.where(first_row, r_bot, i_bot - i_top)], axis=0)
        z_imag = jnp.concatenate(
            [i_top + jnp.where(first_row, 0.0, i_bot), jnp.where(first_row, i_bot, r_top - r_bot)], axis=0)
        return jnp.concatenate([z_real, z_imag], axis=1)

    def fold_cols(both):
        r_top, r_bot = both[:, :half], both[:, half:window]
        i_top, i_bot = both[:, window:window + half], both[:, window + half:]
        z_real = jnp.concatenate(
            [r_top + jnp.where(first_col, 0.0, r_bot), jnp.where(first_col, r_bot, i_bot - i_top)], axis=1)
        z_imag = jnp.concatenate(
            [i_top + jnp.where(first_col, 0.0, i_bot), jnp.where(first_col, i_bot, r_top - r_bot)], axis=1)
        return jnp.concatenate([z_real, z_imag], axis=0)

    def visit(step, carry):
        slots = [TOGETHER * step + i for i in range(TOGETHER)]
        where = [position(slot) for slot in slots]
        live = [(slot < count_ref[0]).astype(jnp.float32) for slot in slots]
        for slot in slots:
            for copy in loads(slot):
                copy.wait()
        patches = [(cut(slot, w, 0), cut(slot, w, 1)) for slot, w in zip(slots, where)]
        waves = [left_product(table, exit_wave(patch)) for patch in patches]
        waves = [right_product(unfold_rows(wave), table_t) for wave in waves]
        sources = []
        for wave, slot, on in zip(waves, slots, live):
            far_real, far_imag = unfold_cols(wave)
            factor = on * (far_real * far_real + far_imag * far_imag - levels[slot])
            sources.append(fold_rows(factor * far_real, factor * far_imag))
        waves = [left_product(table_t, source) for source in sources]
        waves = [right_product(fold_cols(wave), table) for wave in waves]
        for wave, patch, w in zip(waves, patches, where):
            chi_real, chi_imag = wave[:window], wave[window:]
            probe_grad_ref[0] += patch[0] * chi_real + patch[1] * chi_imag
            probe_grad_ref[1] += patch[0] * chi_imag - patch[1] * chi_real
            add_term(w, 0, probe_real * chi_real + probe_imag * chi_imag)
            add_term(w, 1, probe_real * chi_imag - probe_imag * chi_real)
        return carry

    steps = (count_ref[0] + TOGETHER - 1) // TOGETHER

    def fetch_slot(slot, carry):
        for copy in loads(slot):
            copy.start()
        return carry

    lax.fori_loop(0, steps * TOGETHER, fetch_slot, 0)
    grad_ref[...] = jnp.zeros_like(grad_ref)
    probe_grad_ref[...] = jnp.zeros_like(probe_grad_ref)
    lax.fori_loop(0, steps, visit, 0)


def slot_gradients(count, offsets, extended, illumination, measured, dft):
    smem = pl.BlockSpec(memory_space=pltpu.SMEM)
    vmem = pl.BlockSpec(memory_space=pltpu.VMEM)
    hbm = pl.BlockSpec(memory_space=pl.ANY)
    slots, window, _ = measured.shape
    return pl.pallas_call(
        compute_kernel,
        out_shape=(
            jax.ShapeDtypeStruct(extended.shape, jnp.float32),
            jax.ShapeDtypeStruct(illumination.shape, jnp.float32),
        ),
        in_specs=[smem, smem, hbm, vmem, hbm] + [vmem] * 4,
        out_specs=(vmem, vmem),
        scratch_shapes=[
            pltpu.VMEM((slots, 2, window + SUBLANES, window + 128), jnp.float32),
            pltpu.VMEM(measured.shape, jnp.float32),
            pltpu.SemaphoreType.DMA((slots,)),
            pltpu.SemaphoreType.DMA((slots,)),
        ],
        compiler_params=pltpu.CompilerParams(vmem_limit_bytes=VMEM_LIMIT),
        name="slot_gradients",
    )(count, offsets, extended, illumination, measured, *dft)


def place_of():
    return lax.axis_index("ty"), lax.axis_index("tx"), lax.axis_size("ty"), lax.axis_size("tx")


def send_to(source, target, sems, index, row, col):
    send_sem, recv_sem = sems
    return pltpu.make_async_remote_copy(
        src_ref=source,
        dst_ref=target,
        send_sem=send_sem.at[index],
        recv_sem=recv_sem.at[index],
        device_id=(row, col),
        device_id_type=MESH,
    )


def wait_bytes(ref, sem):
    pltpu.make_async_copy(ref, ref, sem).wait()


def greet(partners):
    barrier = pltpu.get_barrier_semaphore()
    for exists, row, col in partners:
        @pl.when(exists)
        def _():
            pl.semaphore_signal(barrier, inc=1, device_id=(row, col), device_id_type=MESH)
    pl.semaphore_wait(barrier, sum(jnp.int32(exists) for exists, _, _ in partners))


class Boundary:
    LINES = 4

    def __init__(self, relay, sems):
        self.relay = relay
        self.first_send, self.hop_recv, self.hop_send, self.last_recv = sems
        self.a, self.b, _, n = place_of()
        self.n = n
        half = n // 2
        self.low, self.high = half - 1, half
        if n >= 16:
            inner = ((half, half + 3, 3, half - 1), (half, n - 4, half - 4, half - 1))
        else:
            inner = ((half, half + 2, 2, half - 1), (half, n - 3, half - 3, half - 1))
        self.paths = ((half, 0, half - 1), *inner, (half, n - 1, half - 1))
        self.at_low, self.at_high = self.b == self.low, self.b == self.high

    @staticmethod
    def scratch(window):
        return [
            pltpu.VMEM((2, 3, window // 2, window), jnp.float32),
            pltpu.SemaphoreType.DMA((2, 3, Boundary.LINES)),
            pltpu.SemaphoreType.DMA((2, 3)),
            pltpu.SemaphoreType.DMA((2, 3)),
            pltpu.SemaphoreType.DMA((2, 3, Boundary.LINES)),
        ]

    def partners(self, every):
        pairs = sorted({tuple(sorted(pair)) for path in self.paths for pair in zip(path, path[1:])})
        found = []
        for p, q in pairs:
            if p // 2 != q // 2 and (every or p % 2 != q % 2):
                found += [(self.b == p, self.a, q), (self.b == q, self.a, p)]
        return found

    def before_z(self, way):
        n_x, n_y, _ = ProbeSum.sizes(lax.axis_size("ty"), self.n)
        high = 2 * n_y
        nodes = sorted({p for line in range(self.LINES)
                        for p, q in zip(self.path(way, line), self.path(way, line)[1:]) if (p >= high) != (q >= high)})
        found = self.b == nodes[0]
        for node in nodes[1:]:
            found = found | (self.b == node)
        return found

    def path(self, way, line):
        return self.paths[line] if way == 1 else self.paths[line][::-1]

    def origin(self, way):
        return self.low if way == 0 else self.high

    @staticmethod
    def quarter(ref, line):
        rows = ref.shape[1] // 2
        return ref.at[line // 2, pl.ds(line % 2 * rows, rows), :]

    def leg(self, way, index, line, k, source, target):
        path = self.path(way, line)
        last = k == len(path) - 2
        return pltpu.make_async_remote_copy(
            src_ref=self.quarter(source, line) if k == 0 else self.relay.at[way, index],
            dst_ref=self.quarter(target, line) if last else self.relay.at[way, index],
            send_sem=self.first_send.at[way, index, line] if k == 0 else self.hop_send.at[way, index],
            recv_sem=self.last_recv.at[way, index, line] if last else self.hop_recv.at[way, index],
            device_id=(self.a, path[k + 1]),
            device_id_type=MESH,
        )

    def start(self, way, index, source, target):
        for line in range(self.LINES):
            self.leg(way, index, line, 0, source, target).start()

    def relays(self, way):
        return [(line, k, node) for line in range(self.LINES)
                for k, node in enumerate(self.path(way, line)) if 0 < k < len(self.path(way, line)) - 1]

    def pass_on(self, way, index, source, target):
        for line, k, node in self.relays(way):
            @pl.when(self.b == node)
            def _():
                self.leg(way, index, line, k - 1, source, target).wait_recv()
                self.leg(way, index, line, k, source, target).start()

    def passed(self, way, index, source, target):
        for line, k, node in self.relays(way):
            @pl.when(self.b == node)
            def _():
                self.leg(way, index, line, k, source, target).wait_send()

    def wait_recv(self, way, index, source, target):
        for line in range(self.LINES):
            self.leg(way, index, line, len(self.path(way, line)) - 2, source, target).wait_recv()

    def wait_send(self, way, index, source, target):
        for line in range(self.LINES):
            self.leg(way, index, line, 0, source, target).wait_send()


class Sideways:
    def __init__(self, boundary, way, index, source, target, sems, slot):
        a, b, _, n_tx = place_of()
        self.boundary = boundary
        self.strip = (way, index, source, target)
        step = 1 if way == 0 else -1
        self.direct = send_to(source, target, sems, slot, a, b + step)
        left, right = b > 0, b < n_tx - 1
        self.has_target, self.has_source = (right, left) if way == 0 else (left, right)
        self.from_origin = b == boundary.origin(way)
        self.at_end = b == boundary.origin(1 - way)

    def start(self):
        self.start_relayed()
        self.start_direct()

    def start_relayed(self):
        pl.when(self.from_origin)(lambda: self.boundary.start(*self.strip))

    def start_direct(self):
        pl.when(self.has_target & ~self.from_origin)(self.direct.start)

    def pass_on(self):
        self.boundary.pass_on(*self.strip)

    def wait_recv(self):
        pl.when(self.at_end)(lambda: self.boundary.wait_recv(*self.strip))
        pl.when(self.has_source & ~self.at_end)(self.direct.wait_recv)

    def wait_send(self):
        pl.when(self.from_origin)(lambda: self.boundary.wait_send(*self.strip))
        pl.when(self.has_target & ~self.from_origin)(self.direct.wait_send)

    def passed(self):
        self.boundary.passed(*self.strip)


def fetch_kernel(
    specimen, patterns, extended, measured_out,
    measured, staged, send, recv, local, *rest,
):
    a, b, n_ty, n_tx = place_of()
    window = measured.shape[1]
    tile = specimen.shape[1]
    half = window // 2
    up, down, left, right = a > 0, a < n_ty - 1, b > 0, b < n_tx - 1
    boundary = Boundary(rest[0], rest[1:])
    near = (True, a, b + 1 - 2 * lax.rem(b, 2))
    greet([(up, a - 1, b), (down, a + 1, b), near, far_neighbour(a, b, n_tx)] + boundary.partners(True))
    sems = (send, recv)
    first, second = pl.ds(0, window), pl.ds(window, tile - window)
    beyond, inside = pl.ds(tile, window), pl.ds(0, tile)

    def aside(index, source, rows):
        return Sideways(
            boundary, 1, index, source.at[:, rows, first], extended.at[:, rows, beyond], sems, 2 + index)

    up_a = send_to(specimen.at[:, first, first], extended.at[:, beyond, first], sems, 0, a - 1, b)
    up_b = send_to(specimen.at[:, first, second], extended.at[:, beyond, second], sems, 1, a - 1, b)
    aside_a = aside(0, specimen, first)
    aside_b = aside(1, specimen, second)
    corner = send_to(
        extended.at[:, beyond, first], extended.at[:, beyond, beyond], sems, 4, a, b - 1)
    corner_up = send_to(
        extended.at[:, first, beyond], extended.at[:, beyond, beyond], sems, 5, a - 1, b)
    corner_left = down & left & ~boundary.at_high
    stage = pltpu.make_async_copy(specimen, staged, local.at[0])
    keep = pltpu.make_async_copy(staged, extended.at[:, inside, inside], local.at[2])
    load = pltpu.make_async_copy(patterns.at[0], measured, local.at[1])
    hold = (lax.rem(a, ProbeSum.sizes(n_ty, n_tx)[0]) == 0) & up & boundary.before_z(1)
    pl.when(up & ~hold)(up_a.start)
    aside_a.start()
    aside_b.start()
    load.start()
    stage.start()
    stage.wait()
    keep.start()

    @pl.when(hold)
    def _():
        aside_a.pass_on()
        aside_b.pass_on()
        up_a.start()

    pl.when(~hold)(aside_a.pass_on)

    @pl.when(up)
    def _():
        up_a.wait_send()
        up_b.start()

    pl.when(~hold)(aside_b.pass_on)
    pl.when(down)(up_a.wait_recv)
    pl.when(corner_left)(corner.start)

    @pl.when(boundary.at_low)
    def _():
        aside_a.wait_recv()
        pl.when(up)(corner_up.start)

    load.wait()
    row = lax.broadcasted_iota(jnp.int32, (window, window), 0)
    col = lax.broadcasted_iota(jnp.int32, (window, window), 1)

    def order(place, freq):
        picked = jnp.where(place <= half, place, window + half - place) == freq
        return picked.astype(jnp.float32).astype(jnp.bfloat16)

    reorder = jnp.concatenate([order(row, col)] * 3, axis=1)
    reorder_back = jnp.concatenate([order(col, row)] * 3, axis=0)

    def rearrange(slot, carry):
        def pieces(value):
            high, low = split(value)
            rest = (value - high.astype(jnp.float32) - low.astype(jnp.float32)).astype(jnp.bfloat16)
            return [high, low, rest]

        rows = jnp.dot(
            reorder, jnp.concatenate(pieces(measured[slot]), axis=0), preferred_element_type=jnp.float32)
        measured_out[slot] = jnp.dot(
            jnp.concatenate(pieces(rows), axis=1), reorder_back, preferred_element_type=jnp.float32)
        return carry

    lax.fori_loop(0, measured.shape[0], rearrange, 0)
    keep.wait()
    pl.when(~boundary.at_low)(aside_a.wait_recv)
    aside_b.wait_recv()
    pl.when(up)(up_b.wait_send)
    pl.when(down)(up_b.wait_recv)
    pl.when(corner_left)(corner.wait_send)
    pl.when(down & right & ~boundary.at_low)(corner.wait_recv)

    @pl.when(boundary.at_low)
    def _():
        pl.when(up)(corner_up.wait_send)
        pl.when(down)(corner_up.wait_recv)

    for strip in (aside_a, aside_b):
        strip.wait_send()
        strip.passed()


def fetch(specimen, patterns):
    window = patterns.shape[2]
    side = specimen.shape[1] + window
    vmem = pl.BlockSpec(memory_space=pltpu.VMEM)
    hbm = pl.BlockSpec(memory_space=pl.ANY)
    return pl.pallas_call(
        fetch_kernel,
        out_shape=(
            jax.ShapeDtypeStruct((2, side, side), jnp.float32),
            jax.ShapeDtypeStruct(patterns.shape[1:], jnp.float32),
        ),
        in_specs=[hbm, hbm],
        out_specs=(hbm, vmem),
        scratch_shapes=[
            pltpu.VMEM(patterns.shape[1:], jnp.float32),
            pltpu.VMEM(specimen.shape, jnp.float32),
            pltpu.SemaphoreType.DMA((6,)),
            pltpu.SemaphoreType.DMA((6,)),
            pltpu.SemaphoreType.DMA((3,)),
        ] + Boundary.scratch(window),
        compiler_params=pltpu.CompilerParams(
            collective_id=0, has_side_effects=True, vmem_limit_bytes=VMEM_LIMIT + 26 * 1024 * 1024),
        name="fetch",
    )(specimen, patterns)


class ProbeSum:
    STAGES = 7

    def __init__(self, terms, buffers, send, recv):
        self.terms = terms
        self.mate, self.mine, self.y_in, self.y_sum, self.z_in, self.x_in, self.z_out, self.full, self.other = buffers
        self.send, self.recv = send, recv
        self.a, self.b, n_ty, n_tx = place_of()
        self.n_x, self.n_y, self.n_z = self.sizes(n_ty, n_tx)
        self.n_low = self.n_z // 2
        self.devices = n_ty * n_tx
        self.core = lax.rem(self.b, 2)
        self.y = lax.rem(self.b // 2, self.n_y)
        self.x = lax.rem(self.a, self.n_x)
        self.z = self.b // (2 * self.n_y) * self.n_low + self.a // self.n_x
        self.mate_col = self.b + 1 - 2 * self.core
        self.y_rows = self.full.shape[0] // self.n_y
        self.z_rows = self.y_rows // self.n_z

    @staticmethod
    def sizes(n_ty, n_tx):
        n_x = 4 if n_ty == 16 else 2
        return n_x, n_tx // 4, 2 * (n_ty // n_x)

    @staticmethod
    def scratch(window, n_ty, n_tx):
        n_x, n_y, n_z = ProbeSum.sizes(n_ty, n_tx)
        y_rows = window // n_y
        z_rows = y_rows // n_z
        shapes = [
            (window, window), (window, window), (n_y - 1, y_rows, window), (y_rows, window),
            (n_z - 1, z_rows, window), (n_x, z_rows, window), (y_rows, window),
            (window, window), (window, window),
        ]
        return [pltpu.VMEM(shape, jnp.float32) for shape in shapes] + [
            pltpu.SemaphoreType.DMA((ProbeSum.STAGES,)),
            pltpu.SemaphoreType.DMA((ProbeSum.STAGES,)),
        ]

    def at_y(self, y):
        return self.a, (self.b // (2 * self.n_y)) * 2 * self.n_y + 2 * y + self.core

    def at_z(self, z):
        return lax.rem(z, self.n_low) * self.n_x + self.x, (z // self.n_low) * 2 * self.n_y + 2 * self.y + self.core

    def at_x(self, x):
        return self.a - self.x + x, self.b

    def partners(self):
        found = [(True, self.a, self.mate_col)]
        found += [(True, *self.at_y(lax.rem(self.y + d, self.n_y))) for d in range(1, self.n_y)]
        found += [(True, *self.at_z(lax.rem(self.z + d, self.n_z))) for d in range(1, self.n_z)]
        found += [(True, *self.at_x(lax.rem(self.x + d, self.n_x))) for d in range(1, self.n_x)]
        n_ty = self.n_low * self.n_x
        wraps_down = (self.x == self.n_x - 1) & (self.a < n_ty - 1)
        wraps_up = (self.x == 0) & (self.a > 0)
        found.append((wraps_down | wraps_up, jnp.where(wraps_up, self.a - 1, self.a + 1), self.b))
        return found

    def to(self, source, target, stage, row, col):
        return send_to(source, target, (self.send, self.recv), stage, row, col)

    @staticmethod
    def rows(ref, index, count):
        return ref.at[pl.ds(pl.multiple_of(index * count, SUBLANES), count), :]

    def each(self, count, go):
        def step(d, carry):
            go(d)
            return carry

        lax.fori_loop(1, count, step, 0)

    def start(self):
        self.to(self.terms.at[1 - self.core], self.mate, 0, self.a, self.mate_col).start()

    def scatter_y(self):
        self.to(self.terms.at[1 - self.core], self.mate, 0, self.a, self.mate_col).wait()
        self.mine[...] = self.terms[self.core] + self.mate[...]

        def go(d):
            y = lax.rem(self.y + d, self.n_y)
            self.to(self.rows(self.mine, y, self.y_rows), self.y_in.at[d - 1], 1, *self.at_y(y)).start()

        self.each(self.n_y, go)

    def scatter_z(self):
        wait_bytes(self.y_in, self.recv.at[1])
        total = self.rows(self.mine, self.y, self.y_rows)[...]
        for d in range(self.n_y - 1):
            total = total + self.y_in[d]
        self.y_sum[...] = total

        def go(d):
            z = lax.rem(self.z + d, self.n_z)
            self.to(self.rows(self.y_sum, z, self.z_rows), self.z_in.at[d - 1], 2, *self.at_z(z)).start()

        self.each(self.n_z, go)

    def across_x(self):
        wait_bytes(self.z_in, self.recv.at[2])
        total = self.rows(self.y_sum, self.z, self.z_rows)[...]
        for d in range(self.n_z - 1):
            total = total + self.z_in[d]
        self.x_in[self.x] = total

        def go(d):
            x = lax.rem(self.x + d, self.n_x)
            self.to(self.x_in.at[self.x], self.x_in.at[self.x], 3, *self.at_x(x)).start()

        self.each(self.n_x, go)

    def gather_z(self):
        wait_bytes(self.x_in.at[pl.ds(0, self.n_x - 1)], self.recv.at[3])
        total = self.x_in[0]
        for i in range(1, self.n_x):
            total = total + self.x_in[i]
        own = self.rows(self.z_out, self.z, self.z_rows)
        own[...] = total

        def go(d):
            z = lax.rem(self.z + d, self.n_z)
            self.to(own, own, 4, *self.at_z(z)).start()

        self.each(self.n_z, go)

    def gather_y(self):
        wait_bytes(self.z_out.at[pl.ds(0, (self.n_z - 1) * self.z_rows)], self.recv.at[4])
        own = self.rows(self.full, self.y, self.y_rows)
        own[...] = self.z_out[...]

        def go(d):
            y = lax.rem(self.y + d, self.n_y)
            self.to(self.z_out, own, 5, *self.at_y(y)).start()

        self.each(self.n_y, go)

    def share(self):
        wait_bytes(self.full.at[pl.ds(0, (self.n_y - 1) * self.y_rows)], self.recv.at[5])
        self.to(self.full, self.other, 6, self.a, self.mate_col).start()

    def finish(self, probe, probe_out):
        step = PROBE_GAIN / (POS_DEV * self.devices)
        probe_out[self.core] = probe[self.core] - step * self.full[...]
        self.to(self.full, self.other, 6, self.a, self.mate_col).wait()
        probe_out[1 - self.core] = probe[1 - self.core] - step * self.other[...]
        wait_bytes(self.y_in, self.send.at[1])
        wait_bytes(self.z_in, self.send.at[2])
        wait_bytes(self.x_in.at[pl.ds(0, self.n_x - 1)], self.send.at[3])
        wait_bytes(self.z_out.at[pl.ds(0, (self.n_z - 1) * self.z_rows)], self.send.at[4])
        wait_bytes(self.full.at[pl.ds(0, (self.n_y - 1) * self.y_rows)], self.send.at[5])


def far_neighbour(a, b, n_tx):
    core = lax.rem(b, 2)
    col = b - 1 + 2 * core
    return ((col >= 0) & (col < n_tx) & (b != n_tx // 2 - 1) & (b != n_tx // 2), a, col)


def exchange_kernel(
    grad, extended, probe, probe_grad, extended_out, probe_out,
    gv, ev, from_left, from_right, from_up, from_down, send, recv, local,
    *rest,
):
    a, b, n_ty, n_tx = place_of()
    window = probe.shape[1]
    side = gv.shape[1]
    tile = side - window
    core = lax.rem(b, 2)
    has_up, has_down, has_left, has_right = a > 0, a < n_ty - 1, b > 0, b < n_tx - 1
    odd = core == 1
    total = ProbeSum(probe_grad, rest[:9], *rest[9:11])
    boundary = Boundary(rest[11], rest[12:])
    greet(total.partners() + [far_neighbour(a, b, n_tx)] + boundary.partners(False))
    sems = (send, recv)
    start, middle, end = pl.ds(0, window), pl.ds(window, tile - window), pl.ds(tile, window)

    def across(rows, index):
        return (
            Sideways(boundary, 0, index, grad.at[:, rows, end], from_left.at[:, rows, :], sems, 2 * index),
            Sideways(boundary, 1, index, grad.at[:, rows, start], from_right.at[:, rows, :], sems, 2 * index + 1),
        )

    def along(source, cols, index):
        return (
            send_to(source.at[:, end, cols], from_up.at[:, :, cols], sems, index, a + 1, b),
            send_to(source.at[:, start, cols], from_down.at[:, :, cols], sems, index + 1, a - 1, b),
        )

    right_top, left_top = across(start, 0)
    right_end, left_end = across(end, 1)
    right_mid, left_mid = across(middle, 2)
    down_1, up_1 = along(grad, middle, 6)
    down_0, up_0 = along(gv, start, 8)
    down_2, up_2 = along(gv, end, 10)
    keep_top = send_to(ev.at[:, start, start], extended_out.at[:, start, end], sems, 12, a, b - 1)
    keep_end = send_to(ev.at[:, end, start], extended_out.at[:, end, end], sems, 13, a, b - 1)

    load_grad = pltpu.make_async_copy(grad, gv, local.at[0])
    load_extended = pltpu.make_async_copy(extended, ev, local.at[1])

    outer = (right_top, right_end, left_top, left_end)
    total.start()
    right_top.start()
    left_top.start()
    pl.when(has_down)(down_1.start)
    pl.when(has_up)(up_1.start)
    load_grad.start()
    load_extended.start()
    total.scatter_y()
    right_end.start()
    left_end.start()
    right_mid.start_relayed()
    left_mid.start_relayed()
    right_top.pass_on()
    left_top.pass_on()
    total.scatter_z()
    right_end.pass_on()
    left_end.pass_on()
    total.across_x()
    late = boundary.at_low | boundary.at_high

    total.gather_z()
    pl.when(late)(total.gather_y)
    load_grad.wait()
    right_top.wait_recv()
    right_end.wait_recv()

    @pl.when(has_left)
    def _():
        gv[:, start, start] += from_left[:, start, :]
        gv[:, end, start] += from_left[:, end, :]

    pl.when(has_down)(down_0.start)
    pl.when(has_up)(up_0.start)
    left_top.wait_recv()
    left_end.wait_recv()

    @pl.when(has_right)
    def _():
        gv[:, start, end] += from_right[:, start, :]
        gv[:, end, end] += from_right[:, end, :]

    pl.when(has_down & odd)(down_2.start)
    pl.when(has_up & odd)(up_2.start)

    pl.when(~late)(total.gather_y)
    for strip in outer:
        strip.wait_send()
    right_mid.start_direct()
    left_mid.start_direct()
    right_mid.pass_on()
    left_mid.pass_on()
    load_extended.wait()
    right_mid.wait_recv()
    left_mid.wait_recv()

    @pl.when(has_left)
    def _():
        gv[:, middle, start] += from_left[:, middle, :]

    @pl.when(has_right)
    def _():
        gv[:, middle, end] += from_right[:, middle, :]

    ev[:, middle, :] -= OBJECT_STEP * gv[:, middle, :]
    store_mid = pltpu.make_async_copy(ev.at[:, middle, :], extended_out.at[:, middle, :], local.at[0])
    store_mid.start()
    total.share()

    def update(rows, cols, received, exists):
        @pl.when(exists)
        def _():
            ev[:, rows, cols] -= OBJECT_STEP * (gv[:, rows, cols] + received[:, :, cols])

        @pl.when(jnp.logical_not(exists))
        def _():
            ev[:, rows, cols] -= OBJECT_STEP * gv[:, rows, cols]

    pl.when(has_up)(down_0.wait_recv)
    pl.when(has_down)(up_0.wait_recv)
    update(start, start, from_up, has_up)
    update(end, start, from_down, has_down)

    @pl.when(odd)
    def _():
        keep_top.start()
        keep_end.start()

    pl.when(has_up)(down_1.wait_recv)
    pl.when(has_down)(up_1.wait_recv)
    update(start, middle, from_up, has_up)
    update(end, middle, from_down, has_down)
    inner = pl.ds(0, tile)
    store_top = pltpu.make_async_copy(ev.at[:, start, inner], extended_out.at[:, start, inner], local.at[1])
    store_end = pltpu.make_async_copy(ev.at[:, end, inner], extended_out.at[:, end, inner], local.at[2])
    store_top.start()
    store_end.start()

    @pl.when(odd)
    def _():
        pl.when(has_up)(down_2.wait_recv)
        pl.when(has_down)(up_2.wait_recv)
        update(start, end, from_up, has_up)
        update(end, end, from_down, has_down)
        rim_top = pltpu.make_async_copy(ev.at[:, start, end], extended_out.at[:, start, end], local.at[3])
        rim_end = pltpu.make_async_copy(ev.at[:, end, end], extended_out.at[:, end, end], local.at[4])
        rim_top.start()
        rim_end.start()
        rim_top.wait()
        rim_end.wait()
        keep_top.wait_send()
        keep_end.wait_send()

    total.finish(probe, probe_out)
    right_mid.wait_send()
    left_mid.wait_send()
    for strip in outer + (right_mid, left_mid):
        strip.passed()

    @pl.when(has_down)
    def _():
        down_0.wait_send()
        down_1.wait_send()
        pl.when(odd)(down_2.wait_send)

    @pl.when(has_up)
    def _():
        up_0.wait_send()
        up_1.wait_send()
        pl.when(odd)(up_2.wait_send)

    store_mid.wait()
    store_top.wait()
    store_end.wait()

    @pl.when(jnp.logical_not(odd))
    def _():
        keep_top.wait_recv()
        keep_end.wait_recv()


def exchange(grad, extended, illumination, probe_grad):
    window = illumination.shape[1]
    side = grad.shape[1]
    vmem = pl.BlockSpec(memory_space=pltpu.VMEM)
    hbm = pl.BlockSpec(memory_space=pl.ANY)
    return pl.pallas_call(
        exchange_kernel,
        out_shape=(
            jax.ShapeDtypeStruct(extended.shape, jnp.float32),
            jax.ShapeDtypeStruct(illumination.shape, jnp.float32),
        ),
        in_specs=[hbm, hbm, vmem, vmem],
        out_specs=(hbm, vmem),
        scratch_shapes=[
            pltpu.VMEM((2, side, side), jnp.float32),
            pltpu.VMEM((2, side, side), jnp.float32),
            pltpu.VMEM((2, side, window), jnp.float32),
            pltpu.VMEM((2, side, window), jnp.float32),
            pltpu.VMEM((2, window, side), jnp.float32),
            pltpu.VMEM((2, window, side), jnp.float32),
            pltpu.SemaphoreType.DMA((14,)),
            pltpu.SemaphoreType.DMA((14,)),
            pltpu.SemaphoreType.DMA((5,)),
        ] + ProbeSum.scratch(window, lax.axis_size("ty"), lax.axis_size("tx")) + Boundary.scratch(window),
        compiler_params=pltpu.CompilerParams(
            collective_id=1, has_side_effects=True, vmem_limit_bytes=VMEM_LIMIT),
        name="exchange",
    )(grad, extended, illumination, probe_grad)


def fold_kernel(
    grad, extended, probe, probe_grad, specimen_out, probe_out,
    gv, ev, corner, from_left, from_up, send, recv, local,
    *rest,
):
    a, b, n_ty, n_tx = place_of()
    window = probe.shape[1]
    side = gv.shape[1]
    tile = side - window
    has_up, has_down, has_left, has_right = a > 0, a < n_ty - 1, b > 0, b < n_tx - 1
    total = ProbeSum(probe_grad, rest[:9], *rest[9:11])
    boundary = Boundary(rest[11], rest[12:])
    greet(total.partners() + [far_neighbour(a, b, n_tx)] + boundary.partners(False))
    sems = (send, recv)
    start, middle, end = pl.ds(0, window), pl.ds(window, tile - window), pl.ds(tile, window)
    inner = pl.ds(0, tile)

    def across(rows, index):
        return Sideways(boundary, 0, index, grad.at[:, rows, end], from_left.at[:, rows, :], sems, index)

    right_end = across(end, 0)
    right_top = across(start, 1)
    right_mid = across(middle, 2)
    down_1 = send_to(grad.at[:, end, middle], from_up.at[:, :, middle], sems, 3, a + 1, b)
    down_0 = send_to(corner, from_up.at[:, :, start], sems, 4, a + 1, b)
    load_grad = pltpu.make_async_copy(grad.at[:, :, inner], gv, local.at[0])
    load_extended = pltpu.make_async_copy(extended.at[:, inner, inner], ev, local.at[1])
    total.start()
    right_end.start()
    right_top.start_relayed()
    right_mid.start_relayed()
    pl.when(has_down)(down_1.start)
    load_grad.start()
    load_extended.start()
    total.scatter_y()
    right_top.start_direct()
    right_end.pass_on()
    total.scatter_z()
    right_top.pass_on()
    load_grad.wait()

    @pl.when(boundary.at_high)
    def _():
        total.across_x()
        total.gather_z()
        total.gather_y()

    right_end.wait_recv()

    @pl.when(has_left)
    def _():
        corner[...] = gv[:, end, start] + from_left[:, end, :]

    @pl.when(jnp.logical_not(has_left))
    def _():
        corner[...] = gv[:, end, start]

    @pl.when(~boundary.at_high)
    def _():
        total.across_x()

    pl.when(has_down)(down_0.start)

    @pl.when(~boundary.at_high)
    def _():
        total.gather_z()
        total.gather_y()

    right_end.wait_send()
    right_mid.start_direct()
    right_mid.pass_on()
    load_extended.wait()
    ev[...] -= OBJECT_STEP * gv[:, inner, :]
    total.share()
    right_top.wait_recv()
    right_mid.wait_recv()

    @pl.when(has_left)
    def _():
        ev[:, :, start] -= OBJECT_STEP * from_left[:, inner, :]

    @pl.when(has_up)
    def _():
        down_1.wait_recv()
        down_0.wait_recv()
        ev[:, start, :] -= OBJECT_STEP * from_up[...]

    specimen_out[...] = ev[...]
    total.finish(probe, probe_out)
    right_top.wait_send()
    right_mid.wait_send()
    for strip in (right_end, right_top, right_mid):
        strip.passed()

    @pl.when(has_down)
    def _():
        down_1.wait_send()
        down_0.wait_send()


def fold(grad, extended, illumination, probe_grad):
    window = illumination.shape[1]
    side = grad.shape[1]
    tile = side - window
    vmem = pl.BlockSpec(memory_space=pltpu.VMEM)
    hbm = pl.BlockSpec(memory_space=pl.ANY)
    return pl.pallas_call(
        fold_kernel,
        out_shape=(
            jax.ShapeDtypeStruct((2, tile, tile), jnp.float32),
            jax.ShapeDtypeStruct(illumination.shape, jnp.float32),
        ),
        in_specs=[hbm, hbm, vmem, vmem],
        out_specs=(vmem, vmem),
        scratch_shapes=[
            pltpu.VMEM((2, side, tile), jnp.float32),
            pltpu.VMEM((2, tile, tile), jnp.float32),
            pltpu.VMEM((2, window, window), jnp.float32),
            pltpu.VMEM((2, side, window), jnp.float32),
            pltpu.VMEM((2, window, tile), jnp.float32),
            pltpu.SemaphoreType.DMA((5,)),
            pltpu.SemaphoreType.DMA((5,)),
            pltpu.SemaphoreType.DMA((2,)),
        ] + ProbeSum.scratch(window, lax.axis_size("ty"), lax.axis_size("tx")) + Boundary.scratch(window),
        compiler_params=pltpu.CompilerParams(
            collective_id=2, has_side_effects=True, vmem_limit_bytes=VMEM_LIMIT),
        name="fold",
    )(grad, extended, illumination, probe_grad)


def body(specimen, illumination, patterns, scan_offsets, counts):
    window = illumination.shape[1]
    tile = specimen.shape[1]
    row_anchor = lax.axis_index("ty") * tile
    col_anchor = lax.axis_index("tx") * tile
    offsets = scan_offsets[0] - jnp.stack([row_anchor, col_anchor])[None, :].astype(jnp.int32)
    count = counts.reshape(1)
    dft = tables(window)
    extended, measured = fetch(specimen, patterns)
    for iteration in range(ITERS):
        grad, probe_grad = slot_gradients(count, offsets, extended, illumination, measured, dft)
        if iteration < ITERS - 1:
            extended, illumination = exchange(grad, extended, illumination, probe_grad)
        else:
            specimen, illumination = fold(grad, extended, illumination, probe_grad)
    return (specimen, illumination)


def solution(mesh):
    placed = (
        P(None, "ty", "tx"),
        P(),
        P("ty", "tx", None, None),
        P("ty", "tx", None),
        P("ty", "tx"),
    )
    return jax.shard_map(
        body, mesh=mesh, in_specs=placed, out_specs=(P(None, "ty", "tx"), P()), check_vma=False
    )
```

```python
import functools

import jax
import jax.numpy as jnp
import ml_dtypes
import numpy as np
from jax import lax
from jax.experimental import pallas as pl
from jax.experimental.pallas import tpu as pltpu
from jax.sharding import PartitionSpec as P

POS_DEV = 3
ITERS = 2
OBJECT_STEP = 0.05
PROBE_GAIN = 0.5
MESH = pl.DeviceIdType.MESH
VMEM_LIMIT = 36 * 1024 * 1024
SUBLANES = 8
TOGETHER = 3


def real_table(window):
    half = window // 2
    k = np.arange(window)
    freq = np.where(k <= half, k, k - half)
    angles = 2.0 * np.pi * ((freq[:, None] * k[None, :]) % window) / window
    table = np.where((k <= half)[:, None], np.cos(angles), np.sin(angles))
    return table / np.sqrt(window)


def split_table(table):
    high = table.astype(ml_dtypes.bfloat16)
    low = (table - high.astype(np.float64)).astype(ml_dtypes.bfloat16)
    return high, low


def tables(window):
    high, low = split_table(real_table(window))
    return [jnp.asarray(t) for t in (high, low, high.T, low.T)]


def split(value):
    high = value.astype(jnp.bfloat16)
    low = (value - high.astype(jnp.float32)).astype(jnp.bfloat16)
    return high, low


def dot(left, right):
    return jnp.dot(left, right, preferred_element_type=jnp.float32)


def left_product(table, value):
    high, low = split(value)
    return dot(table[0][...], high) + dot(table[1][...], high) + dot(table[0][...], low)


def right_product(value, table):
    high, low = split(value)
    return dot(high, table[0][...]) + dot(high, table[1][...]) + dot(low, table[0][...])


def compute_kernel(
    count_ref, offsets_ref, specimen_ref, probe_ref, measured_ref,
    high_ref, low_ref, high_t_ref, low_t_ref,
    grad_ref, probe_grad_ref,
    windows, levels, window_sems, level_sems,
):
    table, table_t = (high_ref, low_ref), (high_t_ref, low_t_ref)
    window = probe_ref.shape[1]
    half = window // 2
    lanes = 128
    blocks = window // lanes
    lane = lax.broadcasted_iota(jnp.int32, (window + SUBLANES, lanes), 1)
    sublane = lax.broadcasted_iota(jnp.int32, (window // SUBLANES, SUBLANES, lanes), 1)
    sublane_ext = lax.broadcasted_iota(jnp.int32, (window // SUBLANES + 1, SUBLANES, lanes), 1)
    first_row = lax.broadcasted_iota(jnp.int32, (half, window), 0) == 0
    first_col = lax.broadcasted_iota(jnp.int32, (window, half), 1) == 0

    probe_real, probe_imag = probe_ref[0], probe_ref[1]

    def position(slot):
        row = offsets_ref[slot, 0]
        col = offsets_ref[slot, 1]
        row_block = pl.multiple_of((row // SUBLANES) * SUBLANES, SUBLANES)
        col_block = pl.multiple_of((col // lanes) * lanes, lanes)
        return row_block, col_block, row - row_block, col - col_block

    def place(where, part, j):
        return (
            part,
            pl.ds(where[0], window + SUBLANES),
            pl.ds(pl.multiple_of(where[1] + lanes * j, lanes), lanes),
        )

    def loads(slot):
        row_block, col_block, _, _ = position(slot)
        rows, cols = pl.ds(row_block, window + SUBLANES), pl.ds(col_block, window + lanes)
        return (
            pltpu.make_async_copy(specimen_ref.at[:, rows, cols], windows.at[slot], window_sems.at[slot]),
            pltpu.make_async_copy(measured_ref.at[slot], levels.at[slot], level_sems.at[slot]),
        )

    def cut(slot, where, part):
        row_rest, col_rest = where[2:]
        keep = lane < lanes - col_rest
        pieces = [
            pltpu.roll(
                windows[slot, part, :, lanes * j:lanes * (j + 1)], lax.rem(lanes - col_rest, lanes), 1)
            for j in range(blocks + 1)
        ]
        columns = []
        for j in range(blocks):
            taken = jnp.where(keep, pieces[j], pieces[j + 1])
            taken = taken.reshape(window // SUBLANES + 1, SUBLANES, lanes)
            taken = pltpu.roll(taken, lax.rem(SUBLANES - row_rest, SUBLANES), 1)
            upper = sublane < SUBLANES - row_rest
            columns.append(jnp.where(upper, taken[:-1], taken[1:]).reshape(window, lanes))
        return jnp.concatenate(columns, axis=1)

    def add_term(where, part, term):
        row_rest, col_rest = where[2:]
        before = lane < col_rest
        above = sublane_ext < row_rest
        turned = []
        for j in range(blocks):
            piece = term[:, lanes * j:lanes * (j + 1)]
            piece = piece.reshape(window // SUBLANES, SUBLANES, lanes)
            piece = pltpu.roll(piece, row_rest, 1)
            edge = jnp.zeros((1, SUBLANES, lanes), jnp.float32)
            piece = jnp.where(
                above,
                jnp.concatenate([edge, piece], axis=0),
                jnp.concatenate([piece, edge], axis=0),
            ).reshape(window + SUBLANES, lanes)
            turned.append(pltpu.roll(piece, col_rest, 1))
        for j in range(blocks + 1):
            if j == 0:
                add = jnp.where(before, 0.0, turned[0])
            elif j == blocks:
                add = jnp.where(before, turned[-1], 0.0)
            else:
                add = jnp.where(before, turned[j - 1], turned[j])
            grad_ref[place(where, part, j)] += add

    def exit_wave(patch):
        real, imag = patch
        psi_real = probe_real * real - probe_imag * imag
        psi_imag = probe_real * imag + probe_imag * real
        return jnp.concatenate([psi_real, psi_imag], axis=1)

    def unfold_rows(both):
        u_top, v_top = both[:half, :window], both[:half, window:]
        u_bot, v_bot = both[half:, :window], both[half:, window:]
        u_add = jnp.where(first_row, 0.0, u_bot)
        v_add = jnp.where(first_row, 0.0, v_bot)
        return jnp.concatenate([
            u_top + v_add, jnp.where(first_row, u_bot, u_top - v_bot),
            v_top - u_add, jnp.where(first_row, v_bot, v_top + u_bot)], axis=0)

    def unfold_cols(both):
        u_top, v_top = both[:window, :half], both[window:, :half]
        u_bot, v_bot = both[:window, half:], both[window:, half:]
        u_add = jnp.where(first_col, 0.0, u_bot)
        v_add = jnp.where(first_col, 0.0, v_bot)
        far_real = jnp.concatenate([u_top + v_add, jnp.where(first_col, u_bot, u_top - v_bot)], axis=1)
        far_imag = jnp.concatenate([v_top - u_add, jnp.where(first_col, v_bot, v_top + u_bot)], axis=1)
        return far_real, far_imag

    def fold_rows(g_real, g_imag):
        r_top, r_bot = g_real[:half], g_real[half:]
        i_top, i_bot = g_imag[:half], g_imag[half:]
        z_real = jnp.concatenate(
            [r_top + jnp.where(first_row, 0.0, r_bot), jnp.where(first_row, r_bot, i_bot - i_top)], axis=0)
        z_imag = jnp.concatenate(
            [i_top + jnp.where(first_row, 0.0, i_bot), jnp.where(first_row, i_bot, r_top - r_bot)], axis=0)
        return jnp.concatenate([z_real, z_imag], axis=1)

    def fold_cols(both):
        r_top, r_bot = both[:, :half], both[:, half:window]
        i_top, i_bot = both[:, window:window + half], both[:, window + half:]
        z_real = jnp.concatenate(
            [r_top + jnp.where(first_col, 0.0, r_bot), jnp.where(first_col, r_bot, i_bot - i_top)], axis=1)
        z_imag = jnp.concatenate(
            [i_top + jnp.where(first_col, 0.0, i_bot), jnp.where(first_col, i_bot, r_top - r_bot)], axis=1)
        return jnp.concatenate([z_real, z_imag], axis=0)

    def visit(step, carry):
        slots = [TOGETHER * step + i for i in range(TOGETHER)]
        where = [position(slot) for slot in slots]
        live = [(slot < count_ref[0]).astype(jnp.float32) for slot in slots]
        for slot in slots:
            for copy in loads(slot):
                copy.wait()
        patches = [(cut(slot, w, 0), cut(slot, w, 1)) for slot, w in zip(slots, where)]
        waves = [left_product(table, exit_wave(patch)) for patch in patches]
        waves = [right_product(unfold_rows(wave), table_t) for wave in waves]
        sources = []
        for wave, slot, on in zip(waves, slots, live):
            far_real, far_imag = unfold_cols(wave)
            factor = on * (far_real * far_real + far_imag * far_imag - levels[slot])
            sources.append(fold_rows(factor * far_real, factor * far_imag))
        waves = [left_product(table_t, source) for source in sources]
        waves = [right_product(fold_cols(wave), table) for wave in waves]
        for wave, patch, w in zip(waves, patches, where):
            chi_real, chi_imag = wave[:window], wave[window:]
            probe_grad_ref[0] += patch[0] * chi_real + patch[1] * chi_imag
            probe_grad_ref[1] += patch[0] * chi_imag - patch[1] * chi_real
            add_term(w, 0, probe_real * chi_real + probe_imag * chi_imag)
            add_term(w, 1, probe_real * chi_imag - probe_imag * chi_real)
        return carry

    steps = (count_ref[0] + TOGETHER - 1) // TOGETHER

    def fetch_slot(slot, carry):
        for copy in loads(slot):
            copy.start()
        return carry

    lax.fori_loop(0, steps * TOGETHER, fetch_slot, 0)
    grad_ref[...] = jnp.zeros_like(grad_ref)
    probe_grad_ref[...] = jnp.zeros_like(probe_grad_ref)
    lax.fori_loop(0, steps, visit, 0)


def slot_gradients(count, offsets, extended, illumination, measured, dft):
    smem = pl.BlockSpec(memory_space=pltpu.SMEM)
    vmem = pl.BlockSpec(memory_space=pltpu.VMEM)
    hbm = pl.BlockSpec(memory_space=pl.ANY)
    slots, window, _ = measured.shape
    return pl.pallas_call(
        compute_kernel,
        out_shape=(
            jax.ShapeDtypeStruct(extended.shape, jnp.float32),
            jax.ShapeDtypeStruct(illumination.shape, jnp.float32),
        ),
        in_specs=[smem, smem, hbm, vmem, hbm] + [vmem] * 4,
        out_specs=(vmem, vmem),
        scratch_shapes=[
            pltpu.VMEM((slots, 2, window + SUBLANES, window + 128), jnp.float32),
            pltpu.VMEM(measured.shape, jnp.float32),
            pltpu.SemaphoreType.DMA((slots,)),
            pltpu.SemaphoreType.DMA((slots,)),
        ],
        compiler_params=pltpu.CompilerParams(vmem_limit_bytes=VMEM_LIMIT),
        name="slot_gradients",
    )(count, offsets, extended, illumination, measured, *dft)


def place_of():
    return lax.axis_index("ty"), lax.axis_index("tx"), lax.axis_size("ty"), lax.axis_size("tx")


def send_to(source, target, sems, index, row, col):
    send_sem, recv_sem = sems
    return pltpu.make_async_remote_copy(
        src_ref=source,
        dst_ref=target,
        send_sem=send_sem.at[index],
        recv_sem=recv_sem.at[index],
        device_id=(row, col),
        device_id_type=MESH,
    )


def wait_bytes(ref, sem):
    pltpu.make_async_copy(ref, ref, sem).wait()


def greet(partners):
    barrier = pltpu.get_barrier_semaphore()
    for exists, row, col in partners:
        @pl.when(exists)
        def _():
            pl.semaphore_signal(barrier, inc=1, device_id=(row, col), device_id_type=MESH)
    pl.semaphore_wait(barrier, sum(jnp.int32(exists) for exists, _, _ in partners))


class Boundary:
    LINES = 4

    def __init__(self, relay, sems):
        self.relay = relay
        self.first_send, self.hop_recv, self.hop_send, self.last_recv = sems
        self.a, self.b, _, n = place_of()
        self.n = n
        half = n // 2
        self.low, self.high = half - 1, half
        if n >= 16:
            inner = ((half, half + 3, 3, half - 1), (half, n - 4, half - 4, half - 1))
        else:
            inner = ((half, half + 2, 2, half - 1), (half, n - 3, half - 3, half - 1))
        self.paths = ((half, 0, half - 1), *inner, (half, n - 1, half - 1))
        self.at_low, self.at_high = self.b == self.low, self.b == self.high

    @staticmethod
    def scratch(window):
        return [
            pltpu.VMEM((2, 3, window // 2, window), jnp.float32),
            pltpu.SemaphoreType.DMA((2, 3, Boundary.LINES)),
            pltpu.SemaphoreType.DMA((2, 3)),
            pltpu.SemaphoreType.DMA((2, 3)),
            pltpu.SemaphoreType.DMA((2, 3, Boundary.LINES)),
        ]

    def partners(self, every):
        pairs = sorted({tuple(sorted(pair)) for path in self.paths for pair in zip(path, path[1:])})
        found = []
        for p, q in pairs:
            if p // 2 != q // 2 and (every or p % 2 != q % 2):
                found += [(self.b == p, self.a, q), (self.b == q, self.a, p)]
        return found

    def before_z(self, way):
        n_x, n_y, _ = ProbeSum.sizes(lax.axis_size("ty"), self.n)
        high = 2 * n_y
        nodes = sorted({p for line in range(self.LINES)
                        for p, q in zip(self.path(way, line), self.path(way, line)[1:]) if (p >= high) != (q >= high)})
        found = self.b == nodes[0]
        for node in nodes[1:]:
            found = found | (self.b == node)
        return found

    def path(self, way, line):
        return self.paths[line] if way == 1 else self.paths[line][::-1]

    def origin(self, way):
        return self.low if way == 0 else self.high

    @staticmethod
    def quarter(ref, line):
        rows = ref.shape[1] // 2
        return ref.at[line // 2, pl.ds(line % 2 * rows, rows), :]

    def leg(self, way, index, line, k, source, target):
        path = self.path(way, line)
        last = k == len(path) - 2
        return pltpu.make_async_remote_copy(
            src_ref=self.quarter(source, line) if k == 0 else self.relay.at[way, index],
            dst_ref=self.quarter(target, line) if last else self.relay.at[way, index],
            send_sem=self.first_send.at[way, index, line] if k == 0 else self.hop_send.at[way, index],
            recv_sem=self.last_recv.at[way, index, line] if last else self.hop_recv.at[way, index],
            device_id=(self.a, path[k + 1]),
            device_id_type=MESH,
        )

    def start(self, way, index, source, target):
        for line in range(self.LINES):
            self.leg(way, index, line, 0, source, target).start()

    def relays(self, way):
        return [(line, k, node) for line in range(self.LINES)
                for k, node in enumerate(self.path(way, line)) if 0 < k < len(self.path(way, line)) - 1]

    def pass_on(self, way, index, source, target):
        for line, k, node in self.relays(way):
            @pl.when(self.b == node)
            def _():
                self.leg(way, index, line, k - 1, source, target).wait_recv()
                self.leg(way, index, line, k, source, target).start()

    def passed(self, way, index, source, target):
        for line, k, node in self.relays(way):
            @pl.when(self.b == node)
            def _():
                self.leg(way, index, line, k, source, target).wait_send()

    def wait_recv(self, way, index, source, target):
        for line in range(self.LINES):
            self.leg(way, index, line, len(self.path(way, line)) - 2, source, target).wait_recv()

    def wait_send(self, way, index, source, target):
        for line in range(self.LINES):
            self.leg(way, index, line, 0, source, target).wait_send()


class Sideways:
    def __init__(self, boundary, way, index, source, target, sems, slot):
        a, b, _, n_tx = place_of()
        self.boundary = boundary
        self.strip = (way, index, source, target)
        step = 1 if way == 0 else -1
        self.direct = send_to(source, target, sems, slot, a, b + step)
        left, right = b > 0, b < n_tx - 1
        self.has_target, self.has_source = (right, left) if way == 0 else (left, right)
        self.from_origin = b == boundary.origin(way)
        self.at_end = b == boundary.origin(1 - way)

    def start(self):
        self.start_relayed()
        self.start_direct()

    def start_relayed(self):
        pl.when(self.from_origin)(lambda: self.boundary.start(*self.strip))

    def start_direct(self):
        pl.when(self.has_target & ~self.from_origin)(self.direct.start)

    def pass_on(self):
        self.boundary.pass_on(*self.strip)

    def wait_recv(self):
        pl.when(self.at_end)(lambda: self.boundary.wait_recv(*self.strip))
        pl.when(self.has_source & ~self.at_end)(self.direct.wait_recv)

    def wait_send(self):
        pl.when(self.from_origin)(lambda: self.boundary.wait_send(*self.strip))
        pl.when(self.has_target & ~self.from_origin)(self.direct.wait_send)

    def passed(self):
        self.boundary.passed(*self.strip)


def fetch_kernel(
    specimen, patterns, extended, measured_out,
    measured, staged, send, recv, local, *rest,
):
    a, b, n_ty, n_tx = place_of()
    window = measured.shape[1]
    tile = specimen.shape[1]
    half = window // 2
    up, down, left, right = a > 0, a < n_ty - 1, b > 0, b < n_tx - 1
    boundary = Boundary(rest[0], rest[1:])
    near = (True, a, b + 1 - 2 * lax.rem(b, 2))
    greet([(up, a - 1, b), (down, a + 1, b), near, far_neighbour(a, b, n_tx)] + boundary.partners(True))
    sems = (send, recv)
    first, second = pl.ds(0, window), pl.ds(window, tile - window)
    beyond, inside = pl.ds(tile, window), pl.ds(0, tile)

    def aside(index, source, rows):
        return Sideways(
            boundary, 1, index, source.at[:, rows, first], extended.at[:, rows, beyond], sems, 2 + index)

    up_a = send_to(specimen.at[:, first, first], extended.at[:, beyond, first], sems, 0, a - 1, b)
    up_b = send_to(specimen.at[:, first, second], extended.at[:, beyond, second], sems, 1, a - 1, b)
    aside_a = aside(0, specimen, first)
    aside_b = aside(1, specimen, second)
    corner = send_to(
        extended.at[:, beyond, first], extended.at[:, beyond, beyond], sems, 4, a, b - 1)
    corner_up = send_to(
        extended.at[:, first, beyond], extended.at[:, beyond, beyond], sems, 5, a - 1, b)
    corner_left = down & left & ~boundary.at_high
    stage = pltpu.make_async_copy(specimen, staged, local.at[0])
    keep = pltpu.make_async_copy(staged, extended.at[:, inside, inside], local.at[2])
    load = pltpu.make_async_copy(patterns.at[0], measured, local.at[1])
    hold = (lax.rem(a, ProbeSum.sizes(n_ty, n_tx)[0]) == 0) & up & boundary.before_z(1)
    pl.when(up & ~hold)(up_a.start)
    aside_a.start()
    aside_b.start()
    load.start()
    stage.start()
    stage.wait()
    keep.start()

    @pl.when(hold)
    def _():
        aside_a.pass_on()
        aside_b.pass_on()
        up_a.start()

    pl.when(~hold)(aside_a.pass_on)

    @pl.when(up)
    def _():
        up_a.wait_send()
        up_b.start()

    pl.when(~hold)(aside_b.pass_on)
    pl.when(down)(up_a.wait_recv)
    pl.when(corner_left)(corner.start)

    @pl.when(boundary.at_low)
    def _():
        aside_a.wait_recv()
        pl.when(up)(corner_up.start)

    load.wait()
    row = lax.broadcasted_iota(jnp.int32, (window, window), 0)
    col = lax.broadcasted_iota(jnp.int32, (window, window), 1)

    def order(place, freq):
        picked = jnp.where(place <= half, place, window + half - place) == freq
        return picked.astype(jnp.float32).astype(jnp.bfloat16)

    reorder = jnp.concatenate([order(row, col)] * 3, axis=1)
    reorder_back = jnp.concatenate([order(col, row)] * 3, axis=0)

    def rearrange(slot, carry):
        def pieces(value):
            high, low = split(value)
            rest = (value - high.astype(jnp.float32) - low.astype(jnp.float32)).astype(jnp.bfloat16)
            return [high, low, rest]

        rows = jnp.dot(
            reorder, jnp.concatenate(pieces(measured[slot]), axis=0), preferred_element_type=jnp.float32)
        measured_out[slot] = jnp.dot(
            jnp.concatenate(pieces(rows), axis=1), reorder_back, preferred_element_type=jnp.float32)
        return carry

    lax.fori_loop(0, measured.shape[0], rearrange, 0)
    keep.wait()
    pl.when(~boundary.at_low)(aside_a.wait_recv)
    aside_b.wait_recv()
    pl.when(up)(up_b.wait_send)
    pl.when(down)(up_b.wait_recv)
    pl.when(corner_left)(corner.wait_send)
    pl.when(down & right & ~boundary.at_low)(corner.wait_recv)

    @pl.when(boundary.at_low)
    def _():
        pl.when(up)(corner_up.wait_send)
        pl.when(down)(corner_up.wait_recv)

    for strip in (aside_a, aside_b):
        strip.wait_send()
        strip.passed()


def fetch(specimen, patterns):
    window = patterns.shape[2]
    side = specimen.shape[1] + window
    vmem = pl.BlockSpec(memory_space=pltpu.VMEM)
    hbm = pl.BlockSpec(memory_space=pl.ANY)
    return pl.pallas_call(
        fetch_kernel,
        out_shape=(
            jax.ShapeDtypeStruct((2, side, side), jnp.float32),
            jax.ShapeDtypeStruct(patterns.shape[1:], jnp.float32),
        ),
        in_specs=[hbm, hbm],
        out_specs=(hbm, vmem),
        scratch_shapes=[
            pltpu.VMEM(patterns.shape[1:], jnp.float32),
            pltpu.VMEM(specimen.shape, jnp.float32),
            pltpu.SemaphoreType.DMA((6,)),
            pltpu.SemaphoreType.DMA((6,)),
            pltpu.SemaphoreType.DMA((3,)),
        ] + Boundary.scratch(window),
        compiler_params=pltpu.CompilerParams(
            collective_id=0, has_side_effects=True, vmem_limit_bytes=VMEM_LIMIT + 26 * 1024 * 1024),
        name="fetch",
    )(specimen, patterns)


class ProbeSum:
    STAGES = 7

    def __init__(self, terms, buffers, send, recv):
        self.terms = terms
        self.mate, self.mine, self.y_in, self.y_sum, self.z_in, self.x_in, self.z_out, self.full, self.other = buffers
        self.send, self.recv = send, recv
        self.a, self.b, n_ty, n_tx = place_of()
        self.n_x, self.n_y, self.n_z = self.sizes(n_ty, n_tx)
        self.n_low = self.n_z // 2
        self.devices = n_ty * n_tx
        self.core = lax.rem(self.b, 2)
        self.y = lax.rem(self.b // 2, self.n_y)
        self.x = lax.rem(self.a, self.n_x)
        self.z = self.b // (2 * self.n_y) * self.n_low + self.a // self.n_x
        self.mate_col = self.b + 1 - 2 * self.core
        self.y_rows = self.full.shape[0] // self.n_y
        self.z_rows = self.y_rows // self.n_z

    @staticmethod
    def sizes(n_ty, n_tx):
        n_x = 4 if n_ty == 16 else 2
        return n_x, n_tx // 4, 2 * (n_ty // n_x)

    @staticmethod
    def scratch(window, n_ty, n_tx):
        n_x, n_y, n_z = ProbeSum.sizes(n_ty, n_tx)
        y_rows = window // n_y
        z_rows = y_rows // n_z
        shapes = [
            (window, window), (window, window), (n_y - 1, y_rows, window), (y_rows, window),
            (n_z - 1, z_rows, window), (n_x, z_rows, window), (y_rows, window),
            (window, window), (window, window),
        ]
        return [pltpu.VMEM(shape, jnp.float32) for shape in shapes] + [
            pltpu.SemaphoreType.DMA((ProbeSum.STAGES,)),
            pltpu.SemaphoreType.DMA((ProbeSum.STAGES,)),
        ]

    def at_y(self, y):
        return self.a, (self.b // (2 * self.n_y)) * 2 * self.n_y + 2 * y + self.core

    def at_z(self, z):
        return lax.rem(z, self.n_low) * self.n_x + self.x, (z // self.n_low) * 2 * self.n_y + 2 * self.y + self.core

    def at_x(self, x):
        return self.a - self.x + x, self.b

    def partners(self):
        found = [(True, self.a, self.mate_col)]
        found += [(True, *self.at_y(lax.rem(self.y + d, self.n_y))) for d in range(1, self.n_y)]
        found += [(True, *self.at_z(lax.rem(self.z + d, self.n_z))) for d in range(1, self.n_z)]
        found += [(True, *self.at_x(lax.rem(self.x + d, self.n_x))) for d in range(1, self.n_x)]
        n_ty = self.n_low * self.n_x
        wraps_down = (self.x == self.n_x - 1) & (self.a < n_ty - 1)
        wraps_up = (self.x == 0) & (self.a > 0)
        found.append((wraps_down | wraps_up, jnp.where(wraps_up, self.a - 1, self.a + 1), self.b))
        return found

    def to(self, source, target, stage, row, col):
        return send_to(source, target, (self.send, self.recv), stage, row, col)

    @staticmethod
    def rows(ref, index, count):
        return ref.at[pl.ds(pl.multiple_of(index * count, SUBLANES), count), :]

    def each(self, count, go):
        def step(d, carry):
            go(d)
            return carry

        lax.fori_loop(1, count, step, 0)

    def start(self):
        self.to(self.terms.at[1 - self.core], self.mate, 0, self.a, self.mate_col).start()

    def scatter_y(self):
        self.to(self.terms.at[1 - self.core], self.mate, 0, self.a, self.mate_col).wait()
        self.mine[...] = self.terms[self.core] + self.mate[...]

        def go(d):
            y = lax.rem(self.y + d, self.n_y)
            self.to(self.rows(self.mine, y, self.y_rows), self.y_in.at[d - 1], 1, *self.at_y(y)).start()

        self.each(self.n_y, go)

    def scatter_z(self):
        wait_bytes(self.y_in, self.recv.at[1])
        total = self.rows(self.mine, self.y, self.y_rows)[...]
        for d in range(self.n_y - 1):
            total = total + self.y_in[d]
        self.y_sum[...] = total

        def go(d):
            z = lax.rem(self.z + d, self.n_z)
            self.to(self.rows(self.y_sum, z, self.z_rows), self.z_in.at[d - 1], 2, *self.at_z(z)).start()

        self.each(self.n_z, go)

    def across_x(self):
        wait_bytes(self.z_in, self.recv.at[2])
        total = self.rows(self.y_sum, self.z, self.z_rows)[...]
        for d in range(self.n_z - 1):
            total = total + self.z_in[d]
        self.x_in[self.x] = total

        def go(d):
            x = lax.rem(self.x + d, self.n_x)
            self.to(self.x_in.at[self.x], self.x_in.at[self.x], 3, *self.at_x(x)).start()

        self.each(self.n_x, go)

    def gather_z(self):
        wait_bytes(self.x_in.at[pl.ds(0, self.n_x - 1)], self.recv.at[3])
        total = self.x_in[0]
        for i in range(1, self.n_x):
            total = total + self.x_in[i]
        own = self.rows(self.z_out, self.z, self.z_rows)
        own[...] = total

        def go(d):
            z = lax.rem(self.z + d, self.n_z)
            self.to(own, own, 4, *self.at_z(z)).start()

        self.each(self.n_z, go)

    def gather_y(self):
        wait_bytes(self.z_out.at[pl.ds(0, (self.n_z - 1) * self.z_rows)], self.recv.at[4])
        own = self.rows(self.full, self.y, self.y_rows)
        own[...] = self.z_out[...]

        def go(d):
            y = lax.rem(self.y + d, self.n_y)
            self.to(self.z_out, own, 5, *self.at_y(y)).start()

        self.each(self.n_y, go)

    def share(self):
        wait_bytes(self.full.at[pl.ds(0, (self.n_y - 1) * self.y_rows)], self.recv.at[5])
        self.to(self.full, self.other, 6, self.a, self.mate_col).start()

    def finish(self, probe, probe_out):
        step = PROBE_GAIN / (POS_DEV * self.devices)
        probe_out[self.core] = probe[self.core] - step * self.full[...]
        self.to(self.full, self.other, 6, self.a, self.mate_col).wait()
        probe_out[1 - self.core] = probe[1 - self.core] - step * self.other[...]
        wait_bytes(self.y_in, self.send.at[1])
        wait_bytes(self.z_in, self.send.at[2])
        wait_bytes(self.x_in.at[pl.ds(0, self.n_x - 1)], self.send.at[3])
        wait_bytes(self.z_out.at[pl.ds(0, (self.n_z - 1) * self.z_rows)], self.send.at[4])
        wait_bytes(self.full.at[pl.ds(0, (self.n_y - 1) * self.y_rows)], self.send.at[5])


def far_neighbour(a, b, n_tx):
    core = lax.rem(b, 2)
    col = b - 1 + 2 * core
    return ((col >= 0) & (col < n_tx) & (b != n_tx // 2 - 1) & (b != n_tx // 2), a, col)


def exchange_kernel(
    grad, extended, probe, probe_grad, extended_out, probe_out,
    gv, ev, from_left, from_right, from_up, from_down, send, recv, local,
    *rest,
):
    a, b, n_ty, n_tx = place_of()
    window = probe.shape[1]
    side = gv.shape[1]
    tile = side - window
    core = lax.rem(b, 2)
    has_up, has_down, has_left, has_right = a > 0, a < n_ty - 1, b > 0, b < n_tx - 1
    odd = core == 1
    total = ProbeSum(probe_grad, rest[:9], *rest[9:11])
    boundary = Boundary(rest[11], rest[12:])
    greet(total.partners() + [far_neighbour(a, b, n_tx)] + boundary.partners(False))
    sems = (send, recv)
    start, middle, end = pl.ds(0, window), pl.ds(window, tile - window), pl.ds(tile, window)

    def across(rows, index):
        return (
            Sideways(boundary, 0, index, grad.at[:, rows, end], from_left.at[:, rows, :], sems, 2 * index),
            Sideways(boundary, 1, index, grad.at[:, rows, start], from_right.at[:, rows, :], sems, 2 * index + 1),
        )

    def along(source, cols, index):
        return (
            send_to(source.at[:, end, cols], from_up.at[:, :, cols], sems, index, a + 1, b),
            send_to(source.at[:, start, cols], from_down.at[:, :, cols], sems, index + 1, a - 1, b),
        )

    right_top, left_top = across(start, 0)
    right_end, left_end = across(end, 1)
    right_mid, left_mid = across(middle, 2)
    down_1, up_1 = along(grad, middle, 6)
    down_0, up_0 = along(gv, start, 8)
    down_2, up_2 = along(gv, end, 10)
    keep_top = send_to(ev.at[:, start, start], extended_out.at[:, start, end], sems, 12, a, b - 1)
    keep_end = send_to(ev.at[:, end, start], extended_out.at[:, end, end], sems, 13, a, b - 1)

    load_grad = pltpu.make_async_copy(grad, gv, local.at[0])
    load_extended = pltpu.make_async_copy(extended, ev, local.at[1])

    outer = (right_top, right_end, left_top, left_end)
    total.start()
    right_top.start()
    left_top.start()
    pl.when(has_down)(down_1.start)
    pl.when(has_up)(up_1.start)
    load_grad.start()
    load_extended.start()
    total.scatter_y()
    right_end.start()
    left_end.start()
    right_mid.start_relayed()
    left_mid.start_relayed()
    right_top.pass_on()
    left_top.pass_on()
    total.scatter_z()
    right_end.pass_on()
    left_end.pass_on()
    total.across_x()
    late = boundary.at_low | boundary.at_high

    total.gather_z()
    pl.when(late)(total.gather_y)
    load_grad.wait()
    right_top.wait_recv()
    right_end.wait_recv()

    @pl.when(has_left)
    def _():
        gv[:, start, start] += from_left[:, start, :]
        gv[:, end, start] += from_left[:, end, :]

    pl.when(has_down)(down_0.start)
    pl.when(has_up)(up_0.start)
    left_top.wait_recv()
    left_end.wait_recv()

    @pl.when(has_right)
    def _():
        gv[:, start, end] += from_right[:, start, :]
        gv[:, end, end] += from_right[:, end, :]

    pl.when(has_down & odd)(down_2.start)
    pl.when(has_up & odd)(up_2.start)

    pl.when(~late)(total.gather_y)
    for strip in outer:
        strip.wait_send()
    right_mid.start_direct()
    left_mid.start_direct()
    right_mid.pass_on()
    left_mid.pass_on()
    load_extended.wait()
    right_mid.wait_recv()
    left_mid.wait_recv()

    @pl.when(has_left)
    def _():
        gv[:, middle, start] += from_left[:, middle, :]

    @pl.when(has_right)
    def _():
        gv[:, middle, end] += from_right[:, middle, :]

    ev[:, middle, :] -= OBJECT_STEP * gv[:, middle, :]
    store_mid = pltpu.make_async_copy(ev.at[:, middle, :], extended_out.at[:, middle, :], local.at[0])
    store_mid.start()
    total.share()

    def update(rows, cols, received, exists):
        @pl.when(exists)
        def _():
            ev[:, rows, cols] -= OBJECT_STEP * (gv[:, rows, cols] + received[:, :, cols])

        @pl.when(jnp.logical_not(exists))
        def _():
            ev[:, rows, cols] -= OBJECT_STEP * gv[:, rows, cols]

    pl.when(has_up)(down_0.wait_recv)
    pl.when(has_down)(up_0.wait_recv)
    update(start, start, from_up, has_up)
    update(end, start, from_down, has_down)

    @pl.when(odd)
    def _():
        keep_top.start()
        keep_end.start()

    pl.when(has_up)(down_1.wait_recv)
    pl.when(has_down)(up_1.wait_recv)
    update(start, middle, from_up, has_up)
    update(end, middle, from_down, has_down)
    inner = pl.ds(0, tile)
    store_top = pltpu.make_async_copy(ev.at[:, start, inner], extended_out.at[:, start, inner], local.at[1])
    store_end = pltpu.make_async_copy(ev.at[:, end, inner], extended_out.at[:, end, inner], local.at[2])
    store_top.start()
    store_end.start()

    @pl.when(odd)
    def _():
        pl.when(has_up)(down_2.wait_recv)
        pl.when(has_down)(up_2.wait_recv)
        update(start, end, from_up, has_up)
        update(end, end, from_down, has_down)
        rim_top = pltpu.make_async_copy(ev.at[:, start, end], extended_out.at[:, start, end], local.at[3])
        rim_end = pltpu.make_async_copy(ev.at[:, end, end], extended_out.at[:, end, end], local.at[4])
        rim_top.start()
        rim_end.start()
        rim_top.wait()
        rim_end.wait()
        keep_top.wait_send()
        keep_end.wait_send()

    total.finish(probe, probe_out)
    right_mid.wait_send()
    left_mid.wait_send()
    for strip in outer + (right_mid, left_mid):
        strip.passed()

    @pl.when(has_down)
    def _():
        down_0.wait_send()
        down_1.wait_send()
        pl.when(odd)(down_2.wait_send)

    @pl.when(has_up)
    def _():
        up_0.wait_send()
        up_1.wait_send()
        pl.when(odd)(up_2.wait_send)

    store_mid.wait()
    store_top.wait()
    store_end.wait()

    @pl.when(jnp.logical_not(odd))
    def _():
        keep_top.wait_recv()
        keep_end.wait_recv()


def exchange(grad, extended, illumination, probe_grad):
    window = illumination.shape[1]
    side = grad.shape[1]
    vmem = pl.BlockSpec(memory_space=pltpu.VMEM)
    hbm = pl.BlockSpec(memory_space=pl.ANY)
    return pl.pallas_call(
        exchange_kernel,
        out_shape=(
            jax.ShapeDtypeStruct(extended.shape, jnp.float32),
            jax.ShapeDtypeStruct(illumination.shape, jnp.float32),
        ),
        in_specs=[hbm, hbm, vmem, vmem],
        out_specs=(hbm, vmem),
        scratch_shapes=[
            pltpu.VMEM((2, side, side), jnp.float32),
            pltpu.VMEM((2, side, side), jnp.float32),
            pltpu.VMEM((2, side, window), jnp.float32),
            pltpu.VMEM((2, side, window), jnp.float32),
            pltpu.VMEM((2, window, side), jnp.float32),
            pltpu.VMEM((2, window, side), jnp.float32),
            pltpu.SemaphoreType.DMA((14,)),
            pltpu.SemaphoreType.DMA((14,)),
            pltpu.SemaphoreType.DMA((5,)),
        ] + ProbeSum.scratch(window, lax.axis_size("ty"), lax.axis_size("tx")) + Boundary.scratch(window),
        compiler_params=pltpu.CompilerParams(
            collective_id=1, has_side_effects=True, vmem_limit_bytes=VMEM_LIMIT),
        name="exchange",
    )(grad, extended, illumination, probe_grad)


def fold_kernel(
    grad, extended, probe, probe_grad, specimen_out, probe_out,
    gv, ev, corner, from_left, from_up, send, recv, local,
    *rest,
):
    a, b, n_ty, n_tx = place_of()
    window = probe.shape[1]
    side = gv.shape[1]
    tile = side - window
    has_up, has_down, has_left, has_right = a > 0, a < n_ty - 1, b > 0, b < n_tx - 1
    total = ProbeSum(probe_grad, rest[:9], *rest[9:11])
    boundary = Boundary(rest[11], rest[12:])
    greet(total.partners() + [far_neighbour(a, b, n_tx)] + boundary.partners(False))
    sems = (send, recv)
    start, middle, end = pl.ds(0, window), pl.ds(window, tile - window), pl.ds(tile, window)
    inner = pl.ds(0, tile)

    def across(rows, index):
        return Sideways(boundary, 0, index, grad.at[:, rows, end], from_left.at[:, rows, :], sems, index)

    right_end = across(end, 0)
    right_top = across(start, 1)
    right_mid = across(middle, 2)
    down_1 = send_to(grad.at[:, end, middle], from_up.at[:, :, middle], sems, 3, a + 1, b)
    down_0 = send_to(corner, from_up.at[:, :, start], sems, 4, a + 1, b)
    load_grad = pltpu.make_async_copy(grad.at[:, :, inner], gv, local.at[0])
    load_extended = pltpu.make_async_copy(extended.at[:, inner, inner], ev, local.at[1])
    total.start()
    right_end.start()
    right_top.start_relayed()
    right_mid.start_relayed()
    pl.when(has_down)(down_1.start)
    load_grad.start()
    load_extended.start()
    total.scatter_y()
    right_top.start_direct()
    right_end.pass_on()
    total.scatter_z()
    right_top.pass_on()
    load_grad.wait()

    total.across_x()
    total.gather_z()
    pl.when(boundary.at_high)(total.gather_y)
    right_end.wait_recv()

    @pl.when(has_left)
    def _():
        corner[...] = gv[:, end, start] + from_left[:, end, :]

    @pl.when(jnp.logical_not(has_left))
    def _():
        corner[...] = gv[:, end, start]

    pl.when(has_down)(down_0.start)
    pl.when(~boundary.at_high)(total.gather_y)
    right_end.wait_send()
    right_mid.start_direct()
    right_mid.pass_on()
    load_extended.wait()
    ev[...] -= OBJECT_STEP * gv[:, inner, :]
    total.share()
    right_top.wait_recv()
    right_mid.wait_recv()

    @pl.when(has_left)
    def _():
        ev[:, :, start] -= OBJECT_STEP * from_left[:, inner, :]

    @pl.when(has_up)
    def _():
        down_1.wait_recv()
        down_0.wait_recv()
        ev[:, start, :] -= OBJECT_STEP * from_up[...]

    specimen_out[...] = ev[...]
    total.finish(probe, probe_out)
    right_top.wait_send()
    right_mid.wait_send()
    for strip in (right_end, right_top, right_mid):
        strip.passed()

    @pl.when(has_down)
    def _():
        down_1.wait_send()
        down_0.wait_send()


def fold(grad, extended, illumination, probe_grad):
    window = illumination.shape[1]
    side = grad.shape[1]
    tile = side - window
    vmem = pl.BlockSpec(memory_space=pltpu.VMEM)
    hbm = pl.BlockSpec(memory_space=pl.ANY)
    return pl.pallas_call(
        fold_kernel,
        out_shape=(
            jax.ShapeDtypeStruct((2, tile, tile), jnp.float32),
            jax.ShapeDtypeStruct(illumination.shape, jnp.float32),
        ),
        in_specs=[hbm, hbm, vmem, vmem],
        out_specs=(vmem, vmem),
        scratch_shapes=[
            pltpu.VMEM((2, side, tile), jnp.float32),
            pltpu.VMEM((2, tile, tile), jnp.float32),
            pltpu.VMEM((2, window, window), jnp.float32),
            pltpu.VMEM((2, side, window), jnp.float32),
            pltpu.VMEM((2, window, tile), jnp.float32),
            pltpu.SemaphoreType.DMA((5,)),
            pltpu.SemaphoreType.DMA((5,)),
            pltpu.SemaphoreType.DMA((2,)),
        ] + ProbeSum.scratch(window, lax.axis_size("ty"), lax.axis_size("tx")) + Boundary.scratch(window),
        compiler_params=pltpu.CompilerParams(
            collective_id=2, has_side_effects=True, vmem_limit_bytes=VMEM_LIMIT),
        name="fold",
    )(grad, extended, illumination, probe_grad)


def body(specimen, illumination, patterns, scan_offsets, counts):
    window = illumination.shape[1]
    tile = specimen.shape[1]
    row_anchor = lax.axis_index("ty") * tile
    col_anchor = lax.axis_index("tx") * tile
    offsets = scan_offsets[0] - jnp.stack([row_anchor, col_anchor])[None, :].astype(jnp.int32)
    count = counts.reshape(1)
    dft = tables(window)
    extended, measured = fetch(specimen, patterns)
    for iteration in range(ITERS):
        grad, probe_grad = slot_gradients(count, offsets, extended, illumination, measured, dft)
        if iteration < ITERS - 1:
            extended, illumination = exchange(grad, extended, illumination, probe_grad)
        else:
            specimen, illumination = fold(grad, extended, illumination, probe_grad)
    return (specimen, illumination)


def solution(mesh):
    placed = (
        P(None, "ty", "tx"),
        P(),
        P("ty", "tx", None, None),
        P("ty", "tx", None),
        P("ty", "tx"),
    )
    return jax.shard_map(
        body, mesh=mesh, in_specs=placed, out_specs=(P(None, "ty", "tx"), P()), check_vma=False
    )
```
